32 devices in a mesh: sec: 4 (over y, core), strip: 8 (over z, x).
Axes of the slice: x: 2, y: 2, z: 4, core: 2. Of those that a mesh axis runs over, the one named last changes fastest.
Arguments:
- positions: float32 [12, 2, 512, 1024], P('sec', None, 'strip'), may hold values from -6 to 6
- velocity: float32 [12, 2, 512, 1024], P('sec', None, 'strip'), may hold values from -4 to 4
- spring_class: int32 [12, 2, 512, 1024], P('sec', None, 'strip'), may hold values from 0 to 7
- match_shift: int32 [12, 2, 64, 8], P('sec', None, 'strip'), may hold values from -3 to 3
- fixed: int32 [12], P('sec'), may hold values 0 or 1
- class_stiffness: float32 [8], replicated, may hold values from 0.1 to 1
- cross_stiffness: float32 [2], replicated, may hold values from 0.2 to 1
Outputs:
- new_positions: float32 [12, 2, 512, 1024], P('sec', None, 'strip')
- new_velocity: float32 [12, 2, 512, 1024], P('sec', None, 'strip')
The draws below stay inside these ranges and needn't reach their ends.
All inputs are finite; a program needn't handle non-finite values. No bound on the sum of `fixed` on one device may be relied on, other than what follows from the above.
Results may differ from the reference program's by a relative error of at most 0.0003.
Values sent between devices are 32-bit elements; how exact they have to be, the bound alone decides.
No kernel may reach another device: no remote copies, remote signals or barrier semaphores. Data moves between devices by JAX's collectives and lax.ppermute only.
A program may use at most 64 MiB of HBM per device.

```python
import math
import jax
import jax.numpy as jnp
from jax import lax

HEIGHT = 512
WIDTH = 1024
BLOCK_ROWS = 8
BLOCK_COLS = 128
MAX_SHIFT = 3
CLASSES = 8
STEPS = 2
SECTIONS = 12


def place_ends(entries, rng, least, high):
    dims = entries.shape
    index_at = [jax.random.randint(jax.random.fold_in(rng, axis), (), 0, dims[axis]) for axis in range(len(dims))]
    entries = entries.at[tuple(index_at)].set(least)
    longest = dims.index(max(dims))
    index_at[longest] = (index_at[longest] + 1) % dims[longest]
    return entries.at[tuple(index_at)].set(high)


def steps_of(stream_key, extent, pieces, low, largest):
    def one(dim, blocks):
        heights = jax.random.uniform(jax.random.fold_in(jax.random.fold_in(stream_key, 6), dim), (blocks,), jnp.float32, low / len(pieces), largest / len(pieces))
        return jnp.repeat(jnp.exp(heights), extent[dim] // blocks).reshape((-1,) + (1,) * (len(extent) - dim - 1))

    level = one(*pieces[0])
    for cut in pieces[1:]:
        level = level * one(*cut)
    return level


def noise(rng, dims, scale, bound, shards=(), kind=jnp.bfloat16):
    drawn = scale * jax.random.normal(rng, dims, jnp.float32)
    if shards:
        drawn = drawn * steps_of(rng, dims, shards, -0.22, 0.18)
    return jnp.clip(drawn, -bound, bound).astype(kind)


def setup_inputs(seed: int = 0) -> dict:
    arg_keys = jax.random.split(jax.random.key(seed), 8)
    return {
        "positions": noise(arg_keys[0], (SECTIONS, 2, HEIGHT, WIDTH), 1.0, 6.0, ((0, 4), (2, 8)), jnp.float32),
        "velocity": noise(arg_keys[1], (SECTIONS, 2, HEIGHT, WIDTH), 0.5, 4.0, ((0, 4), (2, 8)), jnp.float32),
        "spring_class": place_ends(jax.random.randint(arg_keys[2], (SECTIONS, 2, HEIGHT, WIDTH), 0, CLASSES), jax.random.fold_in(arg_keys[2], 1), 0, CLASSES - 1).astype(jnp.int32),
        "match_shift": place_ends(jax.random.randint(arg_keys[3], (SECTIONS, 2, HEIGHT // BLOCK_ROWS, WIDTH // BLOCK_COLS), 0 - MAX_SHIFT, MAX_SHIFT + 1), jax.random.fold_in(arg_keys[3], 1), 0 - MAX_SHIFT, MAX_SHIFT).astype(jnp.int32),
        "fixed": place_ends((jax.random.randint(arg_keys[4], (SECTIONS,), 0, 4) < 1).astype(jnp.int32), jax.random.fold_in(arg_keys[4], 1), 0, 1),
        "class_stiffness": jnp.clip(jnp.exp(jax.random.uniform(arg_keys[5], (CLASSES,), jnp.float32, math.log(0.1), math.log(1.0))), 0.1, 1.0),
        "cross_stiffness": jnp.clip(jnp.exp(jax.random.uniform(arg_keys[6], (2,), jnp.float32, math.log(0.2), math.log(1.0))), 0.2, 1.0),
    }


damping_rate = 0.9
time_step = 0.35


def pull(stretch, axis):
    squared = jnp.sum(stretch * stretch, axis=axis, keepdims=True)
    return stretch * (1.0 + 0.5 * squared / (1.0 + squared))


def lanes(offset):
    expanded = jnp.repeat(jnp.repeat(offset, BLOCK_ROWS, axis=-2), BLOCK_COLS, axis=-1)
    column = lax.broadcasted_iota(jnp.int32, expanded.shape, expanded.ndim - 1)
    block_start = column - column % BLOCK_COLS
    return (block_start + (column - block_start + expanded) % BLOCK_COLS).astype(jnp.int32)


def moved(field, lane_index):
    full_index = jnp.broadcast_to(lane_index[None], field.shape)
    return jnp.take_along_axis(field, full_index, axis=2)


def reference(positions, velocity, spring_class, match_shift, fixed, class_stiffness, cross_stiffness):
    padded_shift = jnp.pad(match_shift, ((2, 0), (0, 0), (0, 0), (0, 0)))
    moving = (fixed == 0).astype(jnp.float32)[:, None, None, None]

    def forces(current):
        padded = jnp.pad(current, ((2, 2), (0, 0), (0, 0), (0, 0)))

        def section_force(index_sec):
            nearby = lax.dynamic_slice_in_dim(padded, index_sec, 5, 0)
            shifts = lax.dynamic_slice_in_dim(padded_shift, index_sec, 3, 0)
            stiffness = class_stiffness[spring_class[index_sec]]
            center = nearby[2]
            across = center[:, :, 1:] - center[:, :, :-1]
            flow_across = stiffness[0][None, :, :-1] * pull(across, 0)
            summed = jnp.pad(flow_across, ((0, 0), (0, 0), (0, 1))) - jnp.pad(flow_across, ((0, 0), (0, 0), (1, 0)))
            down = center[:, 1:] - center[:, :-1]
            flow_down = stiffness[1][None, :-1] * pull(down, 0)
            summed = summed + jnp.pad(flow_down, ((0, 0), (0, 1), (0, 0))) - jnp.pad(flow_down, ((0, 0), (1, 0), (0, 0)))
            for hops in (1, 2):
                valid = (index_sec + hops < SECTIONS).astype(jnp.float32)
                partner = moved(nearby[2 + hops], lanes(shifts[2, hops - 1]))
                summed = summed + cross_stiffness[hops - 1] * pull(partner - center, 0) * valid
                before = (index_sec - hops >= 0).astype(jnp.float32)
                owner_shift = shifts[2 - hops, hops - 1]
                source = nearby[2 - hops]
                pair_term = cross_stiffness[hops - 1] * pull(moved(center, lanes(owner_shift)) - source, 0) * before
                summed = summed - moved(pair_term, lanes(-owner_shift))
            return summed

        return lax.map(section_force, jnp.arange(SECTIONS, dtype=jnp.int32))

    current = positions
    speed = velocity
    for step in range(STEPS):
        force = forces(current)
        speed = (damping_rate * speed + time_step * force) * moving
        current = current + time_step * speed
    return current, speed
```

```python
import functools

import jax
import jax.numpy as jnp
from jax import lax
from jax.experimental import pallas as pl
from jax.experimental.pallas import tpu as pltpu
from jax.sharding import PartitionSpec as P

ROWS = 8
COLS = 128
CLASSES = 8
DAMPING = 0.9
STEP = 0.35

VMEM = pl.BlockSpec(memory_space=pltpu.VMEM)
SMEM = pl.BlockSpec(memory_space=pltpu.SMEM)


def exchange(value, axis, pairing):
    n = lax.axis_size(axis)
    first = 0 if pairing == "a" else 1
    route = []
    for i in range(first, n - 1, 2):
        route += [(i, i + 1), (i + 1, i)]
    return lax.ppermute(value, axis, route)


class Side:
    def __init__(self, pairing, sections):
        i = lax.axis_index("sec")
        n = lax.axis_size("sec")
        odd = lax.rem(i, 2)
        after = odd if pairing == "b" else 1 - odd
        self.after = after == 1
        self.near = jnp.where(self.after, sections - 1, 0)
        self.second = jnp.where(self.after, sections - 2, 1)
        self.last = sections - 1
        self.exists = jnp.where(self.after, i < n - 1, i > 0)

    def pairs(self):
        return (
            (self.near, 0, 1, self.last),
            (self.second, 0, 2, self.last),
            (self.near, 1, 2, self.last - 1),
        )


def inverse(value):
    guess = pl.reciprocal(value, approx=True)
    return guess * (2.0 - value * guess)


def flow(ex, ey, half):
    gain = half * (3.0 - inverse(1.0 + ex * ex + ey * ey))
    return gain * ex, gain * ey


def cols_of(cb):
    return pl.ds(cb * COLS, COLS)


def rows_of(rb):
    start = rb * ROWS
    return pl.ds(start if isinstance(start, int) else pl.multiple_of(start, ROWS), ROWS)


def moved(tile, offset):
    return pltpu.roll(tile, (-offset) & (COLS - 1), 1)


def class_table(stiff_ref):
    lane = lax.broadcasted_iota(jnp.int32, (ROWS, COLS), 1)
    table = jnp.zeros((ROWS, COLS), jnp.float32)
    for k in range(CLASSES):
        table = jnp.where(lane == k, stiff_ref[k] * (0.5 * STEP), table)
    return table


def look_up(table, index):
    full = jnp.broadcast_to(index, table.shape)
    return jnp.take_along_axis(table, full, axis=1, mode="promise_in_bounds")[: index.shape[0]]


def put_rims(u, rim_a, rim_b, kv_row):
    sections, _, rows, width = u.shape
    odd = lax.rem(lax.axis_index("strip"), 2) == 1

    def put(line, cols, first, last):
        rim_a[line : line + 1, cols] = jnp.where(odd, first, last)
        rim_b[line : line + 1, cols] = jnp.where(odd, last, first)

    for s in range(sections):
        for cb in range(width // COLS):
            cols = cols_of(cb)
            for c in range(2):
                put(2 * s + c, cols, u[s, c, pl.ds(0, 1), cols], u[s, c, pl.ds(rows - 1, 1), cols])
            stiff = kv_row(s, cols)
            put(2 * sections + s, cols, stiff, stiff)


def prepare_kernel(u, cls, stiff, near, second, fast, rim_a, rim_b):
    sections, _, rows, width = u.shape
    slow_side = Side("b", sections)
    fast_side = Side("a", sections)
    near[...] = u[slow_side.near]
    second[...] = u[slow_side.second]
    fast[0] = u[fast_side.near]
    fast[1] = u[fast_side.second]
    table = class_table(stiff)

    put_rims(u, rim_a, rim_b, lambda s, cols: look_up(table, cls[s, 1, pl.ds(rows - 1, 1), cols]))


def inside(u, w, total, shift, cross, kh_tile, kv_tile):
    sections, _, rows, width = u.shape
    rbs, cbs = rows // ROWS, width // COLS
    lane = lax.broadcasted_iota(jnp.int32, (ROWS, COLS), 1)
    row = lax.broadcasted_iota(jnp.int32, (ROWS, COLS), 0)

    def across(rb, carry):
        at = rows_of(rb)
        for s in range(sections):
            tiles = [[u[s, c, at, cols_of(cb)] for cb in range(cbs)] for c in range(2)]
            turned = [[pltpu.roll(t, COLS - 1, 1) for t in tiles[c]] for c in range(2)]
            back = []
            flows = []
            for cb in range(cbs):
                half = kh_tile(s, rb, cb)
                if cb == cbs - 1:
                    half = jnp.where(lane == COLS - 1, 0.0, half)
                e = [
                    jnp.where(lane == COLS - 1, turned[c][(cb + 1) % cbs], turned[c][cb]) - tiles[c][cb]
                    for c in range(2)
                ]
                f = flow(e[0], e[1], half)
                flows.append(f)
                back.append([pltpu.roll(f[c], 1, 1) for c in range(2)])
            for cb in range(cbs):
                for c in range(2):
                    got = jnp.where(lane == 0, back[cb - 1][c], back[cb][c])
                    total[s, c, at, cols_of(cb)] = (
                        DAMPING * w[s, c, at, cols_of(cb)] + flows[cb][c] - got
                    )
        return carry

    lax.fori_loop(0, rbs, across, 0)

    def below(cb, carry):
        at = pl.ds(pl.multiple_of(cb * COLS, COLS), COLS)
        for s in range(sections):
            tiles = [[u[s, c, rows_of(rb), at] for rb in range(rbs)] for c in range(2)]
            turned = [[pltpu.roll(t, ROWS - 1, 0) for t in tiles[c]] for c in range(2)]
            before = [jnp.zeros((ROWS, COLS), jnp.float32)] * 2
            for rb in range(rbs):
                half = kv_tile(s, rb, at)
                if rb == rbs - 1:
                    half = jnp.where(row == ROWS - 1, 0.0, half)
                e = [
                    jnp.where(row == ROWS - 1, turned[c][(rb + 1) % rbs], turned[c][rb]) - tiles[c][rb]
                    for c in range(2)
                ]
                f = flow(e[0], e[1], half)
                for c in range(2):
                    down = pltpu.roll(f[c], 1, 0)
                    got = jnp.where(row == 0, before[c], down)
                    before[c] = down
                    total[s, c, rows_of(rb), at] += f[c] - got
        return carry

    lax.fori_loop(0, cbs, below, 0)

    def between(rb, carry):
        at = rows_of(rb)
        for hops in (1, 2):
            half = cross[hops - 1] * (0.5 * STEP)
            for s in range(sections - hops):
                for cb in range(cbs):
                    cols = cols_of(cb)
                    offset = shift[s, hops - 1, rb, cb]
                    e = [moved(u[s + hops, c, at, cols], offset) - u[s, c, at, cols] for c in range(2)]
                    f = flow(e[0], e[1], half)
                    for c in range(2):
                        total[s, c, at, cols] += f[c]
                        total[s + hops, c, at, cols] -= moved(f[c], -offset)
        return carry

    lax.fori_loop(0, rbs, between, 0)


def first_inside_kernel(u, w, cls, shift, stiff, cross, total, half):
    sections, _, rows, width = u.shape
    table = class_table(stiff)

    def kh_tile(s, rb, cb):
        at = rows_of(rb)
        for d in range(2):
            half[s, d, at, cols_of(cb)] = look_up(table, cls[s, d, at, cols_of(cb)])
        return half[s, 0, at, cols_of(cb)]

    def kv_tile(s, rb, at):
        return half[s, 1, rows_of(rb), at]

    inside(u, w, total, shift, cross, kh_tile, kv_tile)


def later_inside_kernel(u, w, half, shift, cross, total):
    def kh_tile(s, rb, cb):
        return half[s, 0, rows_of(rb), cols_of(cb)]

    def kv_tile(s, rb, at):
        return half[s, 1, rows_of(rb), at]

    inside(u, w, total, shift, cross, kh_tile, kv_tile)


def link(side, which, own_shift, before_shift, cross):
    own, _, hops, owner = side.pairs()[which]
    half = jnp.where(side.exists, cross[hops - 1] * (0.5 * STEP), 0.0)

    def offset(rb, cb):
        return jnp.where(
            side.after, own_shift[own, hops - 1, rb, cb], -before_shift[owner, hops - 1, rb, cb]
        )

    return own, half, offset


def pull_tile(u, there, own, half, offset, rb, cb):
    at, cols = rows_of(rb), cols_of(cb)
    amount = offset(rb, cb)
    e = [moved(there(c, at, cols), amount) - u[own, c, at, cols] for c in range(2)]
    return flow(e[0], e[1], half)


def rims_and_fast_kernel(
    u, total_in, half, fast, rim_a, rim_b, own_shift, before_shift, cross, total
):
    sections, _, rows, width = u.shape
    rbs, cbs = rows // ROWS, width // COLS
    side = Side("a", sections)
    links = [link(side, which, own_shift, before_shift, cross) for which in range(3)]

    def body(rb, carry):
        at = rows_of(rb)
        for cb in range(cbs):
            cols = cols_of(cb)
            for which in range(3):
                own, stiff, offset = links[which]
                block = side.pairs()[which][1]
                f = pull_tile(u, lambda c, r, k: fast[block, c, r, k], own, stiff, offset, rb, cb)
                for c in range(2):
                    total[own, c, at, cols] += f[c]
        return carry

    lax.fori_loop(0, rbs, body, 0)

    strip = lax.axis_index("strip")
    odd = lax.rem(strip, 2) == 1
    has_below = strip < lax.axis_size("strip") - 1

    def below(r, cols):
        return jnp.where(odd, rim_b[r : r + 1, cols], rim_a[r : r + 1, cols])

    def above(r, cols):
        return jnp.where(odd, rim_a[r : r + 1, cols], rim_b[r : r + 1, cols])

    last = pl.ds(rows - 1, 1)
    top = pl.ds(0, 1)
    for s in range(sections):
        for cb in range(cbs):
            cols = cols_of(cb)
            stiff = jnp.where(has_below, half[s, 1, last, cols], 0.0)
            e = [below(2 * s + c, cols) - u[s, c, last, cols] for c in range(2)]
            f = flow(e[0], e[1], stiff)
            for c in range(2):
                total[s, c, last, cols] += f[c]
            stiff = above(2 * sections + s, cols)
            stiff = jnp.where(strip > 0, stiff, 0.0)
            e = [u[s, c, top, cols] - above(2 * s + c, cols) for c in range(2)]
            f = flow(e[0], e[1], stiff)
            for c in range(2):
                total[s, c, top, cols] -= f[c]


def moving_of(fixed, s):
    return jnp.where(fixed[s] == 0, 1.0, 0.0)


def settle(u, total, s, at, cols, moving, new_u, new_w, add=None):
    for c in range(2):
        value = total[s, c, at, cols]
        if add is not None:
            value = value + add[c]
        value = value * moving
        new_w[s, c, at, cols] = value
        new_u[s, c, at, cols] = u[s, c, at, cols] + STEP * value


def near_kernel(u, total_in, arrived, own_shift, before_shift, cross, fixed, total, new_u, second, fast):
    sections, _, rows, width = u.shape
    rbs, cbs = rows // ROWS, width // COLS
    side = Side("b", sections)
    fast_side = Side("a", sections)
    links = [link(side, which, own_shift, before_shift, cross) for which in range(2)]

    def body(rb, carry):
        at = rows_of(rb)
        for cb in range(cbs):
            cols = cols_of(cb)
            for which in range(2):
                own, stiff, offset = links[which]
                f = pull_tile(u, lambda c, r, k: arrived[c, r, k], own, stiff, offset, rb, cb)
                for c in range(2):
                    total[own, c, at, cols] += f[c]
        for k in range(1, sections):
            s = jnp.where(side.after, sections - 1 - k, k)
            moving = moving_of(fixed, s)
            for cb in range(cbs):
                settle(u, total, s, at, cols_of(cb), moving, new_u, total)
        for c in range(2):
            second[c, at, :] = new_u[side.second, c, at, :]
            fast[0, c, at, :] = new_u[fast_side.near, c, at, :]
            fast[1, c, at, :] = new_u[fast_side.second, c, at, :]
        return carry

    lax.fori_loop(0, rbs, body, 0)


def far_kernel(
    u, total_in, new_u_in, arrived, half, own_shift, before_shift, cross, fixed,
    total, new_u, near, rim_a, rim_b,
):
    sections, _, rows, width = u.shape
    rbs, cbs = rows // ROWS, width // COLS
    side = Side("b", sections)
    own, stiff, offset = link(side, 2, own_shift, before_shift, cross)
    moving = moving_of(fixed, own)

    def body(rb, carry):
        at = rows_of(rb)
        for cb in range(cbs):
            f = pull_tile(u, lambda c, r, k: arrived[c, r, k], own, stiff, offset, rb, cb)
            settle(u, total, own, at, cols_of(cb), moving, new_u, total, f)
        for c in range(2):
            near[c, at, :] = new_u[own, c, at, :]
        return carry

    lax.fori_loop(0, rbs, body, 0)

    put_rims(new_u, rim_a, rim_b, lambda s, cols: half[s, 1, pl.ds(rows - 1, 1), cols])


def last_far_kernel(u, total_in, arrived, own_shift, before_shift, cross, total):
    sections, _, rows, width = u.shape
    rbs, cbs = rows // ROWS, width // COLS
    side = Side("b", sections)
    own, stiff, offset = link(side, 2, own_shift, before_shift, cross)

    def body(rb, carry):
        at = rows_of(rb)
        for cb in range(cbs):
            f = pull_tile(u, lambda c, r, k: arrived[c, r, k], own, stiff, offset, rb, cb)
            for c in range(2):
                total[own, c, at, cols_of(cb)] += f[c]
        return carry

    lax.fori_loop(0, rbs, body, 0)


def last_near_kernel(u, total, arrived, own_shift, before_shift, cross, fixed, new_u, new_w):
    sections, _, rows, width = u.shape
    rbs, cbs = rows // ROWS, width // COLS
    side = Side("b", sections)
    links = [link(side, which, own_shift, before_shift, cross) for which in range(2)]

    def body(rb, carry):
        at = rows_of(rb)
        for which in range(2):
            own, stiff, offset = links[which]
            moving = moving_of(fixed, own)
            for cb in range(cbs):
                f = pull_tile(u, lambda c, r, k: arrived[c, r, k], own, stiff, offset, rb, cb)
                settle(u, total, own, at, cols_of(cb), moving, new_u, new_w, f)
        for k in range(2, sections):
            s = jnp.where(side.after, sections - 1 - k, k)
            moving = moving_of(fixed, s)
            for cb in range(cbs):
                settle(u, total, s, at, cols_of(cb), moving, new_u, new_w)
        return carry

    lax.fori_loop(0, rbs, body, 0)


def call(kernel, outs, ins, scalars, alias=None, flops=0):
    return pl.pallas_call(
        kernel,
        out_shape=outs,
        in_specs=[VMEM] * len(ins) + [SMEM] * len(scalars),
        out_specs=[VMEM] * len(outs),
        input_output_aliases=alias or {},
        compiler_params=pltpu.CompilerParams(vmem_limit_bytes=16 << 20),
    )(*ins, *scalars)


def per_device(u, w, cls, shift, fixed, stiff, cross):
    sections, _, rows, width = u.shape
    full = jax.ShapeDtypeStruct(u.shape, jnp.float32)
    one = jax.ShapeDtypeStruct(u.shape[1:], jnp.float32)
    two = jax.ShapeDtypeStruct((2,) + u.shape[1:], jnp.float32)
    rim = jax.ShapeDtypeStruct((-(-3 * sections // ROWS) * ROWS, width), jnp.float32)

    near, second, fast, rim_a, rim_b = call(
        prepare_kernel, [one, one, two, rim, rim], [u, cls], [stiff]
    )
    near = exchange(near, "sec", "b")
    far = exchange(second, "sec", "b")
    fast = exchange(fast, "sec", "a")
    n = lax.axis_size("sec")
    before = lax.ppermute(shift, "sec", [(i, i + 1) for i in range(n - 1)])
    rim_a = exchange(rim_a, "strip", "a")
    rim_b = exchange(rim_b, "strip", "b")
    total, half = call(
        first_inside_kernel, [full, full], [u, w, cls], [shift, stiff, cross]
    )
    (total,) = call(
        rims_and_fast_kernel,
        [full],
        [u, total, half, fast, rim_a, rim_b],
        [shift, before, cross],
        {1: 0},
    )
    total, new_u, second, fast = call(
        near_kernel, [full, full, one, two], [u, total, near], [shift, before, cross, fixed], {1: 0}
    )
    second = exchange(second, "sec", "b")
    fast = exchange(fast, "sec", "a")
    w, u, near, rim_a, rim_b = call(
        far_kernel,
        [full, full, one, rim, rim],
        [u, total, new_u, far, half],
        [shift, before, cross, fixed],
        {1: 0, 2: 1},
    )
    near = exchange(near, "sec", "b")
    rim_a = exchange(rim_a, "strip", "a")
    rim_b = exchange(rim_b, "strip", "b")
    (total,) = call(later_inside_kernel, [full], [u, w, half], [shift, cross])
    (total,) = call(
        rims_and_fast_kernel,
        [full],
        [u, total, half, fast, rim_a, rim_b],
        [shift, before, cross],
        {1: 0},
    )
    (total,) = call(last_far_kernel, [full], [u, total, second], [shift, before, cross], {1: 0})
    return tuple(
        call(last_near_kernel, [full, full], [u, total, near], [shift, before, cross, fixed])
    )


def solution(mesh):
    block = P("sec", None, "strip", None)
    return jax.shard_map(
        per_device,
        mesh=mesh,
        in_specs=(block, block, block, block, P("sec"), P(), P()),
        out_specs=(block, block),
        check_vma=False,
    )
```

```python
import jax
import jax.numpy as jnp
from jax import lax
from jax.experimental import pallas as pl
from jax.experimental.pallas import tpu as pltpu
from jax.sharding import PartitionSpec as P

ROWS = 8
COLS = 128
CLASSES = 8
DAMPING = 0.9
STEP = 0.35

VMEM = pl.BlockSpec(memory_space=pltpu.VMEM)
ANY = pl.BlockSpec(memory_space=pl.ANY)

INSIDE, SLOW, FAST, TABLE, MOVING = 0, 2, 4, 6, 7


def exchange(value, axis, pairing):
    n = lax.axis_size(axis)
    first = 0 if pairing == "a" else 1
    route = []
    for i in range(first, n - 1, 2):
        route += [(i, i + 1), (i + 1, i)]
    return lax.ppermute(value, axis, route)


def slow_after():
    return lax.rem(lax.axis_index("sec"), 2) == 1


def by_side(body):
    after = slow_after()

    @pl.when(after)
    def _():
        body(True)

    @pl.when(jnp.logical_not(after))
    def _():
        body(False)


def near_of(after, sections):
    return sections - 1 if after else 0


def second_of(after, sections):
    return sections - 2 if after else 1


def pairs_of(after, sections):
    near, second = near_of(after, sections), second_of(after, sections)
    return ((near, 0, 1), (second, 0, 2), (near, 1, 2))


def inverse(value):
    guess = pl.reciprocal(value, approx=True)
    return guess * (2.0 - value * guess)


def flow(ex, ey, half):
    gain = half * (3.0 - inverse(1.0 + ex * ex + ey * ey))
    return gain * ex, gain * ey


def cols_of(cb):
    return slice(cb * COLS, (cb + 1) * COLS)


def rows_of(rb):
    start = rb * ROWS
    return pl.ds(start if isinstance(start, int) else pl.multiple_of(start, ROWS), ROWS)


def tail_rows(rows):
    return -(-(rows // ROWS) // ROWS) * ROWS


def per_tile(width, make):
    return jnp.concatenate([make(cb) for cb in range(width // COLS)], axis=1)


def turned(wide, amounts):
    return per_tile(wide.shape[1], lambda cb: pltpu.roll(wide[:, cols_of(cb)], amounts[cb], 1))


def gathered(wide, index):
    def one(cb):
        full = jnp.broadcast_to(index[:, cols_of(cb)], (ROWS, COLS))
        return jnp.take_along_axis(wide[:, cols_of(cb)], full, axis=1, mode="promise_in_bounds")

    return per_tile(wide.shape[1], one)


def spread(blocks, width):
    return per_tile(width, lambda cb: jnp.broadcast_to(blocks[:, cb : cb + 1], (blocks.shape[0], COLS)))


def lanes(rows, width):
    return lax.broadcasted_iota(jnp.int32, (rows, width), 1) & (COLS - 1)


def put_tail(shift, out, first, width):
    sections, _, rbs, _ = shift.shape
    lane = lanes(rbs, width)
    parts = [
        spread(shift[s, h], width)
        for s, h in ((sections - 1, 0), (sections - 1, 1), (sections - 2, 1))
    ]
    mixed = jnp.where(lane == 0, parts[0], jnp.where(lane == 1, parts[1], parts[2]))
    out[first : first + rbs, :] = mixed.astype(jnp.float32)


def put_index(after, shift, arrived, first, index):
    sections, _, rbs, _ = shift.shape
    width = index.shape[2]
    lane = lanes(rbs, width)
    for j, (own, _, hops) in enumerate(pairs_of(after, sections)):
        if after:
            offset = spread(shift[own, hops - 1], width)
        else:
            blocks = per_tile(
                width,
                lambda cb: jnp.broadcast_to(
                    arrived[first : first + rbs, cb * COLS + j : cb * COLS + j + 1], (rbs, COLS)
                ),
            )
            offset = -blocks.astype(jnp.int32)
        index[j, 0:rbs, :] = (lane + offset) & (COLS - 1)


def put_rims(u, rim_a, rim_b, kv_row):
    sections, _, rows, _ = u.shape
    odd = lax.rem(lax.axis_index("strip"), 2) == 1

    def put(line, first, last):
        rim_a[line : line + 1, :] = jnp.where(odd, first, last)
        rim_b[line : line + 1, :] = jnp.where(odd, last, first)

    for s in range(sections):
        for c in range(2):
            put(2 * s + c, u[s, c, 0:1, :], u[s, c, rows - 1 : rows, :])
        stiff = kv_row(s)
        put(2 * sections + s, stiff, stiff)


def look_up(table, index):
    def one(cb):
        tile = jnp.broadcast_to(index[:, cols_of(cb)], (ROWS, COLS))
        return jnp.take_along_axis(table, tile, axis=1, mode="promise_in_bounds")[: index.shape[0]]

    return per_tile(index.shape[1], one)


def lead_kernel(u, shift, near):
    sections, _, rows, width = u.shape

    def body(after):
        for c in range(2):
            near[c * rows : (c + 1) * rows, :] = u[near_of(after, sections), c]

    by_side(body)
    put_tail(shift, near, 2 * rows, width)


def prepare_kernel(u, cls, shift, stiff, cross, fixed, second, fast, rim_a, rim_b, splat):
    sections, _, rows, width = u.shape
    i, n = lax.axis_index("sec"), lax.axis_size("sec")
    odd = slow_after()

    def body(after):
        for c in range(2):
            second[c * rows : (c + 1) * rows, :] = u[second_of(after, sections), c]
            fast[c * rows : (c + 1) * rows, :] = u[near_of(not after, sections), c]
            fast[(2 + c) * rows : (3 + c) * rows, :] = u[second_of(not after, sections), c]

    by_side(body)
    put_tail(shift, fast, 4 * rows, width)
    tile = (ROWS, COLS)
    lane = lax.broadcasted_iota(jnp.int32, tile, 1)
    slow_there = jnp.where(odd, i < n - 1, i > 0)
    fast_there = jnp.where(odd, i > 0, i < n - 1)
    for h in range(2):
        k = jnp.full(tile, cross[h] * (0.5 * STEP))
        splat[INSIDE + h] = k
        splat[SLOW + h] = jnp.where(slow_there, k, 0.0)
        splat[FAST + h] = jnp.where(fast_there, k, 0.0)
    table = jnp.zeros(tile, jnp.float32)
    for k in range(CLASSES):
        table = jnp.where(lane == k, stiff[k] * (0.5 * STEP), table)
    splat[TABLE] = table
    for s in range(sections):
        splat[MOVING + s] = jnp.full(tile, jnp.where(fixed[s] == 0, 1.0, 0.0))
    put_rims(u, rim_a, rim_b, lambda s: look_up(table, cls[s, 1, rows - 1 : rows, :]))


def wide_splat(splat, k, width):
    tile = splat[k]
    return per_tile(width, lambda cb: tile)


def inside(u, w, total, half_across, half_below, shift, splat, scalars, sem):
    sections, _, rows, width = u.shape
    rbs, cbs = rows // ROWS, width // COLS
    load = pltpu.make_async_copy(shift, scalars, sem)
    load.start()
    last = lax.broadcasted_iota(jnp.int32, (ROWS, width), 1) == width - 1

    def across(rb, carry):
        at = rows_of(rb)
        for s in range(sections):
            x, y = u[s, 0, at, :], u[s, 1, at, :]
            half = jnp.where(last, 0.0, half_across(s, at))
            f = flow(pltpu.roll(x, width - 1, 1) - x, pltpu.roll(y, width - 1, 1) - y, half)
            new = [DAMPING * w[s, c, at, :] + (f[c] - pltpu.roll(f[c], 1, 1)) for c in range(2)]
            for c in range(2):
                total[s, c, at, :] = new[c]
        return carry

    lax.fori_loop(0, rbs, across, 0, unroll=2)
    bottom = lax.broadcasted_iota(jnp.int32, (rows, COLS), 0) == rows - 1

    def below(cb, carry):
        at = pl.ds(pl.multiple_of(cb * COLS, COLS), COLS)
        for s in range(sections):
            x, y = u[s, 0, :, at], u[s, 1, :, at]
            half = jnp.where(bottom, 0.0, half_below(s, at))
            f = flow(pltpu.roll(x, rows - 1, 0) - x, pltpu.roll(y, rows - 1, 0) - y, half)
            new = [total[s, c, :, at] + (f[c] - pltpu.roll(f[c], 1, 0)) for c in range(2)]
            for c in range(2):
                total[s, c, :, at] = new[c]
        return carry

    lax.fori_loop(0, cbs, below, 0)
    load.wait()

    def between(rb, carry):
        at = rows_of(rb)
        add = [[total[s, c, at, :] for c in range(2)] for s in range(sections)]
        for hops in (1, 2):
            half = wide_splat(splat, INSIDE + hops - 1, width)
            for s in range(sections - hops):
                offsets = [scalars[s, hops - 1, rb, cb] for cb in range(cbs)]
                there = [(-o) & (COLS - 1) for o in offsets]
                back = [o & (COLS - 1) for o in offsets]
                e = [turned(u[s + hops, c, at, :], there) - u[s, c, at, :] for c in range(2)]
                f = flow(e[0], e[1], half)
                for c in range(2):
                    add[s][c] = add[s][c] + f[c]
                    add[s + hops][c] = add[s + hops][c] - turned(f[c], back)
        for s in range(sections):
            for c in range(2):
                total[s, c, at, :] = add[s][c]
        return carry

    lax.fori_loop(0, rbs, between, 0, unroll=2)


def first_inside_kernel(u, w, cls, shift, splat, total, half, scalars, sem):
    table = splat[TABLE]

    def half_across(s, at):
        k = look_up(table, cls[s, 0, at, :])
        half[s, 0, at, :] = k
        half[s, 1, at, :] = look_up(table, cls[s, 1, at, :])
        return k

    def half_below(s, at):
        return half[s, 1, :, at]

    inside(u, w, total, half_across, half_below, shift, splat, scalars, sem)


def later_inside_kernel(u, w, half, shift, splat, total, scalars, sem):
    def half_across(s, at):
        return half[s, 0, at, :]

    def half_below(s, at):
        return half[s, 1, :, at]

    inside(u, w, total, half_across, half_below, shift, splat, scalars, sem)


def side_flow(u, own, arrived, first, index, j, half, rb):
    rows = u.shape[2]
    at = rows_of(rb)
    number = index[j, rb : rb + 1, :]
    e = [
        gathered(arrived[pl.ds(first + c * rows + rb * ROWS, ROWS), :], number) - u[own, c, at, :]
        for c in range(2)
    ]
    return flow(e[0], e[1], half)


def rims_and_fast(u, half, fast, rim_a, rim_b, splat, index, total):
    sections, _, rows, width = u.shape
    rbs = rows // ROWS

    def body(slow_is_after):
        for j, (own, block, hops) in enumerate(pairs_of(not slow_is_after, sections)):
            stiff = wide_splat(splat, FAST + hops - 1, width)
            for rb in range(rbs):
                f = side_flow(u, own, fast, 2 * block * rows, index, j, stiff, rb)
                for c in range(2):
                    total[own, c, rows_of(rb), :] += f[c]

    by_side(body)
    strip = lax.axis_index("strip")
    odd = lax.rem(strip, 2) == 1
    has_below = strip < lax.axis_size("strip") - 1

    def below(r):
        return jnp.where(odd, rim_b[r : r + 1, :], rim_a[r : r + 1, :])

    def above(r):
        return jnp.where(odd, rim_a[r : r + 1, :], rim_b[r : r + 1, :])

    last, top = slice(rows - 1, rows), slice(0, 1)
    for s in range(sections):
        stiff = jnp.where(has_below, half[s, 1, last, :], 0.0)
        f = flow(*[below(2 * s + c) - u[s, c, last, :] for c in range(2)], stiff)
        stiff = jnp.where(strip > 0, above(2 * sections + s), 0.0)
        g = flow(*[u[s, c, top, :] - above(2 * s + c) for c in range(2)], stiff)
        for c in range(2):
            total[s, c, last, :] += f[c]
            total[s, c, top, :] -= g[c]


def first_rims_kernel(u, total_in, half, fast, rim_a, rim_b, shift, splat, total, index):
    rows = u.shape[2]
    by_side(lambda after: put_index(not after, shift, fast, 4 * rows, index))
    rims_and_fast(u, half, fast, rim_a, rim_b, splat, index, total)


def later_rims_kernel(u, total_in, half, fast, rim_a, rim_b, index, splat, total):
    rims_and_fast(u, half, fast, rim_a, rim_b, splat, index, total)


def near_kernel(u, total_in, arrived, shift, splat, total, new_u, second, fast, index):
    sections, _, rows, width = u.shape
    rbs = rows // ROWS

    def body(after):
        put_index(after, shift, arrived, 2 * rows, index)
        pairs = pairs_of(after, sections)
        others = [s for s in range(sections) if s != near_of(after, sections)]
        for rb in range(rbs):
            at = rows_of(rb)
            value = {}
            for j in range(2):
                own, _, hops = pairs[j]
                stiff = wide_splat(splat, SLOW + hops - 1, width)
                f = side_flow(u, own, arrived, 0, index, j, stiff, rb)
                value[own] = [total[own, c, at, :] + f[c] for c in range(2)]
            for s in range(sections):
                for c in range(2):
                    v = value[s][c] if s in value else total[s, c, at, :]
                    if s in others:
                        v = v * wide_splat(splat, MOVING + s, width)
                        moved = u[s, c, at, :] + STEP * v
                        new_u[s, c, at, :] = moved
                        if s == second_of(after, sections):
                            second[pl.ds(c * rows + rb * ROWS, ROWS), :] = moved
                        if s == near_of(not after, sections):
                            fast[pl.ds(c * rows + rb * ROWS, ROWS), :] = moved
                        if s == second_of(not after, sections):
                            fast[pl.ds((2 + c) * rows + rb * ROWS, ROWS), :] = moved
                    total[s, c, at, :] = v

    by_side(body)


def far_kernel(
    u, total_in, new_u_in, arrived, half, index, splat, total, new_u, near, rim_a, rim_b
):
    sections, _, rows, width = u.shape

    def body(after):
        own, _, hops = pairs_of(after, sections)[2]
        stiff = wide_splat(splat, SLOW + hops - 1, width)
        moving = wide_splat(splat, MOVING + own, width)
        for rb in range(rows // ROWS):
            at = rows_of(rb)
            f = side_flow(u, own, arrived, 0, index, 2, stiff, rb)
            for c in range(2):
                v = (total[own, c, at, :] + f[c]) * moving
                moved = u[own, c, at, :] + STEP * v
                total[own, c, at, :] = v
                new_u[own, c, at, :] = moved
                near[pl.ds(c * rows + rb * ROWS, ROWS), :] = moved

    by_side(body)
    put_rims(new_u, rim_a, rim_b, lambda s: half[s, 1, rows - 1 : rows, :])


def last_far_kernel(u, total_in, arrived, index, splat, total, out_u, out_w, new_u, new_w, sem):
    sections, _, rows, width = u.shape

    def body(after):
        pairs = pairs_of(after, sections)
        done = [s for s in range(sections) if s not in (pairs[0][0], pairs[1][0])]
        copies = []
        for k, s in enumerate(done):
            moving = splat[MOVING + s][0:1, 0:1]
            for c in range(2):
                v = total[s, c] * moving
                new_w[k, c] = v
                new_u[k, c] = u[s, c] + STEP * v
            copies += [
                pltpu.make_async_copy(new_u.at[k], out_u.at[s], sem.at[2 * k]),
                pltpu.make_async_copy(new_w.at[k], out_w.at[s], sem.at[2 * k + 1]),
            ]
        for copy in copies:
            copy.start()
        own, _, hops = pairs[2]
        stiff = wide_splat(splat, SLOW + hops - 1, width)
        for rb in range(rows // ROWS):
            f = side_flow(u, own, arrived, 0, index, 2, stiff, rb)
            for c in range(2):
                total[own, c, rows_of(rb), :] += f[c]
        for copy in copies:
            copy.wait()

    by_side(body)


def last_near_kernel(
    u, total, arrived, index, splat, out_u_in, out_w_in, out_u, out_w, new_u, new_w, sem
):
    sections, _, rows, width = u.shape

    def body(after):
        copies = []
        for j in range(2):
            own, _, hops = pairs_of(after, sections)[j]
            stiff = wide_splat(splat, SLOW + hops - 1, width)
            moving = wide_splat(splat, MOVING + own, width)
            for rb in range(rows // ROWS):
                at = rows_of(rb)
                f = side_flow(u, own, arrived, 0, index, j, stiff, rb)
                for c in range(2):
                    v = (total[own, c, at, :] + f[c]) * moving
                    new_w[j, c, at, :] = v
                    new_u[j, c, at, :] = u[own, c, at, :] + STEP * v
            for k, (source, target) in enumerate(((new_u, out_u), (new_w, out_w))):
                copy = pltpu.make_async_copy(source.at[j], target.at[own], sem.at[2 * j + k])
                copy.start()
                copies.append(copy)
        for copy in copies:
            copy.wait()

    by_side(body)


def call(kernel, outs, ins, alias=None, scratch=(), in_specs=None, out_specs=None):
    return pl.pallas_call(
        kernel,
        out_shape=outs,
        in_specs=in_specs or [VMEM] * len(ins),
        out_specs=out_specs or [VMEM] * len(outs),
        input_output_aliases=alias or {},
        scratch_shapes=scratch,
        compiler_params=pltpu.CompilerParams(vmem_limit_bytes=16 << 20),
    )(*ins)


def per_device(u, w, cls, shift, fixed, stiff, cross):
    sections, _, rows, width = u.shape
    rbs = rows // ROWS

    def array(*shape, dtype=jnp.float32):
        return jax.ShapeDtypeStruct(shape, dtype)

    full = array(*u.shape)
    one = array(2 * rows, width)
    two = array(4 * rows, width)
    tail = tail_rows(rows)
    rim = array(-(-3 * sections // ROWS) * ROWS, width)
    splat = array(MOVING + sections, ROWS, COLS)
    index = array(3, tail_rows(rows), width, dtype=jnp.int32)
    smem = pl.BlockSpec(memory_space=pltpu.SMEM)
    scalars = [pltpu.SMEM(shift.shape, jnp.int32), pltpu.SemaphoreType.DMA]

    (near,) = call(lead_kernel, [array(2 * rows + tail, width)], [u, shift])
    near = exchange(near, "sec", "b")
    second, fast, rim_a, rim_b, splat = call(
        prepare_kernel,
        [one, array(4 * rows + tail, width), rim, rim, splat],
        [u, cls, shift, stiff, cross, fixed],
        in_specs=[VMEM] * 3 + [smem] * 3,
    )
    fast = exchange(fast, "sec", "a")
    far = exchange(second, "sec", "b")
    rim_a = exchange(rim_a, "strip", "a")
    rim_b = exchange(rim_b, "strip", "b")
    total, half = call(
        first_inside_kernel, [full, full], [u, w, cls, shift, splat], scratch=scalars
    )
    total, fast_index = call(
        first_rims_kernel, [full, index], [u, total, half, fast, rim_a, rim_b, shift, splat], {1: 0}
    )
    total, new_u, second, fast, index = call(
        near_kernel, [full, full, one, two, index], [u, total, near, shift, splat], {1: 0}
    )
    second = exchange(second, "sec", "b")
    fast = exchange(fast, "sec", "a")
    w, u, near, rim_a, rim_b = call(
        far_kernel,
        [full, full, one, rim, rim],
        [u, total, new_u, far, half, index, splat],
        {1: 0, 2: 1},
    )
    near = exchange(near, "sec", "b")
    rim_a = exchange(rim_a, "strip", "a")
    rim_b = exchange(rim_b, "strip", "b")
    (total,) = call(later_inside_kernel, [full], [u, w, half, shift, splat], scratch=scalars)
    (total,) = call(
        later_rims_kernel, [full], [u, total, half, fast, rim_a, rim_b, fast_index, splat], {1: 0}
    )
    done = max(sections - 2, 1)
    total, out_u, out_w = call(
        last_far_kernel,
        [full, full, full],
        [u, total, second, index, splat],
        {1: 0},
        scratch=[pltpu.VMEM((done, 2, rows, width), jnp.float32)] * 2
        + [pltpu.SemaphoreType.DMA((2 * done,))],
        out_specs=[VMEM, ANY, ANY],
    )
    return tuple(
        call(
            last_near_kernel,
            [full, full],
            [u, total, near, index, splat, out_u, out_w],
            {5: 0, 6: 1},
            scratch=[pltpu.VMEM((2, 2, rows, width), jnp.float32)] * 2
            + [pltpu.SemaphoreType.DMA((4,))],
            in_specs=[VMEM] * 5 + [ANY] * 2,
            out_specs=[ANY] * 2,
        )
    )


def solution(mesh):
    block = P("sec", None, "strip", None)
    return jax.shard_map(
        per_device,
        mesh=mesh,
        in_specs=(block, block, block, block, P("sec"), P(), P()),
        out_specs=(block, block),
        check_vma=False,
    )
```

```python
import jax
import jax.numpy as jnp
from jax import lax
from jax.experimental import pallas as pl
from jax.experimental.pallas import tpu as pltpu
from jax.sharding import PartitionSpec as P

ROWS = 8
COLS = 128
CLASSES = 8
DAMPING = 0.9
STEP = 0.35

VMEM = pl.BlockSpec(memory_space=pltpu.VMEM)
ANY = pl.BlockSpec(memory_space=pl.ANY)
LEAD_LIMIT = 64 << 20

INSIDE, SLOW, FAST, TABLE, MOVING = 0, 2, 4, 6, 7


def exchange(value, axis, pairing):
    n = lax.axis_size(axis)
    first = 0 if pairing == "a" else 1
    route = []
    for i in range(first, n - 1, 2):
        route += [(i, i + 1), (i + 1, i)]
    return lax.ppermute(value, axis, route)


def slow_after():
    return lax.rem(lax.axis_index("sec"), 2) == 1


def by_side(body):
    after = slow_after()

    @pl.when(after)
    def _():
        body(True)

    @pl.when(jnp.logical_not(after))
    def _():
        body(False)


def near_of(after, sections):
    return sections - 1 if after else 0


def second_of(after, sections):
    return sections - 2 if after else 1


def pairs_of(after, sections):
    near, second = near_of(after, sections), second_of(after, sections)
    return ((near, 0, 1), (second, 0, 2), (near, 1, 2))


def inverse(value):
    guess = pl.reciprocal(value, approx=True)
    return guess * (2.0 - value * guess)


def flow(ex, ey, half):
    gain = half * (3.0 - inverse(1.0 + ex * ex + ey * ey))
    return gain * ex, gain * ey


def cols_of(cb):
    return slice(cb * COLS, (cb + 1) * COLS)


def rows_of(rb):
    start = rb * ROWS
    return pl.ds(start if isinstance(start, int) else pl.multiple_of(start, ROWS), ROWS)


def tail_rows(rows):
    return -(-(rows // ROWS) // ROWS) * ROWS


def per_tile(width, make):
    return jnp.concatenate([make(cb) for cb in range(width // COLS)], axis=1)


def turned(wide, amounts):
    return per_tile(wide.shape[1], lambda cb: pltpu.roll(wide[:, cols_of(cb)], amounts[cb], 1))


def gathered(wide, index):
    def one(cb):
        full = jnp.broadcast_to(index[:, cols_of(cb)], (ROWS, COLS))
        return jnp.take_along_axis(wide[:, cols_of(cb)], full, axis=1, mode="promise_in_bounds")

    return per_tile(wide.shape[1], one)


def spread(blocks, width):
    return per_tile(width, lambda cb: jnp.broadcast_to(blocks[:, cb : cb + 1], (blocks.shape[0], COLS)))


def lanes(rows, width):
    return lax.broadcasted_iota(jnp.int32, (rows, width), 1) & (COLS - 1)


def put_tail(shift, out, first, width):
    sections, _, rbs, _ = shift.shape
    lane = lanes(rbs, width)
    parts = [
        spread(shift[s, h], width)
        for s, h in ((sections - 1, 0), (sections - 1, 1), (sections - 2, 1))
    ]
    mixed = jnp.where(lane == 0, parts[0], jnp.where(lane == 1, parts[1], parts[2]))
    out[first : first + rbs, :] = mixed.astype(jnp.float32)


def put_index(after, shift, arrived, first, index):
    sections, _, rbs, _ = shift.shape
    width = index.shape[2]
    lane = lanes(rbs, width)
    for j, (own, _, hops) in enumerate(pairs_of(after, sections)):
        if after:
            offset = spread(shift[own, hops - 1], width)
        else:
            blocks = per_tile(
                width,
                lambda cb: jnp.broadcast_to(
                    arrived[first : first + rbs, cb * COLS + j : cb * COLS + j + 1], (rbs, COLS)
                ),
            )
            offset = -blocks.astype(jnp.int32)
        index[j, 0:rbs, :] = (lane + offset) & (COLS - 1)


def put_rims(first_of, last_of, kv_of, rim_a, rim_b, sections):
    odd = lax.rem(lax.axis_index("strip"), 2) == 1

    def put(line, first, last):
        rim_a[line : line + 1, :] = jnp.where(odd, first, last)
        rim_b[line : line + 1, :] = jnp.where(odd, last, first)

    for s in range(sections):
        for c in range(2):
            put(2 * s + c, first_of(s, c), last_of(s, c))
        stiff = kv_of(s)
        put(2 * sections + s, stiff, stiff)


def look_up(table, index):
    def one(cb):
        tile = jnp.broadcast_to(index[:, cols_of(cb)], (ROWS, COLS))
        return jnp.take_along_axis(table, tile, axis=1, mode="promise_in_bounds")[: index.shape[0]]

    return per_tile(index.shape[1], one)


def put_splat(stiff, cross, fixed, splat):
    sections = fixed.shape[0]
    i, n = lax.axis_index("sec"), lax.axis_size("sec")
    odd = slow_after()
    tile = (ROWS, COLS)
    lane = lax.broadcasted_iota(jnp.int32, tile, 1)
    slow_there = jnp.where(odd, i < n - 1, i > 0)
    fast_there = jnp.where(odd, i > 0, i < n - 1)
    for h in range(2):
        k = jnp.full(tile, cross[h] * (0.5 * STEP))
        splat[INSIDE + h] = k
        splat[SLOW + h] = jnp.where(slow_there, k, 0.0)
        splat[FAST + h] = jnp.where(fast_there, k, 0.0)
    table = jnp.zeros(tile, jnp.float32)
    for k in range(CLASSES):
        table = jnp.where(lane == k, stiff[k] * (0.5 * STEP), table)
    splat[TABLE] = table
    for s in range(sections):
        splat[MOVING + s] = jnp.full(tile, jnp.where(fixed[s] == 0, 1.0, 0.0))


def lead_kernel(
    u, cls, shift, stiff, cross, fixed, slow, fast, rim_a, rim_b, splat,
    shift_here, stiff_here, cross_here, fixed_here, first_here, last_here, cls_here,
    tail_here, rim_a_here, rim_b_here, splat_here, sem,
):
    sections, _, rows, width = u.shape

    def copies(first, pairs):
        return [
            pltpu.make_async_copy(source, target, sem.at[first + k])
            for k, (source, target) in enumerate(pairs)
        ]

    def blocks(after):
        pairs = []
        for out, side in ((slow, after), (fast, not after)):
            for k, own in enumerate((near_of(side, sections), second_of(side, sections))):
                for c in range(2):
                    pairs.append((u.at[own, c], out.at[pl.ds((2 * k + c) * rows, rows)]))
        return copies(0, pairs)

    bottom = pl.ds(rows - ROWS, ROWS)
    small = copies(
        8,
        (
            (shift, shift_here),
            (stiff, stiff_here),
            (cross, cross_here),
            (fixed, fixed_here),
            (u.at[:, :, pl.ds(0, ROWS)], first_here),
            (u.at[:, :, bottom], last_here),
            (cls.at[:, 1, bottom], cls_here),
        ),
    )
    for copy in small:
        copy.start()
    by_side(lambda after: [copy.start() for copy in blocks(after)])
    for copy in small:
        copy.wait()
    put_tail(shift_here, tail_here, 0, width)
    put_splat(stiff_here, cross_here, fixed_here, splat_here)
    table = splat_here[TABLE]
    put_rims(
        lambda s, c: first_here[s, c, 0:1, :],
        lambda s, c: last_here[s, c, ROWS - 1 : ROWS, :],
        lambda s: look_up(table, cls_here[s, ROWS - 1 : ROWS, :]),
        rim_a_here,
        rim_b_here,
        sections,
    )
    after_blocks = pl.ds(4 * rows, tail_here.shape[0])
    results = copies(
        15,
        (
            (tail_here, slow.at[after_blocks]),
            (tail_here, fast.at[after_blocks]),
            (rim_a_here, rim_a),
            (rim_b_here, rim_b),
            (splat_here, splat),
        ),
    )
    for copy in results:
        copy.start()
    by_side(lambda after: [copy.wait() for copy in blocks(after)])
    for copy in results:
        copy.wait()


def hand_on_kernel(*refs):
    pass


def wide_splat(splat, k, width):
    tile = splat[k]
    return per_tile(width, lambda cb: tile)


def chosen(values, index):
    for bit in range(3):
        on = (index & (1 << bit)) != 0
        values = [jnp.where(on, values[k + 1], values[k]) for k in range(0, len(values), 2)]
    return values[0]


def inside(u, w, total, half_across, half_below, shift, splat, scalars, sem):
    sections, _, rows, width = u.shape
    rbs, cbs = rows // ROWS, width // COLS
    load = pltpu.make_async_copy(shift, scalars, sem)
    load.start()
    bottom = lax.broadcasted_iota(jnp.int32, (rows, COLS), 0) == rows - 1

    def below(cb, carry):
        at = pl.ds(pl.multiple_of(cb * COLS, COLS), COLS)
        for s in range(sections):
            x, y = u[s, 0, :, at], u[s, 1, :, at]
            half = jnp.where(bottom, 0.0, half_below(s, at))
            f = flow(pltpu.roll(x, rows - 1, 0) - x, pltpu.roll(y, rows - 1, 0) - y, half)
            new = [f[c] - pltpu.roll(f[c], 1, 0) for c in range(2)]
            if w is not None:
                new = [DAMPING * w[s, c, :, at] + new[c] for c in range(2)]
            for c in range(2):
                total[s, c, :, at] = new[c]
        return carry

    lax.fori_loop(0, cbs, below, 0)
    load.wait()
    last = lax.broadcasted_iota(jnp.int32, (ROWS, width), 1) == width - 1

    def row(rb, carry):
        at = rows_of(rb)
        add = [[total[s, c, at, :] for c in range(2)] for s in range(sections)]
        for s in range(sections):
            x, y = u[s, 0, at, :], u[s, 1, at, :]
            half = jnp.where(last, 0.0, half_across(s, at))
            f = flow(pltpu.roll(x, width - 1, 1) - x, pltpu.roll(y, width - 1, 1) - y, half)
            for c in range(2):
                add[s][c] = add[s][c] + (f[c] - pltpu.roll(f[c], 1, 1))
        for hops in (1, 2):
            half = wide_splat(splat, INSIDE + hops - 1, width)
            for s in range(sections - hops):
                offsets = [scalars[s, hops - 1, rb, cb] for cb in range(cbs)]
                there = [(-o) & (COLS - 1) for o in offsets]
                back = [o & (COLS - 1) for o in offsets]
                e = [turned(u[s + hops, c, at, :], there) - u[s, c, at, :] for c in range(2)]
                f = flow(e[0], e[1], half)
                for c in range(2):
                    add[s][c] = add[s][c] + f[c]
                    add[s + hops][c] = add[s + hops][c] - turned(f[c], back)
        for s in range(sections):
            for c in range(2):
                total[s, c, at, :] = add[s][c]
        return carry

    lax.fori_loop(0, rbs, row, 0)


def first_inside_kernel(u, cls, shift, splat, total, half, scalars, sem):
    table = splat[TABLE]
    values = [jnp.broadcast_to(table[:, k : k + 1], (ROWS, COLS)) for k in range(CLASSES)]
    rows = u.shape[2]

    def half_across(s, at):
        index = cls[s, 0, at, :]
        k = per_tile(index.shape[1], lambda cb: chosen(values, index[:, cols_of(cb)]))
        half[s, 0, at, :] = k
        return k

    def half_below(s, at):
        index = cls[s, 1, :, at]
        k = jnp.concatenate(
            [look_up(table, index[r : r + ROWS]) for r in range(0, rows, ROWS)], axis=0
        )
        half[s, 1, :, at] = k
        return k

    inside(u, None, total, half_across, half_below, shift, splat, scalars, sem)


def later_inside_kernel(u, w, half, shift, splat, total, scalars, sem):
    def half_across(s, at):
        return half[s, 0, at, :]

    def half_below(s, at):
        return half[s, 1, :, at]

    inside(u, w, total, half_across, half_below, shift, splat, scalars, sem)


def side_flow(u, own, arrived, first, index, j, half, rb):
    rows = u.shape[2]
    at = rows_of(rb)
    number = index[j, rb : rb + 1, :]
    e = [
        gathered(arrived[pl.ds(first + c * rows + rb * ROWS, ROWS), :], number) - u[own, c, at, :]
        for c in range(2)
    ]
    return flow(e[0], e[1], half)


def rim_flows(u, half, rim_a, rim_b, total, sections):
    rows = u.shape[2]
    strip = lax.axis_index("strip")
    odd = lax.rem(strip, 2) == 1
    has_below = strip < lax.axis_size("strip") - 1

    def below(r):
        return jnp.where(odd, rim_b[r : r + 1, :], rim_a[r : r + 1, :])

    def above(r):
        return jnp.where(odd, rim_a[r : r + 1, :], rim_b[r : r + 1, :])

    count = u.shape[0]
    last, top = slice(rows - 1, rows), slice(0, 1)
    for s in sections:
        stiff = jnp.where(has_below, half[s, 1, last, :], 0.0)
        f = flow(*[below(2 * s + c) - u[s, c, last, :] for c in range(2)], stiff)
        stiff = jnp.where(strip > 0, above(2 * count + s), 0.0)
        g = flow(*[u[s, c, top, :] - above(2 * s + c) for c in range(2)], stiff)
        for c in range(2):
            total[s, c, last, :] += f[c]
            total[s, c, top, :] -= g[c]


def fast_flows(u, after, fast, index, splat, total, which):
    sections, _, rows, width = u.shape
    for j in which:
        own, block, hops = pairs_of(after, sections)[j]
        stiff = wide_splat(splat, FAST + hops - 1, width)
        for rb in range(rows // ROWS):
            f = side_flow(u, own, fast, 2 * block * rows, index, j, stiff, rb)
            for c in range(2):
                total[own, c, rows_of(rb), :] += f[c]


def first_rims_kernel(u, w, total_in, half, fast, rim_a, rim_b, shift, splat, total, index):
    sections, _, rows, _ = u.shape

    def damp(rb, carry):
        at = rows_of(rb)
        new = [total[s, c, at, :] + DAMPING * w[s, c, at, :] for s in range(sections) for c in range(2)]
        for k, value in enumerate(new):
            total[k // 2, k % 2, at, :] = value
        return carry

    lax.fori_loop(0, rows // ROWS, damp, 0)

    def body(after):
        put_index(not after, shift, fast, 4 * rows, index)
        fast_flows(u, not after, fast, index, splat, total, range(3))

    by_side(body)
    rim_flows(u, half, rim_a, rim_b, total, range(sections))


def later_rims_kernel(
    u, total_in, half, fast, rim_a, rim_b, index, splat, total, out_u, out_w, new_u, new_w, sem
):
    sections, _, rows, width = u.shape

    def body(after):
        near = (near_of(after, sections), second_of(after, sections))
        done = [s for s in range(sections) if s not in near]
        fast_flows(u, not after, fast, index, splat, total, (0, 2))
        rim_flows(u, half, rim_a, rim_b, total, done)
        copies = []
        for k, s in enumerate(done):
            moving = wide_splat(splat, MOVING + s, width)
            for rb in range(rows // ROWS):
                at = rows_of(rb)
                for c in range(2):
                    v = total[s, c, at, :] * moving
                    new_w[k, c, at, :] = v
                    new_u[k, c, at, :] = u[s, c, at, :] + STEP * v
            copies += [
                pltpu.make_async_copy(new_u.at[k], out_u.at[s], sem.at[2 * k]),
                pltpu.make_async_copy(new_w.at[k], out_w.at[s], sem.at[2 * k + 1]),
            ]
        for copy in copies:
            copy.start()
        fast_flows(u, not after, fast, index, splat, total, (1,))
        rim_flows(u, half, rim_a, rim_b, total, near)
        for copy in copies:
            copy.wait()

    by_side(body)


def slow_values(u, after, arrived, index, splat, total, j, rb):
    sections, _, rows, width = u.shape
    own = pairs_of(after, sections)[j][0]
    value = [total[own, c, rows_of(rb), :] for c in range(2)]
    for p, (section, block, hops) in enumerate(pairs_of(after, sections)):
        if section == own:
            stiff = wide_splat(splat, SLOW + hops - 1, width)
            f = side_flow(u, own, arrived, 2 * block * rows, index, p, stiff, rb)
            value = [value[c] + f[c] for c in range(2)]
    return value


def step_kernel(
    u, total, arrived, half, shift, splat, new_u, new_w, slow, fast, index, rim_a, rim_b
):
    sections, _, rows, width = u.shape

    def body(after):
        put_index(after, shift, arrived, 4 * rows, index)
        slow_edge = (near_of(after, sections), second_of(after, sections))
        fast_edge = (near_of(not after, sections), second_of(not after, sections))
        for s in range(sections):
            moving = wide_splat(splat, MOVING + s, width)
            for rb in range(rows // ROWS):
                at = rows_of(rb)
                if s in slow_edge:
                    value = slow_values(u, after, arrived, index, splat, total, slow_edge.index(s), rb)
                else:
                    value = [total[s, c, at, :] for c in range(2)]
                for c in range(2):
                    v = value[c] * moving
                    moved = u[s, c, at, :] + STEP * v
                    new_w[s, c, at, :] = v
                    new_u[s, c, at, :] = moved
                    for edge, out in ((slow_edge, slow), (fast_edge, fast)):
                        if s in edge:
                            first = (2 * edge.index(s) + c) * rows
                            out[pl.ds(first + rb * ROWS, ROWS), :] = moved

    by_side(body)
    last = slice(rows - 1, rows)
    put_rims(
        lambda s, c: new_u[s, c, 0:1, :],
        lambda s, c: new_u[s, c, last, :],
        lambda s: half[s, 1, last, :],
        rim_a,
        rim_b,
        sections,
    )


def last_kernel(u, total, arrived, index, splat, out_u_in, out_w_in, out_u, out_w, new_u, new_w, sem):
    sections, _, rows, width = u.shape
    rbs = rows // ROWS
    part = rbs // 2 if rbs % 2 == 0 else rbs

    def body(after):
        copies = []
        for j in range(2):
            own = pairs_of(after, sections)[j][0]
            moving = wide_splat(splat, MOVING + own, width)
            for rb in range(rbs):
                at = rows_of(rb)
                value = slow_values(u, after, arrived, index, splat, total, j, rb)
                for c in range(2):
                    v = value[c] * moving
                    new_w[j, c, at, :] = v
                    new_u[j, c, at, :] = u[own, c, at, :] + STEP * v
                if (rb + 1) % part == 0:
                    block = pl.ds((rb + 1 - part) * ROWS, part * ROWS)
                    for source, target in ((new_u, out_u), (new_w, out_w)):
                        copy = pltpu.make_async_copy(
                            source.at[j, :, block], target.at[own, :, block], sem.at[len(copies)]
                        )
                        copy.start()
                        copies.append(copy)
        for copy in copies:
            copy.wait()

    by_side(body)


def call(kernel, outs, ins, alias=None, scratch=(), in_specs=None, out_specs=None, limit=16 << 20, cost=None):
    return pl.pallas_call(
        kernel,
        out_shape=outs,
        in_specs=in_specs or [VMEM] * len(ins),
        out_specs=out_specs or [VMEM] * len(outs),
        input_output_aliases=alias or {},
        scratch_shapes=scratch,
        cost_estimate=cost,
        compiler_params=pltpu.CompilerParams(vmem_limit_bytes=limit),
    )(*ins)


def per_device(u, w, cls, shift, fixed, stiff, cross):
    sections, _, rows, width = u.shape

    def array(*shape, dtype=jnp.float32):
        return jax.ShapeDtypeStruct(shape, dtype)

    full = array(*u.shape)
    tail = array(tail_rows(rows), width)
    two = array(4 * rows, width)
    two_tail = array(4 * rows + tail.shape[0], width)
    rim = array(-(-3 * sections // ROWS) * ROWS, width)
    splat = array(MOVING + sections, ROWS, COLS)
    index = array(3, tail.shape[0], width, dtype=jnp.int32)
    scalars = [pltpu.SMEM(shift.shape, jnp.int32), pltpu.SemaphoreType.DMA]

    ends = pltpu.VMEM((sections, 2, ROWS, width), jnp.float32)
    slow, fast, rim_a, rim_b, splat = call(
        lead_kernel,
        [two_tail, two_tail, rim, rim, splat],
        [u, cls, shift, stiff, cross, fixed],
        scratch=[
            pltpu.VMEM(shift.shape, jnp.int32),
            pltpu.SMEM(stiff.shape, jnp.float32),
            pltpu.SMEM(cross.shape, jnp.float32),
            pltpu.SMEM(fixed.shape, jnp.int32),
            ends,
            ends,
            pltpu.VMEM((sections, ROWS, width), jnp.int32),
            pltpu.VMEM(tail.shape, jnp.float32),
            pltpu.VMEM(rim.shape, jnp.float32),
            pltpu.VMEM(rim.shape, jnp.float32),
            pltpu.VMEM(splat.shape, jnp.float32),
            pltpu.SemaphoreType.DMA((20,)),
        ],
        in_specs=[ANY] * 6,
        out_specs=[ANY] * 5,
        limit=LEAD_LIMIT,
    )
    slow, fast, rim_a, rim_b = call(
        hand_on_kernel,
        [two_tail, two_tail, rim, rim],
        [slow, fast, rim_a, rim_b],
        {k: k for k in range(4)},
        in_specs=[ANY] * 4,
        out_specs=[ANY] * 4,
    )
    slow = exchange(slow, "sec", "b")
    fast = exchange(fast, "sec", "a")
    rim_a = exchange(rim_a, "strip", "a")
    rim_b = exchange(rim_b, "strip", "b")
    total, half = call(
        first_inside_kernel, [full, full], [u, cls, shift, splat], scratch=scalars
    )
    total, fast_index = call(
        first_rims_kernel,
        [full, index],
        [u, w, total, half, fast, rim_a, rim_b, shift, splat],
        {2: 0},
    )
    u, w, slow, fast, index, rim_a, rim_b = call(
        step_kernel,
        [full, full, two, two, index, rim, rim],
        [u, total, slow, half, shift, splat],
    )
    slow = exchange(slow, "sec", "b")
    fast = exchange(fast, "sec", "a")
    rim_a = exchange(rim_a, "strip", "a")
    rim_b = exchange(rim_b, "strip", "b")
    (total,) = call(later_inside_kernel, [full], [u, w, half, shift, splat], scratch=scalars)
    done = max(sections - 2, 1)
    total, out_u, out_w = call(
        later_rims_kernel,
        [full, full, full],
        [u, total, half, fast, rim_a, rim_b, fast_index, splat],
        {1: 0},
        scratch=[pltpu.VMEM((done, 2, rows, width), jnp.float32)] * 2
        + [pltpu.SemaphoreType.DMA((2 * done,))],
        out_specs=[VMEM, ANY, ANY],
    )
    return tuple(
        call(
            last_kernel,
            [full, full],
            [u, total, slow, index, splat, out_u, out_w],
            {5: 0, 6: 1},
            scratch=[pltpu.VMEM((2, 2, rows, width), jnp.float32)] * 2
            + [pltpu.SemaphoreType.DMA((8,))],
            in_specs=[VMEM] * 5 + [ANY] * 2,
            out_specs=[ANY] * 2,
        )
    )


def solution(mesh):
    block = P("sec", None, "strip", None)
    return jax.shard_map(
        per_device,
        mesh=mesh,
        in_specs=(block, block, block, block, P("sec"), P(), P()),
        out_specs=(block, block),
        check_vma=False,
    )
```

```python
import jax
import jax.numpy as jnp
from jax import lax
from jax.experimental import pallas as pl
from jax.experimental.pallas import tpu as pltpu
from jax.sharding import PartitionSpec as P

ROWS = 8
COLS = 128
CLASSES = 8
DAMPING = 0.9
STEP = 0.35

VMEM = pl.BlockSpec(memory_space=pltpu.VMEM)
ANY = pl.BlockSpec(memory_space=pl.ANY)

INSIDE, SLOW, FAST, TABLE, MOVING = 0, 2, 4, 6, 7


def exchange(value, axis, pairing):
    n = lax.axis_size(axis)
    first = 0 if pairing == "a" else 1
    route = []
    for i in range(first, n - 1, 2):
        route += [(i, i + 1), (i + 1, i)]
    return lax.ppermute(value, axis, route)


def slow_after():
    return lax.rem(lax.axis_index("sec"), 2) == 1


def by_side(body):
    after = slow_after()

    @pl.when(after)
    def _():
        body(True)

    @pl.when(jnp.logical_not(after))
    def _():
        body(False)


def near_of(after, sections):
    return sections - 1 if after else 0


def second_of(after, sections):
    return sections - 2 if after else 1


def pairs_of(after, sections):
    near, second = near_of(after, sections), second_of(after, sections)
    return ((near, 0, 1), (second, 0, 2), (near, 1, 2))


def inverse(value):
    guess = pl.reciprocal(value, approx=True)
    return guess * (2.0 - value * guess)


def flow(ex, ey, half):
    gain = half * (3.0 - inverse(1.0 + ex * ex + ey * ey))
    return gain * ex, gain * ey


def cols_of(cb):
    return slice(cb * COLS, (cb + 1) * COLS)


def rows_of(rb):
    start = rb * ROWS
    return pl.ds(start if isinstance(start, int) else pl.multiple_of(start, ROWS), ROWS)


def tail_rows(rows):
    return -(-(rows // ROWS) // ROWS) * ROWS


def per_tile(width, make):
    return jnp.concatenate([make(cb) for cb in range(width // COLS)], axis=1)


def turned(wide, amounts):
    return per_tile(wide.shape[1], lambda cb: pltpu.roll(wide[:, cols_of(cb)], amounts[cb], 1))


def gathered(wide, index):
    def one(cb):
        full = jnp.broadcast_to(index[:, cols_of(cb)], (ROWS, COLS))
        return jnp.take_along_axis(wide[:, cols_of(cb)], full, axis=1, mode="promise_in_bounds")

    return per_tile(wide.shape[1], one)


def spread(blocks, width):
    return per_tile(width, lambda cb: jnp.broadcast_to(blocks[:, cb : cb + 1], (blocks.shape[0], COLS)))


def lanes(rows, width):
    return lax.broadcasted_iota(jnp.int32, (rows, width), 1) & (COLS - 1)


def put_index(after, shift, before, index):
    sections, _, rbs, _ = shift.shape
    width = index.shape[2]
    lane = lanes(rbs, width)
    for j, (own, block, hops) in enumerate(pairs_of(after, sections)):
        if after:
            offset = spread(shift[own, hops - 1], width)
        else:
            offset = -spread(before[sections - 1 - block, hops - 1], width)
        index[j, 0:rbs, :] = (lane + offset) & (COLS - 1)


def put_rims(first_of, last_of, kv_of, rim_a, rim_b, sections):
    odd = lax.rem(lax.axis_index("strip"), 2) == 1

    def put(line, first, last):
        rim_a[line : line + 1, :] = jnp.where(odd, first, last)
        rim_b[line : line + 1, :] = jnp.where(odd, last, first)

    for s in range(sections):
        for c in range(2):
            put(2 * s + c, first_of(s, c), last_of(s, c))
        stiff = kv_of(s)
        put(2 * sections + s, stiff, stiff)


def look_up(table, index):
    def one(cb):
        tile = jnp.broadcast_to(index[:, cols_of(cb)], (ROWS, COLS))
        return jnp.take_along_axis(table, tile, axis=1, mode="promise_in_bounds")[: index.shape[0]]

    return per_tile(index.shape[1], one)


def put_splat(stiff, cross, fixed, splat):
    sections = fixed.shape[0]
    i, n = lax.axis_index("sec"), lax.axis_size("sec")
    odd = slow_after()
    tile = (ROWS, COLS)
    lane = lax.broadcasted_iota(jnp.int32, tile, 1)
    slow_there = jnp.where(odd, i < n - 1, i > 0)
    fast_there = jnp.where(odd, i > 0, i < n - 1)
    for h in range(2):
        k = jnp.full(tile, cross[h] * (0.5 * STEP))
        splat[INSIDE + h] = k
        splat[SLOW + h] = jnp.where(slow_there, k, 0.0)
        splat[FAST + h] = jnp.where(fast_there, k, 0.0)
    table = jnp.zeros(tile, jnp.float32)
    for k in range(CLASSES):
        table = jnp.where(lane == k, stiff[k] * (0.5 * STEP), table)
    splat[TABLE] = table
    for s in range(sections):
        splat[MOVING + s] = jnp.full(tile, jnp.where(fixed[s] == 0, 1.0, 0.0))


def lead_kernel(u, slow, fast):
    sections, _, rows, _ = u.shape

    def body(after):
        for out, side in ((slow, after), (fast, not after)):
            for k, own in enumerate((near_of(side, sections), second_of(side, sections))):
                for c in range(2):
                    out[(2 * k + c) * rows : (2 * k + c + 1) * rows, :] = u[own, c]

    by_side(body)


def prepare_kernel(u, cls, before, stiff, cross, fixed, rim_a, rim_b, splat):
    sections, _, rows, _ = u.shape
    last = slice(rows - 1, rows)
    put_splat(stiff, cross, fixed, splat)
    table = splat[TABLE]
    put_rims(
        lambda s, c: u[s, c, 0:1, :],
        lambda s, c: u[s, c, last, :],
        lambda s: look_up(table, cls[s, 1, last, :]),
        rim_a,
        rim_b,
        sections,
    )


def wide_splat(splat, k, width):
    tile = splat[k]
    return per_tile(width, lambda cb: tile)


def chosen(values, index):
    for bit in range(3):
        on = (index & (1 << bit)) != 0
        values = [jnp.where(on, values[k + 1], values[k]) for k in range(0, len(values), 2)]
    return values[0]


def inside(u, w, total, half_across, half_below, shift, splat, scalars, sem):
    sections, _, rows, width = u.shape
    rbs, cbs = rows // ROWS, width // COLS
    load = pltpu.make_async_copy(shift, scalars, sem)
    load.start()
    bottom = lax.broadcasted_iota(jnp.int32, (rows, COLS), 0) == rows - 1

    def below(cb, carry):
        at = pl.ds(pl.multiple_of(cb * COLS, COLS), COLS)
        for s in range(sections):
            x, y = u[s, 0, :, at], u[s, 1, :, at]
            half = jnp.where(bottom, 0.0, half_below(s, at))
            f = flow(pltpu.roll(x, rows - 1, 0) - x, pltpu.roll(y, rows - 1, 0) - y, half)
            new = [f[c] - pltpu.roll(f[c], 1, 0) for c in range(2)]
            if w is not None:
                new = [DAMPING * w[s, c, :, at] + new[c] for c in range(2)]
            for c in range(2):
                total[s, c, :, at] = new[c]
        return carry

    lax.fori_loop(0, cbs, below, 0)
    load.wait()
    last = lax.broadcasted_iota(jnp.int32, (ROWS, width), 1) == width - 1

    def row(rb, carry):
        at = rows_of(rb)
        add = [[total[s, c, at, :] for c in range(2)] for s in range(sections)]
        for s in range(sections):
            x, y = u[s, 0, at, :], u[s, 1, at, :]
            half = jnp.where(last, 0.0, half_across(s, at))
            f = flow(pltpu.roll(x, width - 1, 1) - x, pltpu.roll(y, width - 1, 1) - y, half)
            for c in range(2):
                add[s][c] = add[s][c] + (f[c] - pltpu.roll(f[c], 1, 1))
        for hops in (1, 2):
            half = wide_splat(splat, INSIDE + hops - 1, width)
            for s in range(sections - hops):
                offsets = [scalars[s, hops - 1, rb, cb] for cb in range(cbs)]
                there = [(-o) & (COLS - 1) for o in offsets]
                back = [o & (COLS - 1) for o in offsets]
                e = [turned(u[s + hops, c, at, :], there) - u[s, c, at, :] for c in range(2)]
                f = flow(e[0], e[1], half)
                for c in range(2):
                    add[s][c] = add[s][c] + f[c]
                    add[s + hops][c] = add[s + hops][c] - turned(f[c], back)
        for s in range(sections):
            for c in range(2):
                total[s, c, at, :] = add[s][c]
        return carry

    lax.fori_loop(0, rbs, row, 0)


def first_inside_kernel(u, cls, shift, splat, total, half, scalars, sem):
    table = splat[TABLE]
    values = [jnp.broadcast_to(table[:, k : k + 1], (ROWS, COLS)) for k in range(CLASSES)]
    rows = u.shape[2]

    def half_across(s, at):
        index = cls[s, 0, at, :]
        k = per_tile(index.shape[1], lambda cb: chosen(values, index[:, cols_of(cb)]))
        half[s, 0, at, :] = k
        return k

    def half_below(s, at):
        index = cls[s, 1, :, at]
        k = jnp.concatenate(
            [look_up(table, index[r : r + ROWS]) for r in range(0, rows, ROWS)], axis=0
        )
        half[s, 1, :, at] = k
        return k

    inside(u, None, total, half_across, half_below, shift, splat, scalars, sem)


def later_inside_kernel(u, w, half, shift, splat, total, scalars, sem):
    def half_across(s, at):
        return half[s, 0, at, :]

    def half_below(s, at):
        return half[s, 1, :, at]

    inside(u, w, total, half_across, half_below, shift, splat, scalars, sem)


def side_flow(u, own, arrived, first, index, j, half, rb):
    rows = u.shape[2]
    at = rows_of(rb)
    number = index[j, rb : rb + 1, :]
    e = [
        gathered(arrived[pl.ds(first + c * rows + rb * ROWS, ROWS), :], number) - u[own, c, at, :]
        for c in range(2)
    ]
    return flow(e[0], e[1], half)


def rim_flows(u, half, rim_a, rim_b, total, sections):
    rows = u.shape[2]
    strip = lax.axis_index("strip")
    odd = lax.rem(strip, 2) == 1
    has_below = strip < lax.axis_size("strip") - 1

    def below(r):
        return jnp.where(odd, rim_b[r : r + 1, :], rim_a[r : r + 1, :])

    def above(r):
        return jnp.where(odd, rim_a[r : r + 1, :], rim_b[r : r + 1, :])

    count = u.shape[0]
    last, top = slice(rows - 1, rows), slice(0, 1)
    for s in sections:
        stiff = jnp.where(has_below, half[s, 1, last, :], 0.0)
        f = flow(*[below(2 * s + c) - u[s, c, last, :] for c in range(2)], stiff)
        stiff = jnp.where(strip > 0, above(2 * count + s), 0.0)
        g = flow(*[u[s, c, top, :] - above(2 * s + c) for c in range(2)], stiff)
        for c in range(2):
            total[s, c, last, :] += f[c]
            total[s, c, top, :] -= g[c]


def fast_flows(u, after, fast, index, splat, total, which):
    sections, _, rows, width = u.shape
    for j in which:
        own, block, hops = pairs_of(after, sections)[j]
        stiff = wide_splat(splat, FAST + hops - 1, width)
        for rb in range(rows // ROWS):
            f = side_flow(u, own, fast, 2 * block * rows, index, j, stiff, rb)
            for c in range(2):
                total[own, c, rows_of(rb), :] += f[c]


def first_rims_kernel(u, w, total_in, half, fast, rim_a, rim_b, shift, before, splat, total, index):
    sections, _, rows, _ = u.shape

    def damp(rb, carry):
        at = rows_of(rb)
        new = [total[s, c, at, :] + DAMPING * w[s, c, at, :] for s in range(sections) for c in range(2)]
        for k, value in enumerate(new):
            total[k // 2, k % 2, at, :] = value
        return carry

    lax.fori_loop(0, rows // ROWS, damp, 0)

    def body(after):
        put_index(not after, shift, before, index)
        fast_flows(u, not after, fast, index, splat, total, range(3))

    by_side(body)
    rim_flows(u, half, rim_a, rim_b, total, range(sections))


def later_rims_kernel(
    u, total_in, half, fast, rim_a, rim_b, index, splat, total, out_u, out_w, new_u, new_w, sem
):
    sections, _, rows, width = u.shape

    def body(after):
        near = (near_of(after, sections), second_of(after, sections))
        done = [s for s in range(sections) if s not in near]
        fast_flows(u, not after, fast, index, splat, total, (0, 2))
        rim_flows(u, half, rim_a, rim_b, total, done)
        copies = []
        for k, s in enumerate(done):
            moving = wide_splat(splat, MOVING + s, width)
            for rb in range(rows // ROWS):
                at = rows_of(rb)
                for c in range(2):
                    v = total[s, c, at, :] * moving
                    new_w[k, c, at, :] = v
                    new_u[k, c, at, :] = u[s, c, at, :] + STEP * v
            copies += [
                pltpu.make_async_copy(new_u.at[k], out_u.at[s], sem.at[2 * k]),
                pltpu.make_async_copy(new_w.at[k], out_w.at[s], sem.at[2 * k + 1]),
            ]
        for copy in copies:
            copy.start()
        fast_flows(u, not after, fast, index, splat, total, (1,))
        rim_flows(u, half, rim_a, rim_b, total, near)
        for copy in copies:
            copy.wait()

    by_side(body)


def slow_values(u, after, arrived, index, splat, total, j, rb):
    sections, _, rows, width = u.shape
    own = pairs_of(after, sections)[j][0]
    value = [total[own, c, rows_of(rb), :] for c in range(2)]
    for p, (section, block, hops) in enumerate(pairs_of(after, sections)):
        if section == own:
            stiff = wide_splat(splat, SLOW + hops - 1, width)
            f = side_flow(u, own, arrived, 2 * block * rows, index, p, stiff, rb)
            value = [value[c] + f[c] for c in range(2)]
    return value


def step_kernel(
    u, total, arrived, half, shift, before, splat,
    new_u, new_w, slow, fast, index, rim_a, rim_b,
):
    sections, _, rows, width = u.shape

    def body(after):
        put_index(after, shift, before, index)
        slow_edge = (near_of(after, sections), second_of(after, sections))
        fast_edge = (near_of(not after, sections), second_of(not after, sections))
        for s in range(sections):
            moving = wide_splat(splat, MOVING + s, width)
            for rb in range(rows // ROWS):
                at = rows_of(rb)
                if s in slow_edge:
                    value = slow_values(u, after, arrived, index, splat, total, slow_edge.index(s), rb)
                else:
                    value = [total[s, c, at, :] for c in range(2)]
                for c in range(2):
                    v = value[c] * moving
                    moved = u[s, c, at, :] + STEP * v
                    new_w[s, c, at, :] = v
                    new_u[s, c, at, :] = moved
                    for edge, out in ((slow_edge, slow), (fast_edge, fast)):
                        if s in edge:
                            first = (2 * edge.index(s) + c) * rows
                            out[pl.ds(first + rb * ROWS, ROWS), :] = moved

    by_side(body)
    last = slice(rows - 1, rows)
    put_rims(
        lambda s, c: new_u[s, c, 0:1, :],
        lambda s, c: new_u[s, c, last, :],
        lambda s: half[s, 1, last, :],
        rim_a,
        rim_b,
        sections,
    )


def last_kernel(u, total, arrived, index, splat, out_u_in, out_w_in, out_u, out_w, new_u, new_w, sem):
    sections, _, rows, width = u.shape
    rbs = rows // ROWS
    part = rbs // 2 if rbs % 2 == 0 else rbs

    def body(after):
        copies = []
        for j in range(2):
            own = pairs_of(after, sections)[j][0]
            moving = wide_splat(splat, MOVING + own, width)
            for rb in range(rbs):
                at = rows_of(rb)
                value = slow_values(u, after, arrived, index, splat, total, j, rb)
                for c in range(2):
                    v = value[c] * moving
                    new_w[j, c, at, :] = v
                    new_u[j, c, at, :] = u[own, c, at, :] + STEP * v
                if (rb + 1) % part == 0:
                    block = pl.ds((rb + 1 - part) * ROWS, part * ROWS)
                    for source, target in ((new_u, out_u), (new_w, out_w)):
                        copy = pltpu.make_async_copy(
                            source.at[j, :, block], target.at[own, :, block], sem.at[len(copies)]
                        )
                        copy.start()
                        copies.append(copy)
        for copy in copies:
            copy.wait()

    by_side(body)


def call(kernel, outs, ins, alias=None, scratch=(), in_specs=None, out_specs=None, limit=16 << 20, cost=None):
    return pl.pallas_call(
        kernel,
        out_shape=outs,
        in_specs=in_specs or [VMEM] * len(ins),
        out_specs=out_specs or [VMEM] * len(outs),
        input_output_aliases=alias or {},
        scratch_shapes=scratch,
        cost_estimate=cost,
        compiler_params=pltpu.CompilerParams(vmem_limit_bytes=limit),
    )(*ins)


def per_device(u, w, cls, shift, fixed, stiff, cross):
    sections, _, rows, width = u.shape

    def array(*shape, dtype=jnp.float32):
        return jax.ShapeDtypeStruct(shape, dtype)

    full = array(*u.shape)
    two = array(4 * rows, width)
    rim = array(-(-3 * sections // ROWS) * ROWS, width)
    splat = array(MOVING + sections, ROWS, COLS)
    index = array(3, tail_rows(rows), width, dtype=jnp.int32)
    scalars = [pltpu.SMEM(shift.shape, jnp.int32), pltpu.SemaphoreType.DMA]
    smem = pl.BlockSpec(memory_space=pltpu.SMEM)

    n = lax.axis_size("sec")
    before = lax.ppermute(shift, "sec", [(i, i + 1) for i in range(n - 1)])
    slow, fast = call(lead_kernel, [two, two], [u])
    slow = exchange(slow, "sec", "b")
    fast = exchange(fast, "sec", "a")
    rim_a, rim_b, splat = call(
        prepare_kernel,
        [rim, rim, splat],
        [u, cls, before, stiff, cross, fixed],
        in_specs=[VMEM] * 3 + [smem] * 3,
    )
    rim_a = exchange(rim_a, "strip", "a")
    rim_b = exchange(rim_b, "strip", "b")
    total, half = call(
        first_inside_kernel, [full, full], [u, cls, shift, splat], scratch=scalars
    )
    total, fast_index = call(
        first_rims_kernel,
        [full, index],
        [u, w, total, half, fast, rim_a, rim_b, shift, before, splat],
        {2: 0},
    )
    u, w, slow, fast, index, rim_a, rim_b = call(
        step_kernel,
        [full, full, two, two, index, rim, rim],
        [u, total, slow, half, shift, before, splat],
    )
    slow = exchange(slow, "sec", "b")
    fast = exchange(fast, "sec", "a")
    rim_a = exchange(rim_a, "strip", "a")
    rim_b = exchange(rim_b, "strip", "b")
    (total,) = call(later_inside_kernel, [full], [u, w, half, shift, splat], scratch=scalars)
    done = max(sections - 2, 1)
    total, out_u, out_w = call(
        later_rims_kernel,
        [full, full, full],
        [u, total, half, fast, rim_a, rim_b, fast_index, splat],
        {1: 0},
        scratch=[pltpu.VMEM((done, 2, rows, width), jnp.float32)] * 2
        + [pltpu.SemaphoreType.DMA((2 * done,))],
        out_specs=[VMEM, ANY, ANY],
    )
    return tuple(
        call(
            last_kernel,
            [full, full],
            [u, total, slow, index, splat, out_u, out_w],
            {5: 0, 6: 1},
            scratch=[pltpu.VMEM((2, 2, rows, width), jnp.float32)] * 2
            + [pltpu.SemaphoreType.DMA((8,))],
            in_specs=[VMEM] * 5 + [ANY] * 2,
            out_specs=[ANY] * 2,
        )
    )


def solution(mesh):
    block = P("sec", None, "strip", None)
    return jax.shard_map(
        per_device,
        mesh=mesh,
        in_specs=(block, block, block, block, P("sec"), P(), P()),
        out_specs=(block, block),
        check_vma=False,
    )
```

```python
import jax
import jax.numpy as jnp
from jax import lax
from jax.experimental import pallas as pl
from jax.experimental.pallas import tpu as pltpu
from jax.sharding import PartitionSpec as P

ROWS = 8
COLS = 128
CLASSES = 8
DAMPING = 0.9
STEP = 0.35

VMEM = pl.BlockSpec(memory_space=pltpu.VMEM)
ANY = pl.BlockSpec(memory_space=pl.ANY)

INSIDE, SLOW, FAST, TABLE, MOVING = 0, 2, 4, 6, 7


def exchange(value, axis, pairing):
    n = lax.axis_size(axis)
    first = 0 if pairing == "a" else 1
    route = []
    for i in range(first, n - 1, 2):
        route += [(i, i + 1), (i + 1, i)]
    return lax.ppermute(value, axis, route)


def slow_after():
    return lax.rem(lax.axis_index("sec"), 2) == 1


def by_side(body):
    after = slow_after()

    @pl.when(after)
    def _():
        body(True)

    @pl.when(jnp.logical_not(after))
    def _():
        body(False)


def near_of(after, sections):
    return sections - 1 if after else 0


def second_of(after, sections):
    return sections - 2 if after else 1


def pairs_of(after, sections):
    near, second = near_of(after, sections), second_of(after, sections)
    return ((near, 0, 1), (second, 0, 2), (near, 1, 2))


def inverse(value):
    guess = pl.reciprocal(value, approx=True)
    return guess * (2.0 - value * guess)


def flow(ex, ey, half):
    gain = half * (3.0 - inverse(1.0 + ex * ex + ey * ey))
    return gain * ex, gain * ey


def cols_of(cb):
    return slice(cb * COLS, (cb + 1) * COLS)


def rows_of(rb):
    start = rb * ROWS
    return pl.ds(start if isinstance(start, int) else pl.multiple_of(start, ROWS), ROWS)


def tail_rows(rows):
    return -(-(rows // ROWS) // ROWS) * ROWS


def per_tile(width, make):
    return jnp.concatenate([make(cb) for cb in range(width // COLS)], axis=1)


def turned(wide, amounts):
    return per_tile(wide.shape[1], lambda cb: pltpu.roll(wide[:, cols_of(cb)], amounts[cb], 1))


def gathered(wide, index):
    def one(cb):
        full = jnp.broadcast_to(index[:, cols_of(cb)], (ROWS, COLS))
        return jnp.take_along_axis(wide[:, cols_of(cb)], full, axis=1, mode="promise_in_bounds")

    return per_tile(wide.shape[1], one)


def spread(blocks, width):
    return per_tile(width, lambda cb: jnp.broadcast_to(blocks[:, cb : cb + 1], (blocks.shape[0], COLS)))


def lanes(rows, width):
    return lax.broadcasted_iota(jnp.int32, (rows, width), 1) & (COLS - 1)


def put_tail(shift, out, first, width):
    sections, _, rbs, _ = shift.shape
    lane = lanes(rbs, width)
    parts = [
        spread(shift[s, h], width)
        for s, h in ((sections - 1, 0), (sections - 1, 1), (sections - 2, 1))
    ]
    mixed = jnp.where(lane == 0, parts[0], jnp.where(lane == 1, parts[1], parts[2]))
    out[first : first + rbs, :] = mixed.astype(jnp.float32)


def put_index(after, shift, arrived, first, index):
    sections, _, rbs, _ = shift.shape
    width = index.shape[2]
    lane = lanes(rbs, width)
    for j, (own, _, hops) in enumerate(pairs_of(after, sections)):
        if after:
            offset = spread(shift[own, hops - 1], width)
        else:
            blocks = per_tile(
                width,
                lambda cb: jnp.broadcast_to(
                    arrived[first : first + rbs, cb * COLS + j : cb * COLS + j + 1], (rbs, COLS)
                ),
            )
            offset = -blocks.astype(jnp.int32)
        index[j, 0:rbs, :] = (lane + offset) & (COLS - 1)


def put_rims(first_of, last_of, kv_of, rim_a, rim_b, sections):
    odd = lax.rem(lax.axis_index("strip"), 2) == 1

    def put(line, first, last):
        rim_a[line : line + 1, :] = jnp.where(odd, first, last)
        rim_b[line : line + 1, :] = jnp.where(odd, last, first)

    for s in range(sections):
        for c in range(2):
            put(2 * s + c, first_of(s, c), last_of(s, c))
        stiff = kv_of(s)
        put(2 * sections + s, stiff, stiff)


def look_up(table, index):
    def one(cb):
        tile = jnp.broadcast_to(index[:, cols_of(cb)], (ROWS, COLS))
        return jnp.take_along_axis(table, tile, axis=1, mode="promise_in_bounds")[: index.shape[0]]

    return per_tile(index.shape[1], one)


def put_splat(stiff, cross, fixed, splat):
    sections = fixed.shape[0]
    i, n = lax.axis_index("sec"), lax.axis_size("sec")
    odd = slow_after()
    tile = (ROWS, COLS)
    lane = lax.broadcasted_iota(jnp.int32, tile, 1)
    slow_there = jnp.where(odd, i < n - 1, i > 0)
    fast_there = jnp.where(odd, i > 0, i < n - 1)
    for h in range(2):
        k = jnp.full(tile, cross[h] * (0.5 * STEP))
        splat[INSIDE + h] = k
        splat[SLOW + h] = jnp.where(slow_there, k, 0.0)
        splat[FAST + h] = jnp.where(fast_there, k, 0.0)
    table = jnp.zeros(tile, jnp.float32)
    for k in range(CLASSES):
        table = jnp.where(lane == k, stiff[k] * (0.5 * STEP), table)
    splat[TABLE] = table
    for s in range(sections):
        splat[MOVING + s] = jnp.full(tile, jnp.where(fixed[s] == 0, 1.0, 0.0))


def lead_kernel(u, shift, slow, fast):
    sections, _, rows, width = u.shape

    def body(after):
        for out, side in ((slow, after), (fast, not after)):
            for k, own in enumerate((near_of(side, sections), second_of(side, sections))):
                for c in range(2):
                    out[(2 * k + c) * rows : (2 * k + c + 1) * rows, :] = u[own, c]

    by_side(body)
    put_tail(shift, slow, 4 * rows, width)
    after_blocks = slice(4 * rows, slow.shape[0])
    fast[after_blocks, :] = slow[after_blocks, :]


def prepare_kernel(u, cls, arrived, stiff, cross, fixed, rim_a, rim_b, splat):
    sections, _, rows, _ = u.shape
    last = slice(rows - 1, rows)
    put_splat(stiff, cross, fixed, splat)
    table = splat[TABLE]
    put_rims(
        lambda s, c: u[s, c, 0:1, :],
        lambda s, c: u[s, c, last, :],
        lambda s: look_up(table, cls[s, 1, last, :]),
        rim_a,
        rim_b,
        sections,
    )


def wide_splat(splat, k, width):
    tile = splat[k]
    return per_tile(width, lambda cb: tile)


def chosen(values, index):
    for bit in range(3):
        on = (index & (1 << bit)) != 0
        values = [jnp.where(on, values[k + 1], values[k]) for k in range(0, len(values), 2)]
    return values[0]


def inside(u, w, total, half_across, half_below, shift, splat, scalars, sem):
    sections, _, rows, width = u.shape
    rbs, cbs = rows // ROWS, width // COLS
    load = pltpu.make_async_copy(shift, scalars, sem)
    load.start()
    bottom = lax.broadcasted_iota(jnp.int32, (rows, COLS), 0) == rows - 1

    def below(cb, carry):
        at = pl.ds(pl.multiple_of(cb * COLS, COLS), COLS)
        for s in range(sections):
            x, y = u[s, 0, :, at], u[s, 1, :, at]
            half = jnp.where(bottom, 0.0, half_below(s, at))
            f = flow(pltpu.roll(x, rows - 1, 0) - x, pltpu.roll(y, rows - 1, 0) - y, half)
            new = [f[c] - pltpu.roll(f[c], 1, 0) for c in range(2)]
            if w is not None:
                new = [DAMPING * w[s, c, :, at] + new[c] for c in range(2)]
            for c in range(2):
                total[s, c, :, at] = new[c]
        return carry

    lax.fori_loop(0, cbs, below, 0)
    load.wait()
    last = lax.broadcasted_iota(jnp.int32, (ROWS, width), 1) == width - 1

    def row(rb, carry):
        at = rows_of(rb)
        add = [[total[s, c, at, :] for c in range(2)] for s in range(sections)]
        for s in range(sections):
            x, y = u[s, 0, at, :], u[s, 1, at, :]
            half = jnp.where(last, 0.0, half_across(s, at))
            f = flow(pltpu.roll(x, width - 1, 1) - x, pltpu.roll(y, width - 1, 1) - y, half)
            for c in range(2):
                add[s][c] = add[s][c] + (f[c] - pltpu.roll(f[c], 1, 1))
        for hops in (1, 2):
            half = wide_splat(splat, INSIDE + hops - 1, width)
            for s in range(sections - hops):
                offsets = [scalars[s, hops - 1, rb, cb] for cb in range(cbs)]
                there = [(-o) & (COLS - 1) for o in offsets]
                back = [o & (COLS - 1) for o in offsets]
                e = [turned(u[s + hops, c, at, :], there) - u[s, c, at, :] for c in range(2)]
                f = flow(e[0], e[1], half)
                for c in range(2):
                    add[s][c] = add[s][c] + f[c]
                    add[s + hops][c] = add[s + hops][c] - turned(f[c], back)
        for s in range(sections):
            for c in range(2):
                total[s, c, at, :] = add[s][c]
        return carry

    lax.fori_loop(0, rbs, row, 0)


def first_inside_kernel(u, cls, shift, splat, total, half, scalars, sem):
    table = splat[TABLE]
    values = [jnp.broadcast_to(table[:, k : k + 1], (ROWS, COLS)) for k in range(CLASSES)]
    rows = u.shape[2]

    def half_across(s, at):
        index = cls[s, 0, at, :]
        k = per_tile(index.shape[1], lambda cb: chosen(values, index[:, cols_of(cb)]))
        half[s, 0, at, :] = k
        return k

    def half_below(s, at):
        index = cls[s, 1, :, at]
        k = jnp.concatenate(
            [look_up(table, index[r : r + ROWS]) for r in range(0, rows, ROWS)], axis=0
        )
        half[s, 1, :, at] = k
        return k

    inside(u, None, total, half_across, half_below, shift, splat, scalars, sem)


def later_inside_kernel(u, w, half, shift, splat, total, scalars, sem):
    def half_across(s, at):
        return half[s, 0, at, :]

    def half_below(s, at):
        return half[s, 1, :, at]

    inside(u, w, total, half_across, half_below, shift, splat, scalars, sem)


def side_flow(u, own, arrived, first, index, j, half, rb):
    rows = u.shape[2]
    at = rows_of(rb)
    number = index[j, rb : rb + 1, :]
    e = [
        gathered(arrived[pl.ds(first + c * rows + rb * ROWS, ROWS), :], number) - u[own, c, at, :]
        for c in range(2)
    ]
    return flow(e[0], e[1], half)


def rim_flows(u, half, rim_a, rim_b, total, sections):
    rows = u.shape[2]
    strip = lax.axis_index("strip")
    odd = lax.rem(strip, 2) == 1
    has_below = strip < lax.axis_size("strip") - 1

    def below(r):
        return jnp.where(odd, rim_b[r : r + 1, :], rim_a[r : r + 1, :])

    def above(r):
        return jnp.where(odd, rim_a[r : r + 1, :], rim_b[r : r + 1, :])

    count = u.shape[0]
    last, top = slice(rows - 1, rows), slice(0, 1)
    for s in sections:
        stiff = jnp.where(has_below, half[s, 1, last, :], 0.0)
        f = flow(*[below(2 * s + c) - u[s, c, last, :] for c in range(2)], stiff)
        stiff = jnp.where(strip > 0, above(2 * count + s), 0.0)
        g = flow(*[u[s, c, top, :] - above(2 * s + c) for c in range(2)], stiff)
        for c in range(2):
            total[s, c, last, :] += f[c]
            total[s, c, top, :] -= g[c]


def fast_flows(u, after, fast, index, splat, total, which):
    sections, _, rows, width = u.shape
    for j in which:
        own, block, hops = pairs_of(after, sections)[j]
        stiff = wide_splat(splat, FAST + hops - 1, width)
        for rb in range(rows // ROWS):
            f = side_flow(u, own, fast, 2 * block * rows, index, j, stiff, rb)
            for c in range(2):
                total[own, c, rows_of(rb), :] += f[c]


def first_rims_kernel(u, w, total_in, half, fast, rim_a, rim_b, shift, splat, total, index):
    sections, _, rows, _ = u.shape

    def damp(rb, carry):
        at = rows_of(rb)
        new = [total[s, c, at, :] + DAMPING * w[s, c, at, :] for s in range(sections) for c in range(2)]
        for k, value in enumerate(new):
            total[k // 2, k % 2, at, :] = value
        return carry

    lax.fori_loop(0, rows // ROWS, damp, 0)

    def body(after):
        put_index(not after, shift, fast, 4 * rows, index)
        fast_flows(u, not after, fast, index, splat, total, range(3))

    by_side(body)
    rim_flows(u, half, rim_a, rim_b, total, range(sections))


def later_rims_kernel(
    u, total_in, half, fast, rim_a, rim_b, index, splat, total, out_u, out_w, new_u, new_w, sem
):
    sections, _, rows, width = u.shape

    def body(after):
        near = (near_of(after, sections), second_of(after, sections))
        done = [s for s in range(sections) if s not in near]
        fast_flows(u, not after, fast, index, splat, total, (0, 2))
        rim_flows(u, half, rim_a, rim_b, total, done)
        copies = []
        for k, s in enumerate(done):
            moving = wide_splat(splat, MOVING + s, width)
            for rb in range(rows // ROWS):
                at = rows_of(rb)
                for c in range(2):
                    v = total[s, c, at, :] * moving
                    new_w[k, c, at, :] = v
                    new_u[k, c, at, :] = u[s, c, at, :] + STEP * v
            copies += [
                pltpu.make_async_copy(new_u.at[k], out_u.at[s], sem.at[2 * k]),
                pltpu.make_async_copy(new_w.at[k], out_w.at[s], sem.at[2 * k + 1]),
            ]
        for copy in copies:
            copy.start()
        fast_flows(u, not after, fast, index, splat, total, (1,))
        rim_flows(u, half, rim_a, rim_b, total, near)
        for copy in copies:
            copy.wait()

    by_side(body)


def slow_values(u, after, arrived, index, splat, total, j, rb):
    sections, _, rows, width = u.shape
    own = pairs_of(after, sections)[j][0]
    value = [total[own, c, rows_of(rb), :] for c in range(2)]
    for p, (section, block, hops) in enumerate(pairs_of(after, sections)):
        if section == own:
            stiff = wide_splat(splat, SLOW + hops - 1, width)
            f = side_flow(u, own, arrived, 2 * block * rows, index, p, stiff, rb)
            value = [value[c] + f[c] for c in range(2)]
    return value


def step_kernel(
    u, total, arrived, half, shift, splat,
    new_u, new_w, slow, fast, index, rim_a, rim_b,
):
    sections, _, rows, width = u.shape

    def body(after):
        put_index(after, shift, arrived, 4 * rows, index)
        slow_edge = (near_of(after, sections), second_of(after, sections))
        fast_edge = (near_of(not after, sections), second_of(not after, sections))
        for s in range(sections):
            moving = wide_splat(splat, MOVING + s, width)
            for rb in range(rows // ROWS):
                at = rows_of(rb)
                if s in slow_edge:
                    value = slow_values(u, after, arrived, index, splat, total, slow_edge.index(s), rb)
                else:
                    value = [total[s, c, at, :] for c in range(2)]
                for c in range(2):
                    v = value[c] * moving
                    moved = u[s, c, at, :] + STEP * v
                    new_w[s, c, at, :] = v
                    new_u[s, c, at, :] = moved
                    for edge, out in ((slow_edge, slow), (fast_edge, fast)):
                        if s in edge:
                            first = (2 * edge.index(s) + c) * rows
                            out[pl.ds(first + rb * ROWS, ROWS), :] = moved

    by_side(body)
    last = slice(rows - 1, rows)
    put_rims(
        lambda s, c: new_u[s, c, 0:1, :],
        lambda s, c: new_u[s, c, last, :],
        lambda s: half[s, 1, last, :],
        rim_a,
        rim_b,
        sections,
    )


def last_kernel(u, total, arrived, index, splat, out_u_in, out_w_in, out_u, out_w, new_u, new_w, sem):
    sections, _, rows, width = u.shape
    rbs = rows // ROWS
    part = rbs // 2 if rbs % 2 == 0 else rbs

    def body(after):
        copies = []
        for j in range(2):
            own = pairs_of(after, sections)[j][0]
            moving = wide_splat(splat, MOVING + own, width)
            for rb in range(rbs):
                at = rows_of(rb)
                value = slow_values(u, after, arrived, index, splat, total, j, rb)
                for c in range(2):
                    v = value[c] * moving
                    new_w[j, c, at, :] = v
                    new_u[j, c, at, :] = u[own, c, at, :] + STEP * v
                if (rb + 1) % part == 0:
                    block = pl.ds((rb + 1 - part) * ROWS, part * ROWS)
                    for source, target in ((new_u, out_u), (new_w, out_w)):
                        copy = pltpu.make_async_copy(
                            source.at[j, :, block], target.at[own, :, block], sem.at[len(copies)]
                        )
                        copy.start()
                        copies.append(copy)
        for copy in copies:
            copy.wait()

    by_side(body)


def call(kernel, outs, ins, alias=None, scratch=(), in_specs=None, out_specs=None, limit=16 << 20, cost=None):
    return pl.pallas_call(
        kernel,
        out_shape=outs,
        in_specs=in_specs or [VMEM] * len(ins),
        out_specs=out_specs or [VMEM] * len(outs),
        input_output_aliases=alias or {},
        scratch_shapes=scratch,
        cost_estimate=cost,
        compiler_params=pltpu.CompilerParams(vmem_limit_bytes=limit),
    )(*ins)


def per_device(u, w, cls, shift, fixed, stiff, cross):
    sections, _, rows, width = u.shape

    def array(*shape, dtype=jnp.float32):
        return jax.ShapeDtypeStruct(shape, dtype)

    full = array(*u.shape)
    two = array(4 * rows, width)
    rim = array(-(-3 * sections // ROWS) * ROWS, width)
    splat = array(MOVING + sections, ROWS, COLS)
    index = array(3, tail_rows(rows), width, dtype=jnp.int32)
    scalars = [pltpu.SMEM(shift.shape, jnp.int32), pltpu.SemaphoreType.DMA]
    smem = pl.BlockSpec(memory_space=pltpu.SMEM)

    two_tail = array(4 * rows + index.shape[1], width)
    slow, fast = call(lead_kernel, [two_tail, two_tail], [u, shift])
    slow = exchange(slow, "sec", "b")
    fast = exchange(fast, "sec", "a")
    rim_a, rim_b, splat = call(
        prepare_kernel,
        [rim, rim, splat],
        [u, cls, fast, stiff, cross, fixed],
        in_specs=[VMEM] * 2 + [ANY] + [smem] * 3,
    )
    rim_a = exchange(rim_a, "strip", "a")
    rim_b = exchange(rim_b, "strip", "b")
    total, half = call(
        first_inside_kernel, [full, full], [u, cls, shift, splat], scratch=scalars
    )
    total, fast_index = call(
        first_rims_kernel,
        [full, index],
        [u, w, total, half, fast, rim_a, rim_b, shift, splat],
        {2: 0},
    )
    u, w, slow, fast, index, rim_a, rim_b = call(
        step_kernel,
        [full, full, two, two, index, rim, rim],
        [u, total, slow, half, shift, splat],
    )
    slow = exchange(slow, "sec", "b")
    fast = exchange(fast, "sec", "a")
    rim_a = exchange(rim_a, "strip", "a")
    rim_b = exchange(rim_b, "strip", "b")
    (total,) = call(later_inside_kernel, [full], [u, w, half, shift, splat], scratch=scalars)
    done = max(sections - 2, 1)
    total, out_u, out_w = call(
        later_rims_kernel,
        [full, full, full],
        [u, total, half, fast, rim_a, rim_b, fast_index, splat],
        {1: 0},
        scratch=[pltpu.VMEM((done, 2, rows, width), jnp.float32)] * 2
        + [pltpu.SemaphoreType.DMA((2 * done,))],
        out_specs=[VMEM, ANY, ANY],
    )
    return tuple(
        call(
            last_kernel,
            [full, full],
            [u, total, slow, index, splat, out_u, out_w],
            {5: 0, 6: 1},
            scratch=[pltpu.VMEM((2, 2, rows, width), jnp.float32)] * 2
            + [pltpu.SemaphoreType.DMA((8,))],
            in_specs=[VMEM] * 5 + [ANY] * 2,
            out_specs=[ANY] * 2,
        )
    )


def solution(mesh):
    block = P("sec", None, "strip", None)
    return jax.shard_map(
        per_device,
        mesh=mesh,
        in_specs=(block, block, block, block, P("sec"), P(), P()),
        out_specs=(block, block),
        check_vma=False,
    )
```

```python
import functools

import jax
import jax.numpy as jnp
from jax import lax
from jax.experimental import pallas as pl
from jax.experimental.pallas import tpu as pltpu
from jax.sharding import PartitionSpec as P

ROWS = 8
COLS = 128
CLASSES = 8
DAMPING = 0.9
STEP = 0.35

VMEM = pl.BlockSpec(memory_space=pltpu.VMEM)
ANY = pl.BlockSpec(memory_space=pl.ANY)

INSIDE, SLOW, FAST, TABLE, MOVING = 0, 2, 4, 6, 7


def exchange(value, axis, pairing):
    n = lax.axis_size(axis)
    first = 0 if pairing == "a" else 1
    route = []
    for i in range(first, n - 1, 2):
        route += [(i, i + 1), (i + 1, i)]
    return lax.ppermute(value, axis, route)


def slow_after():
    return lax.rem(lax.axis_index("sec"), 2) == 1


def by_side(body):
    after = slow_after()

    @pl.when(after)
    def _():
        body(True)

    @pl.when(jnp.logical_not(after))
    def _():
        body(False)


def near_of(after, sections):
    return sections - 1 if after else 0


def second_of(after, sections):
    return sections - 2 if after else 1


def pairs_of(after, sections):
    near, second = near_of(after, sections), second_of(after, sections)
    return ((near, 0, 1), (second, 0, 2), (near, 1, 2))


def inverse(value):
    guess = pl.reciprocal(value, approx=True)
    return guess * (2.0 - value * guess)


def flow(ex, ey, half):
    gain = half * (3.0 - inverse(1.0 + ex * ex + ey * ey))
    return gain * ex, gain * ey


def cols_of(cb):
    return slice(cb * COLS, (cb + 1) * COLS)


def rows_of(rb):
    start = rb * ROWS
    return pl.ds(start if isinstance(start, int) else pl.multiple_of(start, ROWS), ROWS)


def tail_rows(rows):
    return -(-(rows // ROWS) // ROWS) * ROWS


def per_tile(width, make):
    return jnp.concatenate([make(cb) for cb in range(width // COLS)], axis=1)


def turned(wide, amounts):
    return per_tile(wide.shape[1], lambda cb: pltpu.roll(wide[:, cols_of(cb)], amounts[cb], 1))


def gathered(wide, index):
    def one(cb):
        full = jnp.broadcast_to(index[:, cols_of(cb)], (ROWS, COLS))
        return jnp.take_along_axis(wide[:, cols_of(cb)], full, axis=1, mode="promise_in_bounds")

    return per_tile(wide.shape[1], one)


def spread(blocks, width):
    return per_tile(width, lambda cb: jnp.broadcast_to(blocks[:, cb : cb + 1], (blocks.shape[0], COLS)))


def lanes(rows, width):
    return lax.broadcasted_iota(jnp.int32, (rows, width), 1) & (COLS - 1)


def put_tail(shift, out, first, width):
    sections, _, rbs, _ = shift.shape
    lane = lanes(rbs, width)
    parts = [
        spread(shift[s, h], width)
        for s, h in ((sections - 1, 0), (sections - 1, 1), (sections - 2, 1))
    ]
    mixed = jnp.where(lane == 0, parts[0], jnp.where(lane == 1, parts[1], parts[2]))
    out[first : first + rbs, :] = mixed.astype(jnp.float32)


def put_index(after, shift, arrived, first, index):
    sections, _, rbs, _ = shift.shape
    width = index.shape[2]
    lane = lanes(rbs, width)
    for j, (own, _, hops) in enumerate(pairs_of(after, sections)):
        if after:
            offset = spread(shift[own, hops - 1], width)
        else:
            blocks = per_tile(
                width,
                lambda cb: jnp.broadcast_to(
                    arrived[first : first + rbs, cb * COLS + j : cb * COLS + j + 1], (rbs, COLS)
                ),
            )
            offset = -blocks.astype(jnp.int32)
        index[j, 0:rbs, :] = (lane + offset) & (COLS - 1)


def put_rims(first_of, last_of, kv_of, rim_a, rim_b, sections):
    odd = lax.rem(lax.axis_index("strip"), 2) == 1

    def put(line, first, last):
        rim_a[line : line + 1, :] = jnp.where(odd, first, last)
        rim_b[line : line + 1, :] = jnp.where(odd, last, first)

    for s in range(sections):
        for c in range(2):
            put(2 * s + c, first_of(s, c), last_of(s, c))
        stiff = kv_of(s)
        put(2 * sections + s, stiff, stiff)


def look_up(table, index):
    def one(cb):
        tile = jnp.broadcast_to(index[:, cols_of(cb)], (ROWS, COLS))
        return jnp.take_along_axis(table, tile, axis=1, mode="promise_in_bounds")[: index.shape[0]]

    return per_tile(index.shape[1], one)


def put_splat(stiff, cross, fixed, splat):
    sections = fixed.shape[0]
    i, n = lax.axis_index("sec"), lax.axis_size("sec")
    odd = slow_after()
    tile = (ROWS, COLS)
    lane = lax.broadcasted_iota(jnp.int32, tile, 1)
    slow_there = jnp.where(odd, i < n - 1, i > 0)
    fast_there = jnp.where(odd, i > 0, i < n - 1)
    for h in range(2):
        k = jnp.full(tile, cross[h] * (0.5 * STEP))
        splat[INSIDE + h] = k
        splat[SLOW + h] = jnp.where(slow_there, k, 0.0)
        splat[FAST + h] = jnp.where(fast_there, k, 0.0)
    table = jnp.zeros(tile, jnp.float32)
    for k in range(CLASSES):
        table = jnp.where(lane == k, stiff[k] * (0.5 * STEP), table)
    splat[TABLE] = table
    for s in range(sections):
        splat[MOVING + s] = jnp.full(tile, jnp.where(fixed[s] == 0, 1.0, 0.0))


def lead_kernel(u, shift, slow, fast):
    sections, _, rows, width = u.shape

    def body(after):
        for out, side in ((slow, after), (fast, not after)):
            for k, own in enumerate((near_of(side, sections), second_of(side, sections))):
                for c in range(2):
                    out[(2 * k + c) * rows : (2 * k + c + 1) * rows, :] = u[own, c]

    by_side(body)
    put_tail(shift, slow, 4 * rows, width)
    after_blocks = slice(4 * rows, slow.shape[0])
    fast[after_blocks, :] = slow[after_blocks, :]


def prepare_kernel(u, cls, arrived, stiff, cross, fixed, rim_a, rim_b, splat):
    sections, _, rows, _ = u.shape
    last = slice(rows - 1, rows)
    put_splat(stiff, cross, fixed, splat)
    table = splat[TABLE]
    put_rims(
        lambda s, c: u[s, c, 0:1, :],
        lambda s, c: u[s, c, last, :],
        lambda s: look_up(table, cls[s, 1, last, :]),
        rim_a,
        rim_b,
        sections,
    )


def wide_splat(splat, k, width):
    tile = splat[k]
    return per_tile(width, lambda cb: tile)


def chosen(values, index):
    for bit in range(3):
        on = (index & (1 << bit)) != 0
        values = [jnp.where(on, values[k + 1], values[k]) for k in range(0, len(values), 2)]
    return values[0]


def inside(u, w, total, half_across, half_below, shift, splat, scalars, sem):
    sections, _, rows, width = u.shape
    rbs, cbs = rows // ROWS, width // COLS
    load = pltpu.make_async_copy(shift, scalars, sem)
    load.start()
    bottom = lax.broadcasted_iota(jnp.int32, (rows, COLS), 0) == rows - 1

    def below(cb, carry):
        at = pl.ds(pl.multiple_of(cb * COLS, COLS), COLS)
        for s in range(sections):
            x, y = u[s, 0, :, at], u[s, 1, :, at]
            half = jnp.where(bottom, 0.0, half_below(s, at))
            f = flow(pltpu.roll(x, rows - 1, 0) - x, pltpu.roll(y, rows - 1, 0) - y, half)
            new = [f[c] - pltpu.roll(f[c], 1, 0) for c in range(2)]
            if w is not None:
                new = [DAMPING * w[s, c, :, at] + new[c] for c in range(2)]
            for c in range(2):
                total[s, c, :, at] = new[c]
        return carry

    lax.fori_loop(0, cbs, below, 0)
    load.wait()
    last = lax.broadcasted_iota(jnp.int32, (ROWS, width), 1) == width - 1

    def row(rb, carry):
        at = rows_of(rb)
        add = [[total[s, c, at, :] for c in range(2)] for s in range(sections)]
        for s in range(sections):
            x, y = u[s, 0, at, :], u[s, 1, at, :]
            half = jnp.where(last, 0.0, half_across(s, at))
            f = flow(pltpu.roll(x, width - 1, 1) - x, pltpu.roll(y, width - 1, 1) - y, half)
            for c in range(2):
                add[s][c] = add[s][c] + (f[c] - pltpu.roll(f[c], 1, 1))
        for hops in (1, 2):
            half = wide_splat(splat, INSIDE + hops - 1, width)
            for s in range(sections - hops):
                offsets = [scalars[s, hops - 1, rb, cb] for cb in range(cbs)]
                there = [(-o) & (COLS - 1) for o in offsets]
                back = [o & (COLS - 1) for o in offsets]
                e = [turned(u[s + hops, c, at, :], there) - u[s, c, at, :] for c in range(2)]
                f = flow(e[0], e[1], half)
                for c in range(2):
                    add[s][c] = add[s][c] + f[c]
                    add[s + hops][c] = add[s + hops][c] - turned(f[c], back)
        for s in range(sections):
            for c in range(2):
                total[s, c, at, :] = add[s][c]
        return carry

    lax.fori_loop(0, rbs, row, 0)


def first_inside_kernel(u, cls, shift, splat, total, half, scalars, sem):
    table = splat[TABLE]
    values = [jnp.broadcast_to(table[:, k : k + 1], (ROWS, COLS)) for k in range(CLASSES)]
    rows = u.shape[2]

    def half_across(s, at):
        index = cls[s, 0, at, :]
        k = per_tile(index.shape[1], lambda cb: chosen(values, index[:, cols_of(cb)]))
        half[s, 0, at, :] = k
        return k

    def half_below(s, at):
        index = cls[s, 1, :, at]
        k = jnp.concatenate(
            [look_up(table, index[r : r + ROWS]) for r in range(0, rows, ROWS)], axis=0
        )
        half[s, 1, :, at] = k
        return k

    inside(u, None, total, half_across, half_below, shift, splat, scalars, sem)


def later_inside_kernel(u, w, half, shift, splat, total, scalars, sem):
    def half_across(s, at):
        return half[s, 0, at, :]

    def half_below(s, at):
        return half[s, 1, :, at]

    inside(u, w, total, half_across, half_below, shift, splat, scalars, sem)


def side_flow(u, own, arrived, block, height, base, index, j, half, rb):
    at = rows_of(rb)
    number = index[j, rb : rb + 1, :]
    e = [
        gathered(arrived[pl.ds((2 * block + c) * height + rb * ROWS - base, ROWS), :], number)
        - u[own, c, at, :]
        for c in range(2)
    ]
    return flow(e[0], e[1], half)


def rim_flows(u, half, rim_a, rim_b, total, sections):
    rows = u.shape[2]
    strip = lax.axis_index("strip")
    odd = lax.rem(strip, 2) == 1
    has_below = strip < lax.axis_size("strip") - 1

    def below(r):
        return jnp.where(odd, rim_b[r : r + 1, :], rim_a[r : r + 1, :])

    def above(r):
        return jnp.where(odd, rim_a[r : r + 1, :], rim_b[r : r + 1, :])

    count = u.shape[0]
    last, top = slice(rows - 1, rows), slice(0, 1)
    for s in sections:
        stiff = jnp.where(has_below, half[s, 1, last, :], 0.0)
        f = flow(*[below(2 * s + c) - u[s, c, last, :] for c in range(2)], stiff)
        stiff = jnp.where(strip > 0, above(2 * count + s), 0.0)
        g = flow(*[u[s, c, top, :] - above(2 * s + c) for c in range(2)], stiff)
        for c in range(2):
            total[s, c, last, :] += f[c]
            total[s, c, top, :] -= g[c]


def fast_flows(u, after, fast, index, splat, total, which):
    sections, _, rows, width = u.shape
    for j in which:
        own, block, hops = pairs_of(after, sections)[j]
        stiff = wide_splat(splat, FAST + hops - 1, width)
        for rb in range(rows // ROWS):
            f = side_flow(u, own, fast, block, rows, 0, index, j, stiff, rb)
            for c in range(2):
                total[own, c, rows_of(rb), :] += f[c]


def first_rims_kernel(u, w, total_in, half, fast, rim_a, rim_b, shift, splat, total, index):
    sections, _, rows, _ = u.shape

    def damp(rb, carry):
        at = rows_of(rb)
        new = [total[s, c, at, :] + DAMPING * w[s, c, at, :] for s in range(sections) for c in range(2)]
        for k, value in enumerate(new):
            total[k // 2, k % 2, at, :] = value
        return carry

    lax.fori_loop(0, rows // ROWS, damp, 0)

    def body(after):
        put_index(not after, shift, fast, 4 * rows, index)
        fast_flows(u, not after, fast, index, splat, total, range(3))

    by_side(body)
    rim_flows(u, half, rim_a, rim_b, total, range(sections))


def later_rims_kernel(
    u, total_in, half, fast, rim_a, rim_b, index, splat, total, out_u, out_w, new_u, new_w, sem
):
    sections, _, rows, width = u.shape

    def body(after):
        near = (near_of(after, sections), second_of(after, sections))
        done = [s for s in range(sections) if s not in near]
        fast_flows(u, not after, fast, index, splat, total, (0, 2))
        rim_flows(u, half, rim_a, rim_b, total, done)
        copies = []
        for k, s in enumerate(done):
            moving = wide_splat(splat, MOVING + s, width)
            for rb in range(rows // ROWS):
                at = rows_of(rb)
                for c in range(2):
                    v = total[s, c, at, :] * moving
                    new_w[k, c, at, :] = v
                    new_u[k, c, at, :] = u[s, c, at, :] + STEP * v
            copies += [
                pltpu.make_async_copy(new_u.at[k], out_u.at[s], sem.at[2 * k]),
                pltpu.make_async_copy(new_w.at[k], out_w.at[s], sem.at[2 * k + 1]),
            ]
        for copy in copies:
            copy.start()
        fast_flows(u, not after, fast, index, splat, total, (1,))
        rim_flows(u, half, rim_a, rim_b, total, near)
        for copy in copies:
            copy.wait()

    by_side(body)


def slow_values(u, after, arrived, height, base, index, splat, total, j, rb):
    sections, _, rows, width = u.shape
    own = pairs_of(after, sections)[j][0]
    value = [total[own, c, rows_of(rb), :] for c in range(2)]
    for p, (section, block, hops) in enumerate(pairs_of(after, sections)):
        if section == own:
            stiff = wide_splat(splat, SLOW + hops - 1, width)
            f = side_flow(u, own, arrived, block, height, base, index, p, stiff, rb)
            value = [value[c] + f[c] for c in range(2)]
    return value


def step_kernel(
    u, total, arrived, half, shift, splat,
    new_u, new_w, slow_top, slow_rest, fast, index, rim_a, rim_b,
):
    sections, _, rows, width = u.shape
    top = slow_top.shape[0] // 4

    def body(after):
        put_index(after, shift, arrived, 4 * rows, index)
        slow_edge = (near_of(after, sections), second_of(after, sections))
        fast_edge = (near_of(not after, sections), second_of(not after, sections))
        for s in range(sections):
            moving = wide_splat(splat, MOVING + s, width)
            for rb in range(rows // ROWS):
                at, row = rows_of(rb), rb * ROWS
                if s in slow_edge:
                    value = slow_values(
                        u, after, arrived, rows, 0, index, splat, total, slow_edge.index(s), rb
                    )
                else:
                    value = [total[s, c, at, :] for c in range(2)]
                for c in range(2):
                    v = value[c] * moving
                    moved = u[s, c, at, :] + STEP * v
                    new_w[s, c, at, :] = v
                    new_u[s, c, at, :] = moved
                    if s in fast_edge:
                        fast[pl.ds((2 * fast_edge.index(s) + c) * rows + row, ROWS), :] = moved
                    if s in slow_edge:
                        k = 2 * slow_edge.index(s) + c
                        if row < top:
                            slow_top[pl.ds(k * top + row, ROWS), :] = moved
                        else:
                            slow_rest[pl.ds(k * (rows - top) + row - top, ROWS), :] = moved

    by_side(body)
    last = slice(rows - 1, rows)
    put_rims(
        lambda s, c: new_u[s, c, 0:1, :],
        lambda s, c: new_u[s, c, last, :],
        lambda s: half[s, 1, last, :],
        rim_a,
        rim_b,
        sections,
    )


def last_kernel(
    base, u, total, arrived, index, splat, out_u_in, out_w_in, out_u, out_w, new_u, new_w, sem
):
    sections, _, rows, width = u.shape
    height = arrived.shape[0] // 4
    rbs = height // ROWS
    part = rbs // 2 if rbs % 2 == 0 else rbs

    def body(after):
        copies = []
        for j in range(2):
            own = pairs_of(after, sections)[j][0]
            moving = wide_splat(splat, MOVING + own, width)
            for k in range(rbs):
                rb = base // ROWS + k
                value = slow_values(u, after, arrived, height, base, index, splat, total, j, rb)
                for c in range(2):
                    v = value[c] * moving
                    new_w[j, c, rows_of(k), :] = v
                    new_u[j, c, rows_of(k), :] = u[own, c, rows_of(rb), :] + STEP * v
                if (k + 1) % part == 0:
                    here = pl.ds((k + 1 - part) * ROWS, part * ROWS)
                    there = pl.ds(base + (k + 1 - part) * ROWS, part * ROWS)
                    for source, target in ((new_u, out_u), (new_w, out_w)):
                        copy = pltpu.make_async_copy(
                            source.at[j, :, here], target.at[own, :, there], sem.at[len(copies)]
                        )
                        copy.start()
                        copies.append(copy)
        for copy in copies:
            copy.wait()

    by_side(body)


def call(kernel, outs, ins, alias=None, scratch=(), in_specs=None, out_specs=None, limit=16 << 20, cost=None):
    return pl.pallas_call(
        kernel,
        out_shape=outs,
        in_specs=in_specs or [VMEM] * len(ins),
        out_specs=out_specs or [VMEM] * len(outs),
        input_output_aliases=alias or {},
        scratch_shapes=scratch,
        cost_estimate=cost,
        compiler_params=pltpu.CompilerParams(vmem_limit_bytes=limit),
    )(*ins)


def per_device(u, w, cls, shift, fixed, stiff, cross):
    sections, _, rows, width = u.shape

    def array(*shape, dtype=jnp.float32):
        return jax.ShapeDtypeStruct(shape, dtype)

    full = array(*u.shape)
    two = array(4 * rows, width)
    rim = array(-(-3 * sections // ROWS) * ROWS, width)
    splat = array(MOVING + sections, ROWS, COLS)
    index = array(3, tail_rows(rows), width, dtype=jnp.int32)
    scalars = [pltpu.SMEM(shift.shape, jnp.int32), pltpu.SemaphoreType.DMA]
    smem = pl.BlockSpec(memory_space=pltpu.SMEM)

    two_tail = array(4 * rows + index.shape[1], width)
    slow, fast = call(lead_kernel, [two_tail, two_tail], [u, shift])
    slow = exchange(slow, "sec", "b")
    fast = exchange(fast, "sec", "a")
    rim_a, rim_b, splat = call(
        prepare_kernel,
        [rim, rim, splat],
        [u, cls, fast, stiff, cross, fixed],
        in_specs=[VMEM] * 2 + [ANY] + [smem] * 3,
    )
    rim_a = exchange(rim_a, "strip", "a")
    rim_b = exchange(rim_b, "strip", "b")
    total, half = call(
        first_inside_kernel, [full, full], [u, cls, shift, splat], scratch=scalars
    )
    total, fast_index = call(
        first_rims_kernel,
        [full, index],
        [u, w, total, half, fast, rim_a, rim_b, shift, splat],
        {2: 0},
    )
    top = max(rows // ROWS * 3 // 4, 1) * ROWS
    u, w, slow_top, slow_rest, fast, index, rim_a, rim_b = call(
        step_kernel,
        [full, full, array(4 * top, width), array(4 * (rows - top), width), two, index, rim, rim],
        [u, total, slow, half, shift, splat],
    )
    slow_top = exchange(slow_top, "sec", "b")
    slow_rest = exchange(slow_rest, "sec", "b")
    fast = exchange(fast, "sec", "a")
    rim_a = exchange(rim_a, "strip", "a")
    rim_b = exchange(rim_b, "strip", "b")
    (total,) = call(later_inside_kernel, [full], [u, w, half, shift, splat], scratch=scalars)
    done = max(sections - 2, 1)
    total, out_u, out_w = call(
        later_rims_kernel,
        [full, full, full],
        [u, total, half, fast, rim_a, rim_b, fast_index, splat],
        {1: 0},
        scratch=[pltpu.VMEM((done, 2, rows, width), jnp.float32)] * 2
        + [pltpu.SemaphoreType.DMA((2 * done,))],
        out_specs=[VMEM, ANY, ANY],
    )
    for base, arrived in ((0, slow_top), (top, slow_rest)):
        height = arrived.shape[0] // 4
        out_u, out_w = call(
            functools.partial(last_kernel, base),
            [full, full],
            [u, total, arrived, index, splat, out_u, out_w],
            {5: 0, 6: 1},
            scratch=[pltpu.VMEM((2, 2, height, width), jnp.float32)] * 2
            + [pltpu.SemaphoreType.DMA((8,))],
            in_specs=[VMEM] * 5 + [ANY] * 2,
            out_specs=[ANY] * 2,
        )
    return out_u, out_w


def solution(mesh):
    block = P("sec", None, "strip", None)
    return jax.shard_map(
        per_device,
        mesh=mesh,
        in_specs=(block, block, block, block, P("sec"), P(), P()),
        out_specs=(block, block),
        check_vma=False,
    )
```

```python
import functools

import jax
import jax.numpy as jnp
from jax import lax
from jax.experimental import pallas as pl
from jax.experimental.pallas import tpu as pltpu
from jax.sharding import PartitionSpec as P

ROWS = 8
COLS = 128
CLASSES = 8
DAMPING = 0.9
STEP = 0.35

VMEM = pl.BlockSpec(memory_space=pltpu.VMEM)
ANY = pl.BlockSpec(memory_space=pl.ANY)

INSIDE, SLOW, FAST, TABLE, MOVING = 0, 2, 4, 6, 7


def exchange(value, axis, pairing):
    n = lax.axis_size(axis)
    first = 0 if pairing == "a" else 1
    route = []
    for i in range(first, n - 1, 2):
        route += [(i, i + 1), (i + 1, i)]
    return lax.ppermute(value, axis, route)


def slow_after():
    return lax.rem(lax.axis_index("sec"), 2) == 1


def by_side(body):
    after = slow_after()

    @pl.when(after)
    def _():
        body(True)

    @pl.when(jnp.logical_not(after))
    def _():
        body(False)


def near_of(after, sections):
    return sections - 1 if after else 0


def second_of(after, sections):
    return sections - 2 if after else 1


def pairs_of(after, sections):
    near, second = near_of(after, sections), second_of(after, sections)
    return ((near, 0, 1), (second, 0, 2), (near, 1, 2))


def inverse(value):
    guess = pl.reciprocal(value, approx=True)
    return guess * (2.0 - value * guess)


def flow(ex, ey, half):
    gain = half * (3.0 - inverse(1.0 + ex * ex + ey * ey))
    return gain * ex, gain * ey


def cols_of(cb):
    return slice(cb * COLS, (cb + 1) * COLS)


def rows_of(rb):
    start = rb * ROWS
    return pl.ds(start if isinstance(start, int) else pl.multiple_of(start, ROWS), ROWS)


def tail_rows(rows):
    return -(-(rows // ROWS) // ROWS) * ROWS


def per_tile(width, make):
    return jnp.concatenate([make(cb) for cb in range(width // COLS)], axis=1)


def turned(wide, amounts):
    return per_tile(wide.shape[1], lambda cb: pltpu.roll(wide[:, cols_of(cb)], amounts[cb], 1))


def gathered(wide, index):
    def one(cb):
        full = jnp.broadcast_to(index[:, cols_of(cb)], (ROWS, COLS))
        return jnp.take_along_axis(wide[:, cols_of(cb)], full, axis=1, mode="promise_in_bounds")

    return per_tile(wide.shape[1], one)


def spread(blocks, width):
    return per_tile(width, lambda cb: jnp.broadcast_to(blocks[:, cb : cb + 1], (blocks.shape[0], COLS)))


def lanes(rows, width):
    return lax.broadcasted_iota(jnp.int32, (rows, width), 1) & (COLS - 1)


def put_tail(shift, out, first, width):
    sections, _, rbs, _ = shift.shape
    lane = lanes(rbs, width)
    parts = [
        spread(shift[s, h], width)
        for s, h in ((sections - 1, 0), (sections - 1, 1), (sections - 2, 1))
    ]
    mixed = jnp.where(lane == 0, parts[0], jnp.where(lane == 1, parts[1], parts[2]))
    out[first : first + rbs, :] = mixed.astype(jnp.float32)


def put_index(after, shift, arrived, first, index):
    sections, _, rbs, _ = shift.shape
    width = index.shape[2]
    lane = lanes(rbs, width)
    for j, (own, _, hops) in enumerate(pairs_of(after, sections)):
        if after:
            offset = spread(shift[own, hops - 1], width)
        else:
            blocks = per_tile(
                width,
                lambda cb: jnp.broadcast_to(
                    arrived[first : first + rbs, cb * COLS + j : cb * COLS + j + 1], (rbs, COLS)
                ),
            )
            offset = -blocks.astype(jnp.int32)
        index[j, 0:rbs, :] = (lane + offset) & (COLS - 1)


def put_rims(first_of, last_of, kv_of, rim_a, rim_b, sections):
    odd = lax.rem(lax.axis_index("strip"), 2) == 1

    def put(line, first, last):
        rim_a[line : line + 1, :] = jnp.where(odd, first, last)
        rim_b[line : line + 1, :] = jnp.where(odd, last, first)

    for s in range(sections):
        for c in range(2):
            put(2 * s + c, first_of(s, c), last_of(s, c))
        stiff = kv_of(s)
        put(2 * sections + s, stiff, stiff)


def look_up(table, index):
    def one(cb):
        tile = jnp.broadcast_to(index[:, cols_of(cb)], (ROWS, COLS))
        return jnp.take_along_axis(table, tile, axis=1, mode="promise_in_bounds")[: index.shape[0]]

    return per_tile(index.shape[1], one)


def put_splat(stiff, cross, fixed, splat):
    sections = fixed.shape[0]
    i, n = lax.axis_index("sec"), lax.axis_size("sec")
    odd = slow_after()
    tile = (ROWS, COLS)
    lane = lax.broadcasted_iota(jnp.int32, tile, 1)
    slow_there = jnp.where(odd, i < n - 1, i > 0)
    fast_there = jnp.where(odd, i > 0, i < n - 1)
    for h in range(2):
        k = jnp.full(tile, cross[h] * (0.5 * STEP))
        splat[INSIDE + h] = k
        splat[SLOW + h] = jnp.where(slow_there, k, 0.0)
        splat[FAST + h] = jnp.where(fast_there, k, 0.0)
    table = jnp.zeros(tile, jnp.float32)
    for k in range(CLASSES):
        table = jnp.where(lane == k, stiff[k] * (0.5 * STEP), table)
    splat[TABLE] = table
    for s in range(sections):
        splat[MOVING + s] = jnp.full(tile, jnp.where(fixed[s] == 0, 1.0, 0.0))


def lead_kernel(u, shift, slow_top, slow_rest, fast):
    sections, _, rows, width = u.shape
    rest = slow_rest.shape[0] // 4
    top = rows - rest

    def body(after):
        for j in range(2):
            for c in range(2):
                k = 2 * j + c
                block = u[(near_of, second_of)[j](after, sections), c]
                slow_top[k * top : (k + 1) * top, :] = block[:top]
                slow_rest[k * rest : (k + 1) * rest, :] = block[top:]
                fast[k * rows : (k + 1) * rows, :] = u[(near_of, second_of)[j](not after, sections), c]

    by_side(body)
    put_tail(shift, slow_top, 4 * top, width)
    fast[4 * rows : fast.shape[0], :] = slow_top[4 * top : slow_top.shape[0], :]


def prepare_kernel(u, cls, arrived, stiff, cross, fixed, rim_a, rim_b, splat):
    sections, _, rows, _ = u.shape
    last = slice(rows - 1, rows)
    put_splat(stiff, cross, fixed, splat)
    table = splat[TABLE]
    put_rims(
        lambda s, c: u[s, c, 0:1, :],
        lambda s, c: u[s, c, last, :],
        lambda s: look_up(table, cls[s, 1, last, :]),
        rim_a,
        rim_b,
        sections,
    )


def wide_splat(splat, k, width):
    tile = splat[k]
    return per_tile(width, lambda cb: tile)


def chosen(values, index):
    for bit in range(3):
        on = (index & (1 << bit)) != 0
        values = [jnp.where(on, values[k + 1], values[k]) for k in range(0, len(values), 2)]
    return values[0]


def inside(u, w, total, half_across, half_below, shift, splat, scalars, sem, forces):
    sections, _, rows, width = u.shape
    rbs, cbs = rows // ROWS, width // COLS
    load = pltpu.make_async_copy(shift, scalars, sem)
    load.start()
    bottom = lax.broadcasted_iota(jnp.int32, (rows, COLS), 0) == rows - 1

    def below(cb, carry):
        at = pl.ds(pl.multiple_of(cb * COLS, COLS), COLS)
        for s in range(sections):
            x, y = u[s, 0, :, at], u[s, 1, :, at]
            half = jnp.where(bottom, 0.0, half_below(s, at))
            f = flow(pltpu.roll(x, rows - 1, 0) - x, pltpu.roll(y, rows - 1, 0) - y, half)
            new = [f[c] - pltpu.roll(f[c], 1, 0) for c in range(2)]
            if w is not None:
                new = [DAMPING * w[s, c, :, at] + new[c] for c in range(2)]
            for c in range(2):
                total[s, c, :, at] = new[c]
        return carry

    lax.fori_loop(0, cbs, below, 0)
    load.wait()
    last = lax.broadcasted_iota(jnp.int32, (ROWS, width), 1) == width - 1
    pairs = [(s, hops) for hops in (1, 2) for s in range(sections - hops)]

    def over_rows(body):
        lax.fori_loop(0, rbs, lambda rb, carry: body(rb, rows_of(rb)) or carry, 0, unroll=True)

    def put(k, s, at, f):
        for c in range(2):
            total[s, c, at, :] += f[c]
            forces[k, c, at, :] = f[c]

    def across(s, rb, at):
        x, y = u[s, 0, at, :], u[s, 1, at, :]
        half = jnp.where(last, 0.0, half_across(s, at))
        f = flow(pltpu.roll(x, width - 1, 1) - x, pltpu.roll(y, width - 1, 1) - y, half)
        put(len(pairs) + s, s, at, f)

    def across_back(s, rb, at):
        for c in range(2):
            total[s, c, at, :] -= pltpu.roll(forces[len(pairs) + s, c, at, :], 1, 1)

    def between(k, rb, at):
        s, hops = pairs[k]
        there = [(-scalars[s, hops - 1, rb, cb]) & (COLS - 1) for cb in range(cbs)]
        e = [turned(u[s + hops, c, at, :], there) - u[s, c, at, :] for c in range(2)]
        put(k, s, at, flow(e[0], e[1], wide_splat(splat, INSIDE + hops - 1, width)))

    def between_back(k, rb, at):
        s, hops = pairs[k]
        back = [scalars[s, hops - 1, rb, cb] & (COLS - 1) for cb in range(cbs)]
        for c in range(2):
            total[s + hops, c, at, :] -= turned(forces[k, c, at, :], back)

    for body, count in (
        (across, sections),
        (between, len(pairs)),
        (across_back, sections),
        (between_back, len(pairs)),
    ):
        for k in range(count):
            over_rows(functools.partial(body, k))


def first_inside_kernel(u, cls, shift, splat, total, half, scalars, sem, forces):
    table = splat[TABLE]
    values = [jnp.broadcast_to(table[:, k : k + 1], (ROWS, COLS)) for k in range(CLASSES)]
    rows = u.shape[2]

    def half_across(s, at):
        index = cls[s, 0, at, :]
        k = per_tile(index.shape[1], lambda cb: chosen(values, index[:, cols_of(cb)]))
        half[s, 0, at, :] = k
        return k

    def half_below(s, at):
        index = cls[s, 1, :, at]
        k = jnp.concatenate(
            [look_up(table, index[r : r + ROWS]) for r in range(0, rows, ROWS)], axis=0
        )
        half[s, 1, :, at] = k
        return k

    inside(u, None, total, half_across, half_below, shift, splat, scalars, sem, forces)


def later_inside_kernel(u, w, half, shift, splat, total, scalars, sem, forces):
    def half_across(s, at):
        return half[s, 0, at, :]

    def half_below(s, at):
        return half[s, 1, :, at]

    inside(u, w, total, half_across, half_below, shift, splat, scalars, sem, forces)


def side_flow(u, own, arrived, block, height, base, index, j, half, rb):
    at = rows_of(rb)
    number = index[j, rb : rb + 1, :]
    e = [
        gathered(arrived[pl.ds((2 * block + c) * height + rb * ROWS - base, ROWS), :], number)
        - u[own, c, at, :]
        for c in range(2)
    ]
    return flow(e[0], e[1], half)


def rim_flows(u, half, rim_a, rim_b, total, sections):
    rows = u.shape[2]
    strip = lax.axis_index("strip")
    odd = lax.rem(strip, 2) == 1
    has_below = strip < lax.axis_size("strip") - 1

    def below(r):
        return jnp.where(odd, rim_b[r : r + 1, :], rim_a[r : r + 1, :])

    def above(r):
        return jnp.where(odd, rim_a[r : r + 1, :], rim_b[r : r + 1, :])

    count = u.shape[0]
    last, top = slice(rows - 1, rows), slice(0, 1)
    for s in sections:
        stiff = jnp.where(has_below, half[s, 1, last, :], 0.0)
        f = flow(*[below(2 * s + c) - u[s, c, last, :] for c in range(2)], stiff)
        stiff = jnp.where(strip > 0, above(2 * count + s), 0.0)
        g = flow(*[u[s, c, top, :] - above(2 * s + c) for c in range(2)], stiff)
        for c in range(2):
            total[s, c, last, :] += f[c]
            total[s, c, top, :] -= g[c]


def fast_flows(u, after, fast, index, splat, total, which):
    sections, _, rows, width = u.shape
    for j in which:
        own, block, hops = pairs_of(after, sections)[j]
        stiff = wide_splat(splat, FAST + hops - 1, width)
        for rb in range(rows // ROWS):
            if isinstance(fast, tuple):
                f = side_flow(u, own, fast[block], 0, rows, 0, index, j, stiff, rb)
            else:
                f = side_flow(u, own, fast, block, rows, 0, index, j, stiff, rb)
            for c in range(2):
                total[own, c, rows_of(rb), :] += f[c]


def first_rims_kernel(u, w, total_in, half, fast, rim_a, rim_b, shift, splat, total, index):
    sections, _, rows, _ = u.shape

    def damp(rb, carry):
        at = rows_of(rb)
        new = [total[s, c, at, :] + DAMPING * w[s, c, at, :] for s in range(sections) for c in range(2)]
        for k, value in enumerate(new):
            total[k // 2, k % 2, at, :] = value
        return carry

    lax.fori_loop(0, rows // ROWS, damp, 0)

    def body(after):
        put_index(not after, shift, fast, 4 * rows, index)
        fast_flows(u, not after, fast, index, splat, total, range(3))

    by_side(body)
    rim_flows(u, half, rim_a, rim_b, total, range(sections))


def later_rims_kernel(
    u, total_in, half, fast_near, fast_far, rim_a, rim_b, index, splat,
    total, out_u, out_w, new_u, new_w, sem,
):
    sections, _, rows, width = u.shape
    fast = (fast_near, fast_far)

    def body(after):
        near = (near_of(after, sections), second_of(after, sections))
        done = [s for s in range(sections) if s not in near]
        fast_flows(u, not after, fast, index, splat, total, (0, 2))
        rim_flows(u, half, rim_a, rim_b, total, done)
        copies = []
        for k, s in enumerate(done):
            moving = wide_splat(splat, MOVING + s, width)
            for rb in range(rows // ROWS):
                at = rows_of(rb)
                for c in range(2):
                    v = total[s, c, at, :] * moving
                    new_w[k, c, at, :] = v
                    new_u[k, c, at, :] = u[s, c, at, :] + STEP * v
            copies += [
                pltpu.make_async_copy(new_u.at[k], out_u.at[s], sem.at[2 * k]),
                pltpu.make_async_copy(new_w.at[k], out_w.at[s], sem.at[2 * k + 1]),
            ]
        for copy in copies:
            copy.start()
        fast_flows(u, not after, fast, index, splat, total, (1,))
        rim_flows(u, half, rim_a, rim_b, total, near)
        for copy in copies:
            copy.wait()

    by_side(body)


def slow_values(u, after, arrived, height, base, index, splat, total, j, rb):
    sections, _, rows, width = u.shape
    own = pairs_of(after, sections)[j][0]
    value = [total[own, c, rows_of(rb), :] for c in range(2)]
    for p, (section, block, hops) in enumerate(pairs_of(after, sections)):
        if section == own:
            stiff = wide_splat(splat, SLOW + hops - 1, width)
            f = side_flow(u, own, arrived, block, height, base, index, p, stiff, rb)
            value = [value[c] + f[c] for c in range(2)]
    return value


def step_rows(u, after, arrived, height, base, index, splat, total, new_u, new_w, sections, sent):
    count, _, _, width = u.shape
    slow_edge = (near_of(after, count), second_of(after, count))
    for s in sections:
        moving = wide_splat(splat, MOVING + s, width)
        for row in range(base, base + height, ROWS):
            at, rb = pl.ds(row, ROWS), row // ROWS
            if s in slow_edge:
                j = slow_edge.index(s)
                value = slow_values(u, after, arrived, height, base, index, splat, total, j, rb)
            else:
                value = [total[s, c, at, :] for c in range(2)]
            for c in range(2):
                v = value[c] * moving
                moved = u[s, c, at, :] + STEP * v
                new_w[s, c, at, :] = v
                new_u[s, c, at, :] = moved
                if s in slow_edge:
                    sent[pl.ds((2 * j + c) * height + row - base, ROWS), :] = moved


def top_kernel(u, total, arrived, shift, splat, new_u, new_w, slow, index):
    sections = u.shape[0]
    height = slow.shape[0] // 4

    def body(after):
        put_index(after, shift, arrived, 4 * height, index)
        edge = (near_of(after, sections), second_of(after, sections))
        step_rows(u, after, arrived, height, 0, index, splat, total, new_u, new_w, edge, slow)

    by_side(body)


def rest_kernel(
    u, total, new_u_in, new_w_in, arrived, index, splat,
    new_u, new_w, slow, fast_near, fast_far,
):
    sections, _, rows, _ = u.shape
    height = slow.shape[0] // 4

    def body(after):
        edge = (near_of(after, sections), second_of(after, sections))
        others = [s for s in range(sections) if s not in edge]
        base = rows - height
        step_rows(u, after, arrived, height, base, index, splat, total, new_u, new_w, edge, slow)
        step_rows(u, after, None, rows, 0, index, splat, total, new_u, new_w, others, None)
        for j, s in enumerate((near_of(not after, sections), second_of(not after, sections))):
            for c in range(2):
                (fast_near, fast_far)[j][c * rows : (c + 1) * rows, :] = new_u[s, c]

    by_side(body)


def rims_kernel(u, half, arrived, rim_a, rim_b):
    sections, _, rows, _ = u.shape
    last = slice(rows - 1, rows)
    put_rims(
        lambda s, c: u[s, c, 0:1, :],
        lambda s, c: u[s, c, last, :],
        lambda s: half[s, 1, last, :],
        rim_a,
        rim_b,
        sections,
    )


def last_kernel(
    base, u, total, arrived, index, splat, out_u_in, out_w_in, out_u, out_w, new_u, new_w, sem
):
    sections, _, rows, width = u.shape
    height = arrived.shape[0] // 4
    rbs = height // ROWS
    part = rbs // 2 if rbs % 2 == 0 else rbs

    def body(after):
        copies = []
        for j in range(2):
            own = pairs_of(after, sections)[j][0]
            moving = wide_splat(splat, MOVING + own, width)
            for k in range(rbs):
                rb = base // ROWS + k
                value = slow_values(u, after, arrived, height, base, index, splat, total, j, rb)
                for c in range(2):
                    v = value[c] * moving
                    new_w[j, c, rows_of(k), :] = v
                    new_u[j, c, rows_of(k), :] = u[own, c, rows_of(rb), :] + STEP * v
                if (k + 1) % part == 0:
                    here = pl.ds((k + 1 - part) * ROWS, part * ROWS)
                    there = pl.ds(base + (k + 1 - part) * ROWS, part * ROWS)
                    for source, target in ((new_u, out_u), (new_w, out_w)):
                        copy = pltpu.make_async_copy(
                            source.at[j, :, here], target.at[own, :, there], sem.at[len(copies)]
                        )
                        copy.start()
                        copies.append(copy)
        for copy in copies:
            copy.wait()

    by_side(body)


def call(kernel, outs, ins, alias=None, scratch=(), in_specs=None, out_specs=None, limit=16 << 20, cost=None):
    return pl.pallas_call(
        kernel,
        out_shape=outs,
        in_specs=in_specs or [VMEM] * len(ins),
        out_specs=out_specs or [VMEM] * len(outs),
        input_output_aliases=alias or {},
        scratch_shapes=scratch,
        cost_estimate=cost,
        compiler_params=pltpu.CompilerParams(vmem_limit_bytes=limit),
    )(*ins)


def per_device(u, w, cls, shift, fixed, stiff, cross):
    sections, _, rows, width = u.shape

    def array(*shape, dtype=jnp.float32):
        return jax.ShapeDtypeStruct(shape, dtype)

    full = array(*u.shape)
    one = array(2 * rows, width)
    rim = array(-(-3 * sections // ROWS) * ROWS, width)
    splat = array(MOVING + sections, ROWS, COLS)
    index = array(3, tail_rows(rows), width, dtype=jnp.int32)
    scalars = [
        pltpu.SMEM(shift.shape, jnp.int32),
        pltpu.SemaphoreType.DMA,
        pltpu.VMEM((3 * sections - 3,) + u.shape[1:], jnp.float32),
    ]
    smem = pl.BlockSpec(memory_space=pltpu.SMEM)

    top = max(rows // ROWS * 3 // 4, 1) * ROWS
    tail = index.shape[1]
    slow_top, slow_rest, fast = call(
        lead_kernel,
        [array(4 * top + tail, width), array(4 * (rows - top), width), array(4 * rows + tail, width)],
        [u, shift],
    )
    slow_top = exchange(slow_top, "sec", "b")
    slow_rest = exchange(slow_rest, "sec", "b")
    fast = exchange(fast, "sec", "a")
    rim_a, rim_b, splat = call(
        prepare_kernel,
        [rim, rim, splat],
        [u, cls, fast, stiff, cross, fixed],
        in_specs=[VMEM] * 2 + [ANY] + [smem] * 3,
    )
    rim_a = exchange(rim_a, "strip", "a")
    rim_b = exchange(rim_b, "strip", "b")
    total, half = call(
        first_inside_kernel, [full, full], [u, cls, shift, splat], scratch=scalars
    )
    total, fast_index = call(
        first_rims_kernel,
        [full, index],
        [u, w, total, half, fast, rim_a, rim_b, shift, splat],
        {2: 0},
    )
    new_u, new_w, slow_top, index = call(
        top_kernel,
        [full, full, array(4 * top, width), index],
        [u, total, slow_top, shift, splat],
    )
    slow_top = exchange(slow_top, "sec", "b")
    u, w, slow_rest, fast_near, fast_far = call(
        rest_kernel,
        [full, full, array(4 * (rows - top), width), one, one],
        [u, total, new_u, new_w, slow_rest, index, splat],
        {2: 0, 3: 1},
    )
    slow_rest = exchange(slow_rest, "sec", "b")
    fast_near = exchange(fast_near, "sec", "a")
    fast_far = exchange(fast_far, "sec", "a")
    rim_a, rim_b = call(
        rims_kernel, [rim, rim], [u, half, fast_near], in_specs=[VMEM] * 2 + [ANY]
    )
    rim_a = exchange(rim_a, "strip", "a")
    rim_b = exchange(rim_b, "strip", "b")
    (total,) = call(later_inside_kernel, [full], [u, w, half, shift, splat], scratch=scalars)
    done = max(sections - 2, 1)
    total, out_u, out_w = call(
        later_rims_kernel,
        [full, full, full],
        [u, total, half, fast_near, fast_far, rim_a, rim_b, fast_index, splat],
        {1: 0},
        in_specs=[VMEM] * 9,
        scratch=[pltpu.VMEM((done, 2, rows, width), jnp.float32)] * 2
        + [pltpu.SemaphoreType.DMA((2 * done,))],
        out_specs=[VMEM, ANY, ANY],
    )
    for base, arrived in ((0, slow_top), (top, slow_rest)):
        height = arrived.shape[0] // 4
        out_u, out_w = call(
            functools.partial(last_kernel, base),
            [full, full],
            [u, total, arrived, index, splat, out_u, out_w],
            {5: 0, 6: 1},
            scratch=[pltpu.VMEM((2, 2, height, width), jnp.float32)] * 2
            + [pltpu.SemaphoreType.DMA((8,))],
            in_specs=[VMEM] * 5 + [ANY] * 2,
            out_specs=[ANY] * 2,
        )
    return out_u, out_w


def solution(mesh):
    block = P("sec", None, "strip", None)
    return jax.shard_map(
        per_device,
        mesh=mesh,
        in_specs=(block, block, block, block, P("sec"), P(), P()),
        out_specs=(block, block),
        check_vma=False,
    )
```

```python
import functools

import jax
import jax.numpy as jnp
from jax import lax
from jax.experimental import pallas as pl
from jax.experimental.pallas import tpu as pltpu
from jax.sharding import PartitionSpec as P

ROWS = 8
COLS = 128
CLASSES = 8
DAMPING = 0.9
STEP = 0.35

VMEM = pl.BlockSpec(memory_space=pltpu.VMEM)
ANY = pl.BlockSpec(memory_space=pl.ANY)

INSIDE, SLOW, FAST, TABLE, MOVING = 0, 2, 4, 6, 7


def exchange(value, axis, pairing):
    n = lax.axis_size(axis)
    first = 0 if pairing == "a" else 1
    route = []
    for i in range(first, n - 1, 2):
        route += [(i, i + 1), (i + 1, i)]
    return lax.ppermute(value, axis, route)


def slow_after():
    return lax.rem(lax.axis_index("sec"), 2) == 1


def by_side(body):
    after = slow_after()

    @pl.when(after)
    def _():
        body(True)

    @pl.when(jnp.logical_not(after))
    def _():
        body(False)


def near_of(after, sections):
    return sections - 1 if after else 0


def second_of(after, sections):
    return sections - 2 if after else 1


def pairs_of(after, sections):
    near, second = near_of(after, sections), second_of(after, sections)
    return ((near, 0, 1), (second, 0, 2), (near, 1, 2))


def inverse(value):
    guess = pl.reciprocal(value, approx=True)
    return guess * (2.0 - value * guess)


def flow(ex, ey, half):
    gain = half * (3.0 - inverse(1.0 + ex * ex + ey * ey))
    return gain * ex, gain * ey


def cols_of(cb):
    return slice(cb * COLS, (cb + 1) * COLS)


def rows_of(rb):
    start = rb * ROWS
    return pl.ds(start if isinstance(start, int) else pl.multiple_of(start, ROWS), ROWS)


def tail_rows(rows):
    return -(-(rows // ROWS) // ROWS) * ROWS


def per_tile(width, make):
    return jnp.concatenate([make(cb) for cb in range(width // COLS)], axis=1)


def turned(wide, amounts):
    return per_tile(wide.shape[1], lambda cb: pltpu.roll(wide[:, cols_of(cb)], amounts[cb], 1))


def gathered(wide, index):
    def one(cb):
        full = jnp.broadcast_to(index[:, cols_of(cb)], (ROWS, COLS))
        return jnp.take_along_axis(wide[:, cols_of(cb)], full, axis=1, mode="promise_in_bounds")

    return per_tile(wide.shape[1], one)


def spread(blocks, width):
    return per_tile(width, lambda cb: jnp.broadcast_to(blocks[:, cb : cb + 1], (blocks.shape[0], COLS)))


def lanes(rows, width):
    return lax.broadcasted_iota(jnp.int32, (rows, width), 1) & (COLS - 1)


def put_index(after, shift, before, index):
    sections, _, rbs, _ = shift.shape
    width = index.shape[2]
    lane = lanes(rbs, width)
    for j, (own, block, hops) in enumerate(pairs_of(after, sections)):
        if after:
            offset = spread(shift[own, hops - 1], width)
        else:
            offset = -spread(before[sections - 1 - block, hops - 1], width)
        index[j, 0:rbs, :] = (lane + offset) & (COLS - 1)


def put_rims(first_of, last_of, kv_of, rim_a, rim_b, sections):
    odd = lax.rem(lax.axis_index("strip"), 2) == 1

    def put(line, first, last):
        rim_a[line : line + 1, :] = jnp.where(odd, first, last)
        rim_b[line : line + 1, :] = jnp.where(odd, last, first)

    for s in range(sections):
        for c in range(2):
            put(2 * s + c, first_of(s, c), last_of(s, c))
        stiff = kv_of(s)
        put(2 * sections + s, stiff, stiff)


def look_up(table, index):
    def one(cb):
        tile = jnp.broadcast_to(index[:, cols_of(cb)], (ROWS, COLS))
        return jnp.take_along_axis(table, tile, axis=1, mode="promise_in_bounds")[: index.shape[0]]

    return per_tile(index.shape[1], one)


def put_splat(stiff, cross, fixed, splat):
    sections = fixed.shape[0]
    i, n = lax.axis_index("sec"), lax.axis_size("sec")
    odd = slow_after()
    tile = (ROWS, COLS)
    lane = lax.broadcasted_iota(jnp.int32, tile, 1)
    slow_there = jnp.where(odd, i < n - 1, i > 0)
    fast_there = jnp.where(odd, i > 0, i < n - 1)
    for h in range(2):
        k = jnp.full(tile, cross[h] * (0.5 * STEP))
        splat[INSIDE + h] = k
        splat[SLOW + h] = jnp.where(slow_there, k, 0.0)
        splat[FAST + h] = jnp.where(fast_there, k, 0.0)
    table = jnp.zeros(tile, jnp.float32)
    for k in range(CLASSES):
        table = jnp.where(lane == k, stiff[k] * (0.5 * STEP), table)
    splat[TABLE] = table
    for s in range(sections):
        splat[MOVING + s] = jnp.full(tile, jnp.where(fixed[s] == 0, 1.0, 0.0))


def lead_kernel(u, slow, fast):
    sections, _, rows, _ = u.shape

    def body(after):
        for out, side in ((slow, after), (fast, not after)):
            for k, own in enumerate((near_of(side, sections), second_of(side, sections))):
                for c in range(2):
                    out[(2 * k + c) * rows : (2 * k + c + 1) * rows, :] = u[own, c]

    by_side(body)


def prepare_kernel(u, cls, shift, arrived, stiff, cross, fixed, rim_a, rim_b, splat, offsets):
    sections, _, rows, _ = u.shape
    last = slice(rows - 1, rows)
    offsets[...] = shift[...]
    put_splat(stiff, cross, fixed, splat)
    table = splat[TABLE]
    put_rims(
        lambda s, c: u[s, c, 0:1, :],
        lambda s, c: u[s, c, last, :],
        lambda s: look_up(table, cls[s, 1, last, :]),
        rim_a,
        rim_b,
        sections,
    )


def wide_splat(splat, k, width):
    tile = splat[k]
    return per_tile(width, lambda cb: tile)


def chosen(values, index):
    for bit in range(3):
        on = (index & (1 << bit)) != 0
        values = [jnp.where(on, values[k + 1], values[k]) for k in range(0, len(values), 2)]
    return values[0]


def inside(u, w, total, half_across, half_below, shift, splat, scalars, sem, forces):
    sections, _, rows, width = u.shape
    rbs, cbs = rows // ROWS, width // COLS
    load = pltpu.make_async_copy(shift, scalars, sem)
    load.start()
    bottom = lax.broadcasted_iota(jnp.int32, (rows, COLS), 0) == rows - 1

    def below(cb, carry):
        at = pl.ds(pl.multiple_of(cb * COLS, COLS), COLS)
        for s in range(sections):
            x, y = u[s, 0, :, at], u[s, 1, :, at]
            half = jnp.where(bottom, 0.0, half_below(s, at))
            f = flow(pltpu.roll(x, rows - 1, 0) - x, pltpu.roll(y, rows - 1, 0) - y, half)
            new = [f[c] - pltpu.roll(f[c], 1, 0) for c in range(2)]
            if w is not None:
                new = [DAMPING * w[s, c, :, at] + new[c] for c in range(2)]
            for c in range(2):
                total[s, c, :, at] = new[c]
        return carry

    lax.fori_loop(0, cbs, below, 0)
    load.wait()
    last = lax.broadcasted_iota(jnp.int32, (ROWS, width), 1) == width - 1
    pairs = [(s, hops) for hops in (1, 2) for s in range(sections - hops)]

    def over_rows(body):
        lax.fori_loop(0, rbs, lambda rb, carry: body(rb, rows_of(rb)) or carry, 0, unroll=True)

    def put(k, s, at, f):
        for c in range(2):
            total[s, c, at, :] += f[c]
            forces[k, c, at, :] = f[c]

    def across(s, rb, at):
        x, y = u[s, 0, at, :], u[s, 1, at, :]
        half = jnp.where(last, 0.0, half_across(s, at))
        f = flow(pltpu.roll(x, width - 1, 1) - x, pltpu.roll(y, width - 1, 1) - y, half)
        put(len(pairs) + s, s, at, f)

    def across_back(s, rb, at):
        for c in range(2):
            total[s, c, at, :] -= pltpu.roll(forces[len(pairs) + s, c, at, :], 1, 1)

    def between(k, rb, at):
        s, hops = pairs[k]
        there = [(-scalars[s, hops - 1, rb, cb]) & (COLS - 1) for cb in range(cbs)]
        e = [turned(u[s + hops, c, at, :], there) - u[s, c, at, :] for c in range(2)]
        put(k, s, at, flow(e[0], e[1], wide_splat(splat, INSIDE + hops - 1, width)))

    def between_back(k, rb, at):
        s, hops = pairs[k]
        back = [scalars[s, hops - 1, rb, cb] & (COLS - 1) for cb in range(cbs)]
        for c in range(2):
            total[s + hops, c, at, :] -= turned(forces[k, c, at, :], back)

    for body, count in (
        (across, sections),
        (between, len(pairs)),
        (across_back, sections),
        (between_back, len(pairs)),
    ):
        for k in range(count):
            over_rows(functools.partial(body, k))


def first_inside_kernel(u, cls, shift, splat, total, half, scalars, sem, forces):
    table = splat[TABLE]
    values = [jnp.broadcast_to(table[:, k : k + 1], (ROWS, COLS)) for k in range(CLASSES)]
    rows = u.shape[2]

    def half_across(s, at):
        index = cls[s, 0, at, :]
        k = per_tile(index.shape[1], lambda cb: chosen(values, index[:, cols_of(cb)]))
        half[s, 0, at, :] = k
        return k

    def half_below(s, at):
        index = cls[s, 1, :, at]
        k = jnp.concatenate(
            [look_up(table, index[r : r + ROWS]) for r in range(0, rows, ROWS)], axis=0
        )
        half[s, 1, :, at] = k
        return k

    inside(u, None, total, half_across, half_below, shift, splat, scalars, sem, forces)


def later_inside_kernel(u, w, half, shift, splat, total, scalars, sem, forces):
    def half_across(s, at):
        return half[s, 0, at, :]

    def half_below(s, at):
        return half[s, 1, :, at]

    inside(u, w, total, half_across, half_below, shift, splat, scalars, sem, forces)


def side_flow(u, own, arrived, block, height, base, index, j, half, rb):
    at = rows_of(rb)
    number = index[j, rb : rb + 1, :]
    e = [
        gathered(arrived[pl.ds((2 * block + c) * height + rb * ROWS - base, ROWS), :], number)
        - u[own, c, at, :]
        for c in range(2)
    ]
    return flow(e[0], e[1], half)


def rim_flows(u, half, rim_a, rim_b, total, sections):
    rows = u.shape[2]
    strip = lax.axis_index("strip")
    odd = lax.rem(strip, 2) == 1
    has_below = strip < lax.axis_size("strip") - 1

    def below(r):
        return jnp.where(odd, rim_b[r : r + 1, :], rim_a[r : r + 1, :])

    def above(r):
        return jnp.where(odd, rim_a[r : r + 1, :], rim_b[r : r + 1, :])

    count = u.shape[0]
    last, top = slice(rows - 1, rows), slice(0, 1)
    for s in sections:
        stiff = jnp.where(has_below, half[s, 1, last, :], 0.0)
        f = flow(*[below(2 * s + c) - u[s, c, last, :] for c in range(2)], stiff)
        stiff = jnp.where(strip > 0, above(2 * count + s), 0.0)
        g = flow(*[u[s, c, top, :] - above(2 * s + c) for c in range(2)], stiff)
        for c in range(2):
            total[s, c, last, :] += f[c]
            total[s, c, top, :] -= g[c]


def fast_flows(u, after, fast, index, splat, total, which):
    sections, _, rows, width = u.shape
    for j in which:
        own, block, hops = pairs_of(after, sections)[j]
        stiff = wide_splat(splat, FAST + hops - 1, width)
        for rb in range(rows // ROWS):
            f = side_flow(u, own, fast, block, rows, 0, index, j, stiff, rb)
            for c in range(2):
                total[own, c, rows_of(rb), :] += f[c]


def first_rims_kernel(
    u, w, total_in, half, fast, rim_a, rim_b, shift, before, splat, total, index
):
    sections, _, rows, _ = u.shape

    def damp(rb, carry):
        at = rows_of(rb)
        new = [total[s, c, at, :] + DAMPING * w[s, c, at, :] for s in range(sections) for c in range(2)]
        for k, value in enumerate(new):
            total[k // 2, k % 2, at, :] = value
        return carry

    lax.fori_loop(0, rows // ROWS, damp, 0)

    def body(after):
        put_index(not after, shift, before, index)
        fast_flows(u, not after, fast, index, splat, total, range(3))

    by_side(body)
    rim_flows(u, half, rim_a, rim_b, total, range(sections))


def later_rims_kernel(
    u, total_in, half, fast, rim_a, rim_b, index, splat,
    total, out_u, out_w, new_u, new_w, sem,
):
    sections, _, rows, width = u.shape

    def body(after):
        near = (near_of(after, sections), second_of(after, sections))
        done = [s for s in range(sections) if s not in near]
        fast_flows(u, not after, fast, index, splat, total, (0, 2))
        rim_flows(u, half, rim_a, rim_b, total, done)
        copies = []
        for k, s in enumerate(done):
            moving = wide_splat(splat, MOVING + s, width)
            for rb in range(rows // ROWS):
                at = rows_of(rb)
                for c in range(2):
                    v = total[s, c, at, :] * moving
                    new_w[k, c, at, :] = v
                    new_u[k, c, at, :] = u[s, c, at, :] + STEP * v
            copies += [
                pltpu.make_async_copy(new_u.at[k], out_u.at[s], sem.at[2 * k]),
                pltpu.make_async_copy(new_w.at[k], out_w.at[s], sem.at[2 * k + 1]),
            ]
        for copy in copies:
            copy.start()
        fast_flows(u, not after, fast, index, splat, total, (1,))
        rim_flows(u, half, rim_a, rim_b, total, near)
        for copy in copies:
            copy.wait()

    by_side(body)


def slow_values(u, after, arrived, height, base, index, splat, total, j, rb):
    sections, _, rows, width = u.shape
    own = pairs_of(after, sections)[j][0]
    value = [total[own, c, rows_of(rb), :] for c in range(2)]
    for p, (section, block, hops) in enumerate(pairs_of(after, sections)):
        if section == own:
            stiff = wide_splat(splat, SLOW + hops - 1, width)
            f = side_flow(u, own, arrived, block, height, base, index, p, stiff, rb)
            value = [value[c] + f[c] for c in range(2)]
    return value


def step_kernel(
    u, total, arrived, half, shift, before, splat,
    new_u, new_w, slow, fast, index, rim_a, rim_b,
):
    sections, _, rows, width = u.shape

    def body(after):
        put_index(after, shift, before, index)
        slow_edge = (near_of(after, sections), second_of(after, sections))
        fast_edge = (near_of(not after, sections), second_of(not after, sections))
        for s in range(sections):
            moving = wide_splat(splat, MOVING + s, width)
            for rb in range(rows // ROWS):
                at, row = rows_of(rb), rb * ROWS
                if s in slow_edge:
                    value = slow_values(
                        u, after, arrived, rows, 0, index, splat, total, slow_edge.index(s), rb
                    )
                else:
                    value = [total[s, c, at, :] for c in range(2)]
                for c in range(2):
                    v = value[c] * moving
                    moved = u[s, c, at, :] + STEP * v
                    new_w[s, c, at, :] = v
                    new_u[s, c, at, :] = moved
                    for edge, out in ((slow_edge, slow), (fast_edge, fast)):
                        if s in edge:
                            out[pl.ds((2 * edge.index(s) + c) * rows + row, ROWS), :] = moved

    by_side(body)
    last = slice(rows - 1, rows)
    put_rims(
        lambda s, c: new_u[s, c, 0:1, :],
        lambda s, c: new_u[s, c, last, :],
        lambda s: half[s, 1, last, :],
        rim_a,
        rim_b,
        sections,
    )


def last_kernel(
    base, u, total, arrived, index, splat, out_u_in, out_w_in, out_u, out_w, new_u, new_w, sem
):
    sections, _, rows, width = u.shape
    height = arrived.shape[0] // 4
    rbs = height // ROWS
    part = rbs // 2 if rbs % 2 == 0 else rbs

    def body(after):
        copies = []
        for j in range(2):
            own = pairs_of(after, sections)[j][0]
            moving = wide_splat(splat, MOVING + own, width)
            for k in range(rbs):
                rb = base // ROWS + k
                value = slow_values(u, after, arrived, height, base, index, splat, total, j, rb)
                for c in range(2):
                    v = value[c] * moving
                    new_w[j, c, rows_of(k), :] = v
                    new_u[j, c, rows_of(k), :] = u[own, c, rows_of(rb), :] + STEP * v
                if (k + 1) % part == 0:
                    here = pl.ds((k + 1 - part) * ROWS, part * ROWS)
                    there = pl.ds(base + (k + 1 - part) * ROWS, part * ROWS)
                    for source, target in ((new_u, out_u), (new_w, out_w)):
                        copy = pltpu.make_async_copy(
                            source.at[j, :, here], target.at[own, :, there], sem.at[len(copies)]
                        )
                        copy.start()
                        copies.append(copy)
        for copy in copies:
            copy.wait()

    by_side(body)


def call(kernel, outs, ins, alias=None, scratch=(), in_specs=None, out_specs=None, limit=16 << 20, cost=None):
    return pl.pallas_call(
        kernel,
        out_shape=outs,
        in_specs=in_specs or [VMEM] * len(ins),
        out_specs=out_specs or [VMEM] * len(outs),
        input_output_aliases=alias or {},
        scratch_shapes=scratch,
        cost_estimate=cost,
        compiler_params=pltpu.CompilerParams(vmem_limit_bytes=limit),
    )(*ins)


def per_device(u, w, cls, shift, fixed, stiff, cross):
    sections, _, rows, width = u.shape

    def array(*shape, dtype=jnp.float32):
        return jax.ShapeDtypeStruct(shape, dtype)

    full = array(*u.shape)
    two = array(4 * rows, width)
    rim = array(-(-3 * sections // ROWS) * ROWS, width)
    splat = array(MOVING + sections, ROWS, COLS)
    index = array(3, tail_rows(rows), width, dtype=jnp.int32)
    scalars = [
        pltpu.SMEM(shift.shape, jnp.int32),
        pltpu.SemaphoreType.DMA,
        pltpu.VMEM((3 * sections - 3,) + u.shape[1:], jnp.float32),
    ]
    smem = pl.BlockSpec(memory_space=pltpu.SMEM)

    slow, fast = call(lead_kernel, [two, two], [u])
    slow = exchange(slow, "sec", "b")
    fast = exchange(fast, "sec", "a")
    rim_a, rim_b, splat, offsets = call(
        prepare_kernel,
        [rim, rim, splat, array(*shift.shape, dtype=jnp.int32)],
        [u, cls, shift, fast, stiff, cross, fixed],
        in_specs=[VMEM] * 3 + [ANY] + [smem] * 3,
    )
    before_fast = exchange(offsets, "sec", "a")
    before_slow = exchange(offsets, "sec", "b")
    rim_a = exchange(rim_a, "strip", "a")
    rim_b = exchange(rim_b, "strip", "b")
    total, half = call(
        first_inside_kernel, [full, full], [u, cls, shift, splat], scratch=scalars
    )
    total, fast_index = call(
        first_rims_kernel,
        [full, index],
        [u, w, total, half, fast, rim_a, rim_b, shift, before_fast, splat],
        {2: 0},
    )
    u, w, slow, fast, index, rim_a, rim_b = call(
        step_kernel,
        [full, full, two, two, index, rim, rim],
        [u, total, slow, half, shift, before_slow, splat],
    )
    slow = exchange(slow, "sec", "b")
    fast = exchange(fast, "sec", "a")
    rim_a = exchange(rim_a, "strip", "a")
    rim_b = exchange(rim_b, "strip", "b")
    (total,) = call(later_inside_kernel, [full], [u, w, half, shift, splat], scratch=scalars)
    done = max(sections - 2, 1)
    total, out_u, out_w = call(
        later_rims_kernel,
        [full, full, full],
        [u, total, half, fast, rim_a, rim_b, fast_index, splat],
        {1: 0},
        in_specs=[VMEM] * 8,
        scratch=[pltpu.VMEM((done, 2, rows, width), jnp.float32)] * 2
        + [pltpu.SemaphoreType.DMA((2 * done,))],
        out_specs=[VMEM, ANY, ANY],
    )
    return tuple(
        call(
            functools.partial(last_kernel, 0),
            [full, full],
            [u, total, slow, index, splat, out_u, out_w],
            {5: 0, 6: 1},
            scratch=[pltpu.VMEM((2, 2, rows, width), jnp.float32)] * 2
            + [pltpu.SemaphoreType.DMA((8,))],
            in_specs=[VMEM] * 5 + [ANY] * 2,
            out_specs=[ANY] * 2,
        )
    )


def solution(mesh):
    block = P("sec", None, "strip", None)
    return jax.shard_map(
        per_device,
        mesh=mesh,
        in_specs=(block, block, block, block, P("sec"), P(), P()),
        out_specs=(block, block),
        check_vma=False,
    )
```

```python
import functools

import jax
import jax.numpy as jnp
from jax import lax
from jax.experimental import pallas as pl
from jax.experimental.pallas import tpu as pltpu
from jax.sharding import PartitionSpec as P

ROWS = 8
COLS = 128
CLASSES = 8
DAMPING = 0.9
STEP = 0.35

VMEM = pl.BlockSpec(memory_space=pltpu.VMEM)
ANY = pl.BlockSpec(memory_space=pl.ANY)

INSIDE, SLOW, FAST, TABLE, MOVING = 0, 2, 4, 6, 7


def exchange(value, axis, pairing):
    n = lax.axis_size(axis)
    first = 0 if pairing == "a" else 1
    route = []
    for i in range(first, n - 1, 2):
        route += [(i, i + 1), (i + 1, i)]
    return lax.ppermute(value, axis, route)


def slow_after():
    return lax.rem(lax.axis_index("sec"), 2) == 1


def by_side(body):
    after = slow_after()

    @pl.when(after)
    def _():
        body(True)

    @pl.when(jnp.logical_not(after))
    def _():
        body(False)


def near_of(after, sections):
    return sections - 1 if after else 0


def second_of(after, sections):
    return sections - 2 if after else 1


def pairs_of(after, sections):
    near, second = near_of(after, sections), second_of(after, sections)
    return ((near, 0, 1), (second, 0, 2), (near, 1, 2))


def inverse(value):
    guess = pl.reciprocal(value, approx=True)
    return guess * (2.0 - value * guess)


def flow(ex, ey, half):
    gain = half * (3.0 - inverse(1.0 + ex * ex + ey * ey))
    return gain * ex, gain * ey


def cols_of(cb):
    return slice(cb * COLS, (cb + 1) * COLS)


def rows_of(rb):
    start = rb * ROWS
    return pl.ds(start if isinstance(start, int) else pl.multiple_of(start, ROWS), ROWS)


def tail_rows(rows):
    return -(-(rows // ROWS) // ROWS) * ROWS


def per_tile(width, make):
    return jnp.concatenate([make(cb) for cb in range(width // COLS)], axis=1)


def turned(wide, amounts):
    return per_tile(wide.shape[1], lambda cb: pltpu.roll(wide[:, cols_of(cb)], amounts[cb], 1))


def gathered(wide, index):
    def one(cb):
        full = jnp.broadcast_to(index[:, cols_of(cb)], (ROWS, COLS))
        return jnp.take_along_axis(wide[:, cols_of(cb)], full, axis=1, mode="promise_in_bounds")

    return per_tile(wide.shape[1], one)


def spread(blocks, width):
    return per_tile(width, lambda cb: jnp.broadcast_to(blocks[:, cb : cb + 1], (blocks.shape[0], COLS)))


def lanes(rows, width):
    return lax.broadcasted_iota(jnp.int32, (rows, width), 1) & (COLS - 1)


def put_index(after, shift, before, index):
    sections, _, rbs, _ = shift.shape
    width = index.shape[2]
    lane = lanes(rbs, width)
    for j, (own, block, hops) in enumerate(pairs_of(after, sections)):
        if after:
            offset = spread(shift[own, hops - 1], width)
        else:
            offset = -spread(before[sections - 1 - block, hops - 1], width)
        index[j, 0:rbs, :] = (lane + offset) & (COLS - 1)


def put_rims(first_of, last_of, kv_of, rim_a, rim_b, sections):
    odd = lax.rem(lax.axis_index("strip"), 2) == 1

    def put(line, first, last):
        rim_a[line : line + 1, :] = jnp.where(odd, first, last)
        rim_b[line : line + 1, :] = jnp.where(odd, last, first)

    for s in range(sections):
        for c in range(2):
            put(2 * s + c, first_of(s, c), last_of(s, c))
        stiff = kv_of(s)
        put(2 * sections + s, stiff, stiff)


def look_up(table, index):
    def one(cb):
        tile = jnp.broadcast_to(index[:, cols_of(cb)], (ROWS, COLS))
        return jnp.take_along_axis(table, tile, axis=1, mode="promise_in_bounds")[: index.shape[0]]

    return per_tile(index.shape[1], one)


def put_splat(stiff, cross, fixed, splat):
    sections = fixed.shape[0]
    i, n = lax.axis_index("sec"), lax.axis_size("sec")
    odd = slow_after()
    tile = (ROWS, COLS)
    lane = lax.broadcasted_iota(jnp.int32, tile, 1)
    slow_there = jnp.where(odd, i < n - 1, i > 0)
    fast_there = jnp.where(odd, i > 0, i < n - 1)
    for h in range(2):
        k = jnp.full(tile, cross[h] * (0.5 * STEP))
        splat[INSIDE + h] = k
        splat[SLOW + h] = jnp.where(slow_there, k, 0.0)
        splat[FAST + h] = jnp.where(fast_there, k, 0.0)
    table = jnp.zeros(tile, jnp.float32)
    for k in range(CLASSES):
        table = jnp.where(lane == k, stiff[k] * (0.5 * STEP), table)
    splat[TABLE] = table
    for s in range(sections):
        splat[MOVING + s] = jnp.full(tile, jnp.where(fixed[s] == 0, 1.0, 0.0))


def lead_kernel(u, slow, fast):
    sections, _, rows, _ = u.shape

    def body(after):
        for out, side in ((slow, after), (fast, not after)):
            for k, own in enumerate((near_of(side, sections), second_of(side, sections))):
                for c in range(2):
                    out[(2 * k + c) * rows : (2 * k + c + 1) * rows, :] = u[own, c]

    by_side(body)


def prepare_kernel(u, cls, arrived, stiff, cross, fixed, rim_a, rim_b, splat):
    sections, _, rows, _ = u.shape
    last = slice(rows - 1, rows)
    put_splat(stiff, cross, fixed, splat)
    table = splat[TABLE]
    put_rims(
        lambda s, c: u[s, c, 0:1, :],
        lambda s, c: u[s, c, last, :],
        lambda s: look_up(table, cls[s, 1, last, :]),
        rim_a,
        rim_b,
        sections,
    )


def wide_splat(splat, k, width):
    tile = splat[k]
    return per_tile(width, lambda cb: tile)


def chosen(values, index):
    for bit in range(3):
        on = (index & (1 << bit)) != 0
        values = [jnp.where(on, values[k + 1], values[k]) for k in range(0, len(values), 2)]
    return values[0]


def inside(u, w, total, half_across, half_below, shift, splat, scalars, sem, forces):
    sections, _, rows, width = u.shape
    rbs, cbs = rows // ROWS, width // COLS
    load = pltpu.make_async_copy(shift, scalars, sem)
    load.start()
    bottom = lax.broadcasted_iota(jnp.int32, (rows, COLS), 0) == rows - 1

    def below(cb, carry):
        at = pl.ds(pl.multiple_of(cb * COLS, COLS), COLS)
        for s in range(sections):
            x, y = u[s, 0, :, at], u[s, 1, :, at]
            half = jnp.where(bottom, 0.0, half_below(s, at))
            f = flow(pltpu.roll(x, rows - 1, 0) - x, pltpu.roll(y, rows - 1, 0) - y, half)
            new = [f[c] - pltpu.roll(f[c], 1, 0) for c in range(2)]
            if w is not None:
                new = [DAMPING * w[s, c, :, at] + new[c] for c in range(2)]
            for c in range(2):
                total[s, c, :, at] = new[c]
        return carry

    lax.fori_loop(0, cbs, below, 0)
    load.wait()
    last = lax.broadcasted_iota(jnp.int32, (ROWS, width), 1) == width - 1
    pairs = [(s, hops) for hops in (1, 2) for s in range(sections - hops)]

    def over_rows(body):
        lax.fori_loop(0, rbs, lambda rb, carry: body(rb, rows_of(rb)) or carry, 0, unroll=True)

    def put(k, s, at, f):
        for c in range(2):
            total[s, c, at, :] += f[c]
            forces[k, c, at, :] = f[c]

    def across(s, rb, at):
        x, y = u[s, 0, at, :], u[s, 1, at, :]
        half = jnp.where(last, 0.0, half_across(s, at))
        f = flow(pltpu.roll(x, width - 1, 1) - x, pltpu.roll(y, width - 1, 1) - y, half)
        put(len(pairs) + s, s, at, f)

    def across_back(s, rb, at):
        for c in range(2):
            total[s, c, at, :] -= pltpu.roll(forces[len(pairs) + s, c, at, :], 1, 1)

    def between(k, rb, at):
        s, hops = pairs[k]
        there = [(-scalars[s, hops - 1, rb, cb]) & (COLS - 1) for cb in range(cbs)]
        e = [turned(u[s + hops, c, at, :], there) - u[s, c, at, :] for c in range(2)]
        put(k, s, at, flow(e[0], e[1], wide_splat(splat, INSIDE + hops - 1, width)))

    def between_back(k, rb, at):
        s, hops = pairs[k]
        back = [scalars[s, hops - 1, rb, cb] & (COLS - 1) for cb in range(cbs)]
        for c in range(2):
            total[s + hops, c, at, :] -= turned(forces[k, c, at, :], back)

    for body, count in (
        (across, sections),
        (between, len(pairs)),
        (across_back, sections),
        (between_back, len(pairs)),
    ):
        for k in range(count):
            over_rows(functools.partial(body, k))


def first_inside_kernel(u, cls, shift, splat, total, half, scalars, sem, forces):
    table = splat[TABLE]
    values = [jnp.broadcast_to(table[:, k : k + 1], (ROWS, COLS)) for k in range(CLASSES)]
    rows = u.shape[2]

    def half_across(s, at):
        index = cls[s, 0, at, :]
        k = per_tile(index.shape[1], lambda cb: chosen(values, index[:, cols_of(cb)]))
        half[s, 0, at, :] = k
        return k

    def half_below(s, at):
        index = cls[s, 1, :, at]
        k = jnp.concatenate(
            [look_up(table, index[r : r + ROWS]) for r in range(0, rows, ROWS)], axis=0
        )
        half[s, 1, :, at] = k
        return k

    inside(u, None, total, half_across, half_below, shift, splat, scalars, sem, forces)


def later_inside_kernel(u, w, half, shift, splat, total, scalars, sem, forces):
    def half_across(s, at):
        return half[s, 0, at, :]

    def half_below(s, at):
        return half[s, 1, :, at]

    inside(u, w, total, half_across, half_below, shift, splat, scalars, sem, forces)


def side_flow(u, own, arrived, block, height, base, index, j, half, rb):
    at = rows_of(rb)
    number = index[j, rb : rb + 1, :]
    e = [
        gathered(arrived[pl.ds((2 * block + c) * height + rb * ROWS - base, ROWS), :], number)
        - u[own, c, at, :]
        for c in range(2)
    ]
    return flow(e[0], e[1], half)


def rim_flows(u, half, rim_a, rim_b, total, sections):
    rows = u.shape[2]
    strip = lax.axis_index("strip")
    odd = lax.rem(strip, 2) == 1
    has_below = strip < lax.axis_size("strip") - 1

    def below(r):
        return jnp.where(odd, rim_b[r : r + 1, :], rim_a[r : r + 1, :])

    def above(r):
        return jnp.where(odd, rim_a[r : r + 1, :], rim_b[r : r + 1, :])

    count = u.shape[0]
    last, top = slice(rows - 1, rows), slice(0, 1)
    for s in sections:
        stiff = jnp.where(has_below, half[s, 1, last, :], 0.0)
        f = flow(*[below(2 * s + c) - u[s, c, last, :] for c in range(2)], stiff)
        stiff = jnp.where(strip > 0, above(2 * count + s), 0.0)
        g = flow(*[u[s, c, top, :] - above(2 * s + c) for c in range(2)], stiff)
        for c in range(2):
            total[s, c, last, :] += f[c]
            total[s, c, top, :] -= g[c]


def fast_flows(u, after, fast, index, splat, total, which):
    sections, _, rows, width = u.shape
    for j in which:
        own, block, hops = pairs_of(after, sections)[j]
        stiff = wide_splat(splat, FAST + hops - 1, width)
        for rb in range(rows // ROWS):
            f = side_flow(u, own, fast, block, rows, 0, index, j, stiff, rb)
            for c in range(2):
                total[own, c, rows_of(rb), :] += f[c]


def first_rims_kernel(
    u, w, total_in, half, fast, rim_a, rim_b, shift, before, splat, total, index
):
    sections, _, rows, _ = u.shape

    def damp(rb, carry):
        at = rows_of(rb)
        new = [total[s, c, at, :] + DAMPING * w[s, c, at, :] for s in range(sections) for c in range(2)]
        for k, value in enumerate(new):
            total[k // 2, k % 2, at, :] = value
        return carry

    lax.fori_loop(0, rows // ROWS, damp, 0)

    def body(after):
        put_index(not after, shift, before, index)
        fast_flows(u, not after, fast, index, splat, total, range(3))

    by_side(body)
    rim_flows(u, half, rim_a, rim_b, total, range(sections))


def later_rims_kernel(
    u, total_in, half, fast, rim_a, rim_b, index, splat,
    total, out_u, out_w, new_u, new_w, sem,
):
    sections, _, rows, width = u.shape

    def body(after):
        near = (near_of(after, sections), second_of(after, sections))
        done = [s for s in range(sections) if s not in near]
        fast_flows(u, not after, fast, index, splat, total, (0, 2))
        rim_flows(u, half, rim_a, rim_b, total, done)
        copies = []
        for k, s in enumerate(done):
            moving = wide_splat(splat, MOVING + s, width)
            for rb in range(rows // ROWS):
                at = rows_of(rb)
                for c in range(2):
                    v = total[s, c, at, :] * moving
                    new_w[k, c, at, :] = v
                    new_u[k, c, at, :] = u[s, c, at, :] + STEP * v
            copies += [
                pltpu.make_async_copy(new_u.at[k], out_u.at[s], sem.at[2 * k]),
                pltpu.make_async_copy(new_w.at[k], out_w.at[s], sem.at[2 * k + 1]),
            ]
        for copy in copies:
            copy.start()
        fast_flows(u, not after, fast, index, splat, total, (1,))
        rim_flows(u, half, rim_a, rim_b, total, near)
        for copy in copies:
            copy.wait()

    by_side(body)


def slow_values(u, after, arrived, height, base, index, splat, total, j, rb):
    sections, _, rows, width = u.shape
    own = pairs_of(after, sections)[j][0]
    value = [total[own, c, rows_of(rb), :] for c in range(2)]
    for p, (section, block, hops) in enumerate(pairs_of(after, sections)):
        if section == own:
            stiff = wide_splat(splat, SLOW + hops - 1, width)
            f = side_flow(u, own, arrived, block, height, base, index, p, stiff, rb)
            value = [value[c] + f[c] for c in range(2)]
    return value


def step_kernel(
    u, total, arrived, half, shift, before, splat,
    new_u, new_w, slow, fast, index, rim_a, rim_b,
):
    sections, _, rows, width = u.shape

    def body(after):
        put_index(after, shift, before, index)
        slow_edge = (near_of(after, sections), second_of(after, sections))
        fast_edge = (near_of(not after, sections), second_of(not after, sections))
        for s in range(sections):
            moving = wide_splat(splat, MOVING + s, width)
            for rb in range(rows // ROWS):
                at, row = rows_of(rb), rb * ROWS
                if s in slow_edge:
                    value = slow_values(
                        u, after, arrived, rows, 0, index, splat, total, slow_edge.index(s), rb
                    )
                else:
                    value = [total[s, c, at, :] for c in range(2)]
                for c in range(2):
                    v = value[c] * moving
                    moved = u[s, c, at, :] + STEP * v
                    new_w[s, c, at, :] = v
                    new_u[s, c, at, :] = moved
                    for edge, out in ((slow_edge, slow), (fast_edge, fast)):
                        if s in edge:
                            out[pl.ds((2 * edge.index(s) + c) * rows + row, ROWS), :] = moved

    by_side(body)
    last = slice(rows - 1, rows)
    put_rims(
        lambda s, c: new_u[s, c, 0:1, :],
        lambda s, c: new_u[s, c, last, :],
        lambda s: half[s, 1, last, :],
        rim_a,
        rim_b,
        sections,
    )


def last_kernel(
    base, u, total, arrived, index, splat, out_u_in, out_w_in, out_u, out_w, new_u, new_w, sem
):
    sections, _, rows, width = u.shape
    height = arrived.shape[0] // 4
    rbs = height // ROWS
    part = rbs // 2 if rbs % 2 == 0 else rbs

    def body(after):
        copies = []
        for j in range(2):
            own = pairs_of(after, sections)[j][0]
            moving = wide_splat(splat, MOVING + own, width)
            for k in range(rbs):
                rb = base // ROWS + k
                value = slow_values(u, after, arrived, height, base, index, splat, total, j, rb)
                for c in range(2):
                    v = value[c] * moving
                    new_w[j, c, rows_of(k), :] = v
                    new_u[j, c, rows_of(k), :] = u[own, c, rows_of(rb), :] + STEP * v
                if (k + 1) % part == 0:
                    here = pl.ds((k + 1 - part) * ROWS, part * ROWS)
                    there = pl.ds(base + (k + 1 - part) * ROWS, part * ROWS)
                    for source, target in ((new_u, out_u), (new_w, out_w)):
                        copy = pltpu.make_async_copy(
                            source.at[j, :, here], target.at[own, :, there], sem.at[len(copies)]
                        )
                        copy.start()
                        copies.append(copy)
        for copy in copies:
            copy.wait()

    by_side(body)


def call(kernel, outs, ins, alias=None, scratch=(), in_specs=None, out_specs=None, limit=16 << 20, cost=None):
    return pl.pallas_call(
        kernel,
        out_shape=outs,
        in_specs=in_specs or [VMEM] * len(ins),
        out_specs=out_specs or [VMEM] * len(outs),
        input_output_aliases=alias or {},
        scratch_shapes=scratch,
        cost_estimate=cost,
        compiler_params=pltpu.CompilerParams(vmem_limit_bytes=limit),
    )(*ins)


def per_device(u, w, cls, shift, fixed, stiff, cross):
    sections, _, rows, width = u.shape

    def array(*shape, dtype=jnp.float32):
        return jax.ShapeDtypeStruct(shape, dtype)

    full = array(*u.shape)
    two = array(4 * rows, width)
    rim = array(-(-3 * sections // ROWS) * ROWS, width)
    splat = array(MOVING + sections, ROWS, COLS)
    index = array(3, tail_rows(rows), width, dtype=jnp.int32)
    scalars = [
        pltpu.SMEM(shift.shape, jnp.int32),
        pltpu.SemaphoreType.DMA,
        pltpu.VMEM((3 * sections - 3,) + u.shape[1:], jnp.float32),
    ]
    smem = pl.BlockSpec(memory_space=pltpu.SMEM)

    slow, fast = call(lead_kernel, [two, two], [u])
    slow = exchange(slow, "sec", "b")
    fast = exchange(fast, "sec", "a")
    rim_a, rim_b, splat = call(
        prepare_kernel,
        [rim, rim, splat],
        [u, cls, fast, stiff, cross, fixed],
        in_specs=[VMEM] * 2 + [ANY] + [smem] * 3,
    )
    before_fast = exchange(shift, "sec", "a")
    before_slow = exchange(shift, "sec", "b")
    rim_a = exchange(rim_a, "strip", "a")
    rim_b = exchange(rim_b, "strip", "b")
    total, half = call(
        first_inside_kernel, [full, full], [u, cls, shift, splat], scratch=scalars
    )
    total, fast_index = call(
        first_rims_kernel,
        [full, index],
        [u, w, total, half, fast, rim_a, rim_b, shift, before_fast, splat],
        {2: 0},
    )
    u, w, slow, fast, index, rim_a, rim_b = call(
        step_kernel,
        [full, full, two, two, index, rim, rim],
        [u, total, slow, half, shift, before_slow, splat],
    )
    slow = exchange(slow, "sec", "b")
    fast = exchange(fast, "sec", "a")
    rim_a = exchange(rim_a, "strip", "a")
    rim_b = exchange(rim_b, "strip", "b")
    (total,) = call(later_inside_kernel, [full], [u, w, half, shift, splat], scratch=scalars)
    done = max(sections - 2, 1)
    total, out_u, out_w = call(
        later_rims_kernel,
        [full, full, full],
        [u, total, half, fast, rim_a, rim_b, fast_index, splat],
        {1: 0},
        in_specs=[VMEM] * 8,
        scratch=[pltpu.VMEM((done, 2, rows, width), jnp.float32)] * 2
        + [pltpu.SemaphoreType.DMA((2 * done,))],
        out_specs=[VMEM, ANY, ANY],
    )
    return tuple(
        call(
            functools.partial(last_kernel, 0),
            [full, full],
            [u, total, slow, index, splat, out_u, out_w],
            {5: 0, 6: 1},
            scratch=[pltpu.VMEM((2, 2, rows, width), jnp.float32)] * 2
            + [pltpu.SemaphoreType.DMA((8,))],
            in_specs=[VMEM] * 5 + [ANY] * 2,
            out_specs=[ANY] * 2,
        )
    )


def solution(mesh):
    block = P("sec", None, "strip", None)
    return jax.shard_map(
        per_device,
        mesh=mesh,
        in_specs=(block, block, block, block, P("sec"), P(), P()),
        out_specs=(block, block),
        check_vma=False,
    )
```

```python
import functools

import jax
import jax.numpy as jnp
from jax import lax
from jax.experimental import pallas as pl
from jax.experimental.pallas import tpu as pltpu
from jax.sharding import PartitionSpec as P

ROWS = 8
COLS = 128
CLASSES = 8
DAMPING = 0.9
STEP = 0.35

VMEM = pl.BlockSpec(memory_space=pltpu.VMEM)
ANY = pl.BlockSpec(memory_space=pl.ANY)

INSIDE, SLOW, FAST, TABLE, MOVING = 0, 2, 4, 6, 7


def exchange(value, axis, pairing):
    n = lax.axis_size(axis)
    first = 0 if pairing == "a" else 1
    route = []
    for i in range(first, n - 1, 2):
        route += [(i, i + 1), (i + 1, i)]
    return lax.ppermute(value, axis, route)


def slow_after():
    return lax.rem(lax.axis_index("sec"), 2) == 1


def by_side(body):
    after = slow_after()

    @pl.when(after)
    def _():
        body(True)

    @pl.when(jnp.logical_not(after))
    def _():
        body(False)


def near_of(after, sections):
    return sections - 1 if after else 0


def second_of(after, sections):
    return sections - 2 if after else 1


def pairs_of(after, sections):
    near, second = near_of(after, sections), second_of(after, sections)
    return ((near, 0, 1), (second, 0, 2), (near, 1, 2))


def inverse(value):
    guess = pl.reciprocal(value, approx=True)
    return guess * (2.0 - value * guess)


def flow(ex, ey, half):
    gain = half * (3.0 - inverse(1.0 + ex * ex + ey * ey))
    return gain * ex, gain * ey


def cols_of(cb):
    return slice(cb * COLS, (cb + 1) * COLS)


def rows_of(rb):
    start = rb * ROWS
    return pl.ds(start if isinstance(start, int) else pl.multiple_of(start, ROWS), ROWS)


def tail_rows(rows):
    return -(-(rows // ROWS) // ROWS) * ROWS


def per_tile(width, make):
    return jnp.concatenate([make(cb) for cb in range(width // COLS)], axis=1)


def turned(wide, amounts):
    return per_tile(wide.shape[1], lambda cb: pltpu.roll(wide[:, cols_of(cb)], amounts[cb], 1))


def gathered(wide, index):
    def one(cb):
        full = jnp.broadcast_to(index[:, cols_of(cb)], (ROWS, COLS))
        return jnp.take_along_axis(wide[:, cols_of(cb)], full, axis=1, mode="promise_in_bounds")

    return per_tile(wide.shape[1], one)


def spread(blocks, width):
    return per_tile(width, lambda cb: jnp.broadcast_to(blocks[:, cb : cb + 1], (blocks.shape[0], COLS)))


def lanes(rows, width):
    return lax.broadcasted_iota(jnp.int32, (rows, width), 1) & (COLS - 1)


def put_index(after, shift, before, index):
    sections, _, rbs, _ = shift.shape
    width = index.shape[2]
    lane = lanes(rbs, width)
    for j, (own, block, hops) in enumerate(pairs_of(after, sections)):
        if after:
            offset = spread(shift[own, hops - 1], width)
        else:
            offset = -spread(before[sections - 1 - block, hops - 1], width)
        index[j, 0:rbs, :] = (lane + offset) & (COLS - 1)


def put_rims(first_of, last_of, kv_of, rim_a, rim_b, sections):
    odd = lax.rem(lax.axis_index("strip"), 2) == 1

    def put(line, first, last):
        rim_a[line : line + 1, :] = jnp.where(odd, first, last)
        rim_b[line : line + 1, :] = jnp.where(odd, last, first)

    for s in range(sections):
        for c in range(2):
            put(2 * s + c, first_of(s, c), last_of(s, c))
        stiff = kv_of(s)
        put(2 * sections + s, stiff, stiff)


def look_up(table, index):
    def one(cb):
        tile = jnp.broadcast_to(index[:, cols_of(cb)], (ROWS, COLS))
        return jnp.take_along_axis(table, tile, axis=1, mode="promise_in_bounds")[: index.shape[0]]

    return per_tile(index.shape[1], one)


def put_splat(stiff, cross, fixed, splat):
    sections = fixed.shape[0]
    i, n = lax.axis_index("sec"), lax.axis_size("sec")
    odd = slow_after()
    tile = (ROWS, COLS)
    lane = lax.broadcasted_iota(jnp.int32, tile, 1)
    slow_there = jnp.where(odd, i < n - 1, i > 0)
    fast_there = jnp.where(odd, i > 0, i < n - 1)
    for h in range(2):
        k = jnp.full(tile, cross[h] * (0.5 * STEP))
        splat[INSIDE + h] = k
        splat[SLOW + h] = jnp.where(slow_there, k, 0.0)
        splat[FAST + h] = jnp.where(fast_there, k, 0.0)
    table = jnp.zeros(tile, jnp.float32)
    for k in range(CLASSES):
        table = jnp.where(lane == k, stiff[k] * (0.5 * STEP), table)
    splat[TABLE] = table
    for s in range(sections):
        splat[MOVING + s] = jnp.full(tile, jnp.where(fixed[s] == 0, 1.0, 0.0))


def lead_kernel(u, slow, fast):
    sections, _, rows, _ = u.shape

    def body(after):
        for out, side in ((slow, after), (fast, not after)):
            for k, own in enumerate((near_of(side, sections), second_of(side, sections))):
                for c in range(2):
                    out[(2 * k + c) * rows : (2 * k + c + 1) * rows, :] = u[own, c]

    by_side(body)


def prepare_kernel(u, cls, arrived, stiff, cross, fixed, rim_a, rim_b, splat):
    sections, _, rows, _ = u.shape
    last = slice(rows - 1, rows)
    put_splat(stiff, cross, fixed, splat)
    table = splat[TABLE]
    put_rims(
        lambda s, c: u[s, c, 0:1, :],
        lambda s, c: u[s, c, last, :],
        lambda s: look_up(table, cls[s, 1, last, :]),
        rim_a,
        rim_b,
        sections,
    )


def wide_splat(splat, k, width):
    tile = splat[k]
    return per_tile(width, lambda cb: tile)


def chosen(values, index):
    for bit in range(3):
        on = (index & (1 << bit)) != 0
        values = [jnp.where(on, values[k + 1], values[k]) for k in range(0, len(values), 2)]
    return values[0]


def inside(u, w, total, half_across, half_below, shift, splat, scalars, sem, forces):
    sections, _, rows, width = u.shape
    rbs, cbs = rows // ROWS, width // COLS
    load = pltpu.make_async_copy(shift, scalars, sem)
    load.start()
    bottom = lax.broadcasted_iota(jnp.int32, (rows, COLS), 0) == rows - 1

    def below(cb, carry):
        at = pl.ds(pl.multiple_of(cb * COLS, COLS), COLS)
        for s in range(sections):
            x, y = u[s, 0, :, at], u[s, 1, :, at]
            half = jnp.where(bottom, 0.0, half_below(s, at))
            f = flow(pltpu.roll(x, rows - 1, 0) - x, pltpu.roll(y, rows - 1, 0) - y, half)
            new = [f[c] - pltpu.roll(f[c], 1, 0) for c in range(2)]
            if w is not None:
                new = [DAMPING * w[s, c, :, at] + new[c] for c in range(2)]
            for c in range(2):
                total[s, c, :, at] = new[c]
        return carry

    lax.fori_loop(0, cbs, below, 0)
    load.wait()
    last = lax.broadcasted_iota(jnp.int32, (ROWS, width), 1) == width - 1
    pairs = [(s, hops) for hops in (1, 2) for s in range(sections - hops)]

    def over_rows(body):
        lax.fori_loop(0, rbs, lambda rb, carry: body(rb, rows_of(rb)) or carry, 0, unroll=True)

    def put(k, s, at, f):
        for c in range(2):
            total[s, c, at, :] += f[c]
            forces[k, c, at, :] = f[c]

    def across(s, rb, at):
        x, y = u[s, 0, at, :], u[s, 1, at, :]
        half = jnp.where(last, 0.0, half_across(s, at))
        f = flow(pltpu.roll(x, width - 1, 1) - x, pltpu.roll(y, width - 1, 1) - y, half)
        put(len(pairs) + s, s, at, f)

    def across_back(s, rb, at):
        for c in range(2):
            total[s, c, at, :] -= pltpu.roll(forces[len(pairs) + s, c, at, :], 1, 1)

    def between(k, rb, at):
        s, hops = pairs[k]
        there = [(-scalars[s, hops - 1, rb, cb]) & (COLS - 1) for cb in range(cbs)]
        e = [turned(u[s + hops, c, at, :], there) - u[s, c, at, :] for c in range(2)]
        put(k, s, at, flow(e[0], e[1], wide_splat(splat, INSIDE + hops - 1, width)))

    def between_back(k, rb, at):
        s, hops = pairs[k]
        back = [scalars[s, hops - 1, rb, cb] & (COLS - 1) for cb in range(cbs)]
        for c in range(2):
            total[s + hops, c, at, :] -= turned(forces[k, c, at, :], back)

    for body, count in (
        (across, sections),
        (between, len(pairs)),
        (across_back, sections),
        (between_back, len(pairs)),
    ):
        for k in range(count):
            over_rows(functools.partial(body, k))


def first_inside_kernel(u, cls, shift, splat, total, half, scalars, sem, forces):
    table = splat[TABLE]
    values = [jnp.broadcast_to(table[:, k : k + 1], (ROWS, COLS)) for k in range(CLASSES)]
    rows = u.shape[2]

    def half_across(s, at):
        index = cls[s, 0, at, :]
        k = per_tile(index.shape[1], lambda cb: chosen(values, index[:, cols_of(cb)]))
        half[s, 0, at, :] = k
        return k

    def half_below(s, at):
        index = cls[s, 1, :, at]
        k = jnp.concatenate(
            [look_up(table, index[r : r + ROWS]) for r in range(0, rows, ROWS)], axis=0
        )
        half[s, 1, :, at] = k
        return k

    inside(u, None, total, half_across, half_below, shift, splat, scalars, sem, forces)


def later_inside_kernel(u, w, half, shift, splat, total, scalars, sem, forces):
    def half_across(s, at):
        return half[s, 0, at, :]

    def half_below(s, at):
        return half[s, 1, :, at]

    inside(u, w, total, half_across, half_below, shift, splat, scalars, sem, forces)


def side_flow(u, own, arrived, block, height, base, index, j, half, rb):
    at = rows_of(rb)
    number = index[j, rb : rb + 1, :]
    e = [
        gathered(arrived[pl.ds((2 * block + c) * height + rb * ROWS - base, ROWS), :], number)
        - u[own, c, at, :]
        for c in range(2)
    ]
    return flow(e[0], e[1], half)


def rim_flows(u, half, rim_a, rim_b, total, sections):
    rows = u.shape[2]
    strip = lax.axis_index("strip")
    odd = lax.rem(strip, 2) == 1
    has_below = strip < lax.axis_size("strip") - 1

    def below(r):
        return jnp.where(odd, rim_b[r : r + 1, :], rim_a[r : r + 1, :])

    def above(r):
        return jnp.where(odd, rim_a[r : r + 1, :], rim_b[r : r + 1, :])

    count = u.shape[0]
    last, top = slice(rows - 1, rows), slice(0, 1)
    for s in sections:
        stiff = jnp.where(has_below, half[s, 1, last, :], 0.0)
        f = flow(*[below(2 * s + c) - u[s, c, last, :] for c in range(2)], stiff)
        stiff = jnp.where(strip > 0, above(2 * count + s), 0.0)
        g = flow(*[u[s, c, top, :] - above(2 * s + c) for c in range(2)], stiff)
        for c in range(2):
            total[s, c, last, :] += f[c]
            total[s, c, top, :] -= g[c]


def fast_flows(u, after, fast, index, splat, total, which):
    sections, _, rows, width = u.shape
    for j in which:
        own, block, hops = pairs_of(after, sections)[j]
        stiff = wide_splat(splat, FAST + hops - 1, width)
        for rb in range(rows // ROWS):
            f = side_flow(u, own, fast, block, rows, 0, index, j, stiff, rb)
            for c in range(2):
                total[own, c, rows_of(rb), :] += f[c]


def first_rims_kernel(
    u, w, total_in, half, fast, rim_a, rim_b, shift, before, splat, total, index
):
    sections, _, rows, _ = u.shape

    def damp(rb, carry):
        at = rows_of(rb)
        new = [total[s, c, at, :] + DAMPING * w[s, c, at, :] for s in range(sections) for c in range(2)]
        for k, value in enumerate(new):
            total[k // 2, k % 2, at, :] = value
        return carry

    lax.fori_loop(0, rows // ROWS, damp, 0)

    def body(after):
        put_index(not after, shift, before, index)
        fast_flows(u, not after, fast, index, splat, total, range(3))

    by_side(body)
    rim_flows(u, half, rim_a, rim_b, total, range(sections))


def later_rims_kernel(
    u, total_in, half, fast, rim_a, rim_b, index, splat,
    total, out_u, out_w, new_u, new_w, sem,
):
    sections, _, rows, width = u.shape

    def body(after):
        near = (near_of(after, sections), second_of(after, sections))
        done = [s for s in range(sections) if s not in near]
        fast_flows(u, not after, fast, index, splat, total, (0, 2))
        rim_flows(u, half, rim_a, rim_b, total, done)
        copies = []
        for k, s in enumerate(done):
            moving = wide_splat(splat, MOVING + s, width)
            for rb in range(rows // ROWS):
                at = rows_of(rb)
                for c in range(2):
                    v = total[s, c, at, :] * moving
                    new_w[k, c, at, :] = v
                    new_u[k, c, at, :] = u[s, c, at, :] + STEP * v
            copies += [
                pltpu.make_async_copy(new_u.at[k], out_u.at[s], sem.at[2 * k]),
                pltpu.make_async_copy(new_w.at[k], out_w.at[s], sem.at[2 * k + 1]),
            ]
        for copy in copies:
            copy.start()
        fast_flows(u, not after, fast, index, splat, total, (1,))
        rim_flows(u, half, rim_a, rim_b, total, near)
        for copy in copies:
            copy.wait()

    by_side(body)


def slow_values(u, after, arrived, height, base, index, splat, total, j, rb):
    sections, _, rows, width = u.shape
    own = pairs_of(after, sections)[j][0]
    value = [total[own, c, rows_of(rb), :] for c in range(2)]
    for p, (section, block, hops) in enumerate(pairs_of(after, sections)):
        if section == own:
            stiff = wide_splat(splat, SLOW + hops - 1, width)
            f = side_flow(u, own, arrived, block, height, base, index, p, stiff, rb)
            value = [value[c] + f[c] for c in range(2)]
    return value


def step_kernel(
    u, total, arrived, half, shift, before, splat,
    new_u, new_w, slow_top, slow_rest, fast, index, rim_a, rim_b,
):
    sections, _, rows, width = u.shape
    top = slow_top.shape[0] // 4

    def body(after):
        put_index(after, shift, before, index)
        slow_edge = (near_of(after, sections), second_of(after, sections))
        fast_edge = (near_of(not after, sections), second_of(not after, sections))
        for s in range(sections):
            moving = wide_splat(splat, MOVING + s, width)
            for rb in range(rows // ROWS):
                at, row = rows_of(rb), rb * ROWS
                if s in slow_edge:
                    value = slow_values(
                        u, after, arrived, rows, 0, index, splat, total, slow_edge.index(s), rb
                    )
                else:
                    value = [total[s, c, at, :] for c in range(2)]
                for c in range(2):
                    v = value[c] * moving
                    moved = u[s, c, at, :] + STEP * v
                    new_w[s, c, at, :] = v
                    new_u[s, c, at, :] = moved
                    if s in fast_edge:
                        fast[pl.ds((2 * fast_edge.index(s) + c) * rows + row, ROWS), :] = moved
                    if s in slow_edge:
                        k = 2 * slow_edge.index(s) + c
                        if row < top:
                            slow_top[pl.ds(k * top + row, ROWS), :] = moved
                        else:
                            slow_rest[pl.ds(k * (rows - top) + row - top, ROWS), :] = moved

    by_side(body)
    last = slice(rows - 1, rows)
    put_rims(
        lambda s, c: new_u[s, c, 0:1, :],
        lambda s, c: new_u[s, c, last, :],
        lambda s: half[s, 1, last, :],
        rim_a,
        rim_b,
        sections,
    )


def last_kernel(
    base, u, total, arrived, index, splat, out_u_in, out_w_in, out_u, out_w, new_u, new_w, sem
):
    sections, _, rows, width = u.shape
    height = arrived.shape[0] // 4
    rbs = height // ROWS
    ends = sorted({(rbs + 1) // 2, rbs})

    def body(after):
        copies = []
        for j in range(2):
            own = pairs_of(after, sections)[j][0]
            moving = wide_splat(splat, MOVING + own, width)
            for k in range(rbs):
                rb = base // ROWS + k
                value = slow_values(u, after, arrived, height, base, index, splat, total, j, rb)
                for c in range(2):
                    v = value[c] * moving
                    new_w[j, c, rows_of(k), :] = v
                    new_u[j, c, rows_of(k), :] = u[own, c, rows_of(rb), :] + STEP * v
                if k + 1 in ends:
                    first = 0 if k + 1 == ends[0] else ends[0]
                    size = (k + 1 - first) * ROWS
                    here = pl.ds(first * ROWS, size)
                    there = pl.ds(base + first * ROWS, size)
                    for source, target in ((new_u, out_u), (new_w, out_w)):
                        copy = pltpu.make_async_copy(
                            source.at[j, :, here], target.at[own, :, there], sem.at[len(copies)]
                        )
                        copy.start()
                        copies.append(copy)
        for copy in copies:
            copy.wait()

    by_side(body)


def call(kernel, outs, ins, alias=None, scratch=(), in_specs=None, out_specs=None, limit=16 << 20, cost=None):
    return pl.pallas_call(
        kernel,
        out_shape=outs,
        in_specs=in_specs or [VMEM] * len(ins),
        out_specs=out_specs or [VMEM] * len(outs),
        input_output_aliases=alias or {},
        scratch_shapes=scratch,
        cost_estimate=cost,
        compiler_params=pltpu.CompilerParams(vmem_limit_bytes=limit),
    )(*ins)


def per_device(u, w, cls, shift, fixed, stiff, cross):
    sections, _, rows, width = u.shape

    def array(*shape, dtype=jnp.float32):
        return jax.ShapeDtypeStruct(shape, dtype)

    full = array(*u.shape)
    two = array(4 * rows, width)
    rim = array(-(-3 * sections // ROWS) * ROWS, width)
    splat = array(MOVING + sections, ROWS, COLS)
    index = array(3, tail_rows(rows), width, dtype=jnp.int32)
    scalars = [
        pltpu.SMEM(shift.shape, jnp.int32),
        pltpu.SemaphoreType.DMA,
        pltpu.VMEM((3 * sections - 3,) + u.shape[1:], jnp.float32),
    ]
    smem = pl.BlockSpec(memory_space=pltpu.SMEM)

    slow, fast = call(lead_kernel, [two, two], [u])
    slow = exchange(slow, "sec", "b")
    fast = exchange(fast, "sec", "a")
    rim_a, rim_b, splat = call(
        prepare_kernel,
        [rim, rim, splat],
        [u, cls, fast, stiff, cross, fixed],
        in_specs=[VMEM] * 2 + [ANY] + [smem] * 3,
    )
    before_fast = exchange(shift, "sec", "a")
    before_slow = exchange(shift, "sec", "b")
    rim_a = exchange(rim_a, "strip", "a")
    rim_b = exchange(rim_b, "strip", "b")
    total, half = call(
        first_inside_kernel, [full, full], [u, cls, shift, splat], scratch=scalars
    )
    total, fast_index = call(
        first_rims_kernel,
        [full, index],
        [u, w, total, half, fast, rim_a, rim_b, shift, before_fast, splat],
        {2: 0},
    )
    top = max(rows // ROWS * 7 // 8, 1) * ROWS
    u, w, slow_top, slow_rest, fast, index, rim_a, rim_b = call(
        step_kernel,
        [full, full, array(4 * top, width), array(4 * (rows - top), width), two, index, rim, rim],
        [u, total, slow, half, shift, before_slow, splat],
    )
    slow_top = exchange(slow_top, "sec", "b")
    slow_rest = exchange(slow_rest, "sec", "b")
    fast = exchange(fast, "sec", "a")
    rim_a = exchange(rim_a, "strip", "a")
    rim_b = exchange(rim_b, "strip", "b")
    (total,) = call(later_inside_kernel, [full], [u, w, half, shift, splat], scratch=scalars)
    done = max(sections - 2, 1)
    total, out_u, out_w = call(
        later_rims_kernel,
        [full, full, full],
        [u, total, half, fast, rim_a, rim_b, fast_index, splat],
        {1: 0},
        in_specs=[VMEM] * 8,
        scratch=[pltpu.VMEM((done, 2, rows, width), jnp.float32)] * 2
        + [pltpu.SemaphoreType.DMA((2 * done,))],
        out_specs=[VMEM, ANY, ANY],
    )
    for base, arrived in ((0, slow_top), (top, slow_rest)):
        height = arrived.shape[0] // 4
        out_u, out_w = call(
            functools.partial(last_kernel, base),
            [full, full],
            [u, total, arrived, index, splat, out_u, out_w],
            {5: 0, 6: 1},
            scratch=[pltpu.VMEM((2, 2, height, width), jnp.float32)] * 2
            + [pltpu.SemaphoreType.DMA((8,))],
            in_specs=[VMEM] * 5 + [ANY] * 2,
            out_specs=[ANY] * 2,
        )
    return out_u, out_w


def solution(mesh):
    block = P("sec", None, "strip", None)
    return jax.shard_map(
        per_device,
        mesh=mesh,
        in_specs=(block, block, block, block, P("sec"), P(), P()),
        out_specs=(block, block),
        check_vma=False,
    )
```

```python
import functools

import jax
import jax.numpy as jnp
from jax import lax
from jax.experimental import pallas as pl
from jax.experimental.pallas import tpu as pltpu
from jax.sharding import PartitionSpec as P

ROWS = 8
COLS = 128
CLASSES = 8
DAMPING = 0.9
STEP = 0.35

VMEM = pl.BlockSpec(memory_space=pltpu.VMEM)
ANY = pl.BlockSpec(memory_space=pl.ANY)

INSIDE, SLOW, FAST, TABLE, MOVING = 0, 2, 4, 6, 7


def exchange(value, axis, pairing):
    n = lax.axis_size(axis)
    first = 0 if pairing == "a" else 1
    route = []
    for i in range(first, n - 1, 2):
        route += [(i, i + 1), (i + 1, i)]
    return lax.ppermute(value, axis, route)


def slow_after():
    return lax.rem(lax.axis_index("sec"), 2) == 1


def by_side(body):
    after = slow_after()

    @pl.when(after)
    def _():
        body(True)

    @pl.when(jnp.logical_not(after))
    def _():
        body(False)


def near_of(after, sections):
    return sections - 1 if after else 0


def second_of(after, sections):
    return sections - 2 if after else 1


def pairs_of(after, sections):
    near, second = near_of(after, sections), second_of(after, sections)
    return ((near, 0, 1), (second, 0, 2), (near, 1, 2))


def inverse(value):
    guess = pl.reciprocal(value, approx=True)
    return guess * (2.0 - value * guess)


def flow(ex, ey, half):
    gain = half * (3.0 - inverse(1.0 + ex * ex + ey * ey))
    return gain * ex, gain * ey


def cols_of(cb):
    return slice(cb * COLS, (cb + 1) * COLS)


def rows_of(rb):
    start = rb * ROWS
    return pl.ds(start if isinstance(start, int) else pl.multiple_of(start, ROWS), ROWS)


def tail_rows(rows):
    return -(-(rows // ROWS) // ROWS) * ROWS


def per_tile(width, make):
    return jnp.concatenate([make(cb) for cb in range(width // COLS)], axis=1)


def turned(wide, amounts):
    return per_tile(wide.shape[1], lambda cb: pltpu.roll(wide[:, cols_of(cb)], amounts[cb], 1))


def gathered(wide, index):
    def one(cb):
        full = jnp.broadcast_to(index[:, cols_of(cb)], (ROWS, COLS))
        return jnp.take_along_axis(wide[:, cols_of(cb)], full, axis=1, mode="promise_in_bounds")

    return per_tile(wide.shape[1], one)


def spread(blocks, width):
    return per_tile(width, lambda cb: jnp.broadcast_to(blocks[:, cb : cb + 1], (blocks.shape[0], COLS)))


def lanes(rows, width):
    return lax.broadcasted_iota(jnp.int32, (rows, width), 1) & (COLS - 1)


def put_index(after, shift, before, index):
    sections, _, rbs, _ = shift.shape
    width = index.shape[2]
    lane = lanes(rbs, width)
    for j, (own, block, hops) in enumerate(pairs_of(after, sections)):
        if after:
            offset = spread(shift[own, hops - 1], width)
        else:
            offset = -spread(before[sections - 1 - block, hops - 1], width)
        index[j, 0:rbs, :] = (lane + offset) & (COLS - 1)


def put_rims(first_of, last_of, kv_of, rim_a, rim_b, sections):
    odd = lax.rem(lax.axis_index("strip"), 2) == 1

    def put(line, first, last):
        rim_a[line : line + 1, :] = jnp.where(odd, first, last)
        rim_b[line : line + 1, :] = jnp.where(odd, last, first)

    for s in range(sections):
        for c in range(2):
            put(2 * s + c, first_of(s, c), last_of(s, c))
        stiff = kv_of(s)
        put(2 * sections + s, stiff, stiff)


def look_up(table, index):
    def one(cb):
        tile = jnp.broadcast_to(index[:, cols_of(cb)], (ROWS, COLS))
        return jnp.take_along_axis(table, tile, axis=1, mode="promise_in_bounds")[: index.shape[0]]

    return per_tile(index.shape[1], one)


def put_splat(stiff, cross, fixed, splat):
    sections = fixed.shape[0]
    i, n = lax.axis_index("sec"), lax.axis_size("sec")
    odd = slow_after()
    tile = (ROWS, COLS)
    lane = lax.broadcasted_iota(jnp.int32, tile, 1)
    slow_there = jnp.where(odd, i < n - 1, i > 0)
    fast_there = jnp.where(odd, i > 0, i < n - 1)
    for h in range(2):
        k = jnp.full(tile, cross[h] * (0.5 * STEP))
        splat[INSIDE + h] = k
        splat[SLOW + h] = jnp.where(slow_there, k, 0.0)
        splat[FAST + h] = jnp.where(fast_there, k, 0.0)
    table = jnp.zeros(tile, jnp.float32)
    for k in range(CLASSES):
        table = jnp.where(lane == k, stiff[k] * (0.5 * STEP), table)
    splat[TABLE] = table
    for s in range(sections):
        splat[MOVING + s] = jnp.full(tile, jnp.where(fixed[s] == 0, 1.0, 0.0))


def lead_kernel(u, slow, fast):
    sections, _, rows, _ = u.shape

    def body(after):
        for out, side in ((slow, after), (fast, not after)):
            for k, own in enumerate((near_of(side, sections), second_of(side, sections))):
                for c in range(2):
                    out[(2 * k + c) * rows : (2 * k + c + 1) * rows, :] = u[own, c]

    by_side(body)


def prepare_kernel(u, cls, arrived, stiff, cross, fixed, rim_a, rim_b, splat):
    sections, _, rows, _ = u.shape
    last = slice(rows - 1, rows)
    put_splat(stiff, cross, fixed, splat)
    table = splat[TABLE]
    put_rims(
        lambda s, c: u[s, c, 0:1, :],
        lambda s, c: u[s, c, last, :],
        lambda s: look_up(table, cls[s, 1, last, :]),
        rim_a,
        rim_b,
        sections,
    )


def wide_splat(splat, k, width):
    tile = splat[k]
    return per_tile(width, lambda cb: tile)


def chosen(values, index):
    for bit in range(3):
        on = (index & (1 << bit)) != 0
        values = [jnp.where(on, values[k + 1], values[k]) for k in range(0, len(values), 2)]
    return values[0]


def inside(u, w, total, half_across, half_below, shift, splat, scalars, sem, forces):
    sections, _, rows, width = u.shape
    rbs, cbs = rows // ROWS, width // COLS
    load = pltpu.make_async_copy(shift, scalars, sem)
    load.start()
    bottom = lax.broadcasted_iota(jnp.int32, (rows, COLS), 0) == rows - 1

    def below(cb, carry):
        at = pl.ds(pl.multiple_of(cb * COLS, COLS), COLS)
        for s in range(sections):
            x, y = u[s, 0, :, at], u[s, 1, :, at]
            half = jnp.where(bottom, 0.0, half_below(s, at))
            f = flow(pltpu.roll(x, rows - 1, 0) - x, pltpu.roll(y, rows - 1, 0) - y, half)
            new = [f[c] - pltpu.roll(f[c], 1, 0) for c in range(2)]
            if w is not None:
                new = [DAMPING * w[s, c, :, at] + new[c] for c in range(2)]
            for c in range(2):
                total[s, c, :, at] = new[c]
        return carry

    lax.fori_loop(0, cbs, below, 0)
    load.wait()
    last = lax.broadcasted_iota(jnp.int32, (ROWS, width), 1) == width - 1
    pairs = [(s, hops) for hops in (1, 2) for s in range(sections - hops)]

    def over_rows(body):
        lax.fori_loop(0, rbs, lambda rb, carry: body(rb, rows_of(rb)) or carry, 0, unroll=True)

    def put(k, s, at, f):
        for c in range(2):
            total[s, c, at, :] += f[c]
            forces[k, c, at, :] = f[c]

    def across(s, rb, at):
        x, y = u[s, 0, at, :], u[s, 1, at, :]
        half = jnp.where(last, 0.0, half_across(s, at))
        f = flow(pltpu.roll(x, width - 1, 1) - x, pltpu.roll(y, width - 1, 1) - y, half)
        put(len(pairs) + s, s, at, f)

    def across_back(s, rb, at):
        for c in range(2):
            total[s, c, at, :] -= pltpu.roll(forces[len(pairs) + s, c, at, :], 1, 1)

    def between(k, rb, at):
        s, hops = pairs[k]
        there = [(-scalars[s, hops - 1, rb, cb]) & (COLS - 1) for cb in range(cbs)]
        e = [turned(u[s + hops, c, at, :], there) - u[s, c, at, :] for c in range(2)]
        put(k, s, at, flow(e[0], e[1], wide_splat(splat, INSIDE + hops - 1, width)))

    def between_back(k, rb, at):
        s, hops = pairs[k]
        back = [scalars[s, hops - 1, rb, cb] & (COLS - 1) for cb in range(cbs)]
        for c in range(2):
            total[s + hops, c, at, :] -= turned(forces[k, c, at, :], back)

    for body, count in (
        (across, sections),
        (between, len(pairs)),
        (across_back, sections),
        (between_back, len(pairs)),
    ):
        for k in range(count):
            over_rows(functools.partial(body, k))


def first_inside_kernel(u, cls, shift, splat, total, half, scalars, sem, forces):
    table = splat[TABLE]
    values = [jnp.broadcast_to(table[:, k : k + 1], (ROWS, COLS)) for k in range(CLASSES)]
    rows = u.shape[2]

    def half_across(s, at):
        index = cls[s, 0, at, :]
        k = per_tile(index.shape[1], lambda cb: chosen(values, index[:, cols_of(cb)]))
        half[s, 0, at, :] = k
        return k

    def half_below(s, at):
        index = cls[s, 1, :, at]
        k = jnp.concatenate(
            [look_up(table, index[r : r + ROWS]) for r in range(0, rows, ROWS)], axis=0
        )
        half[s, 1, :, at] = k
        return k

    inside(u, None, total, half_across, half_below, shift, splat, scalars, sem, forces)


def later_inside_kernel(u, w, half, shift, splat, total, scalars, sem, forces):
    def half_across(s, at):
        return half[s, 0, at, :]

    def half_below(s, at):
        return half[s, 1, :, at]

    inside(u, w, total, half_across, half_below, shift, splat, scalars, sem, forces)


def side_flow(u, own, arrived, block, height, base, index, j, half, rb):
    at = rows_of(rb)
    number = index[j, rb : rb + 1, :]
    e = [
        gathered(arrived[pl.ds((2 * block + c) * height + rb * ROWS - base, ROWS), :], number)
        - u[own, c, at, :]
        for c in range(2)
    ]
    return flow(e[0], e[1], half)


def rim_flows(u, half, rim_a, rim_b, total, sections):
    rows = u.shape[2]
    strip = lax.axis_index("strip")
    odd = lax.rem(strip, 2) == 1
    has_below = strip < lax.axis_size("strip") - 1

    def below(r):
        return jnp.where(odd, rim_b[r : r + 1, :], rim_a[r : r + 1, :])

    def above(r):
        return jnp.where(odd, rim_a[r : r + 1, :], rim_b[r : r + 1, :])

    count = u.shape[0]
    last, top = slice(rows - 1, rows), slice(0, 1)
    for s in sections:
        stiff = jnp.where(has_below, half[s, 1, last, :], 0.0)
        f = flow(*[below(2 * s + c) - u[s, c, last, :] for c in range(2)], stiff)
        stiff = jnp.where(strip > 0, above(2 * count + s), 0.0)
        g = flow(*[u[s, c, top, :] - above(2 * s + c) for c in range(2)], stiff)
        for c in range(2):
            total[s, c, last, :] += f[c]
            total[s, c, top, :] -= g[c]


def fast_flows(u, after, fast, index, splat, total, which):
    sections, _, rows, width = u.shape
    for j in which:
        own, block, hops = pairs_of(after, sections)[j]
        stiff = wide_splat(splat, FAST + hops - 1, width)
        for rb in range(rows // ROWS):
            f = side_flow(u, own, fast, block, rows, 0, index, j, stiff, rb)
            for c in range(2):
                total[own, c, rows_of(rb), :] += f[c]


def first_rims_kernel(
    u, w, total_in, half, fast, rim_a, rim_b, shift, before, splat,
    total, index, new_u, new_w, sent,
):
    sections, _, rows, _ = u.shape

    def damp(rb, carry):
        at = rows_of(rb)
        new = [total[s, c, at, :] + DAMPING * w[s, c, at, :] for s in range(sections) for c in range(2)]
        for k, value in enumerate(new):
            total[k // 2, k % 2, at, :] = value
        return carry

    lax.fori_loop(0, rows // ROWS, damp, 0)

    def body(after):
        put_index(not after, shift, before, index)
        fast_flows(u, not after, fast, index, splat, total, range(3))

    by_side(body)
    rim_flows(u, half, rim_a, rim_b, total, range(sections))

    def settle(after):
        slow_edge = (near_of(after, sections), second_of(after, sections))
        fast_edge = (near_of(not after, sections), second_of(not after, sections))
        for s in range(sections):
            if s in slow_edge:
                continue
            moving = wide_splat(splat, MOVING + s, u.shape[3])
            for row in range(0, rows, ROWS):
                at = pl.ds(row, ROWS)
                for c in range(2):
                    v = total[s, c, at, :] * moving
                    moved = u[s, c, at, :] + STEP * v
                    new_w[s, c, at, :] = v
                    new_u[s, c, at, :] = moved
                    if s in fast_edge:
                        sent[pl.ds((2 * fast_edge.index(s) + c) * rows + row, ROWS), :] = moved

    by_side(settle)


def later_rims_kernel(
    u, total_in, half, fast, rim_a, rim_b, index, splat,
    total, out_u, out_w, new_u, new_w, sem,
):
    sections, _, rows, width = u.shape

    def body(after):
        near = (near_of(after, sections), second_of(after, sections))
        done = [s for s in range(sections) if s not in near]
        fast_flows(u, not after, fast, index, splat, total, (0, 2))
        rim_flows(u, half, rim_a, rim_b, total, done)
        copies = []
        for k, s in enumerate(done):
            moving = wide_splat(splat, MOVING + s, width)
            for rb in range(rows // ROWS):
                at = rows_of(rb)
                for c in range(2):
                    v = total[s, c, at, :] * moving
                    new_w[k, c, at, :] = v
                    new_u[k, c, at, :] = u[s, c, at, :] + STEP * v
            copies += [
                pltpu.make_async_copy(new_u.at[k], out_u.at[s], sem.at[2 * k]),
                pltpu.make_async_copy(new_w.at[k], out_w.at[s], sem.at[2 * k + 1]),
            ]
        for copy in copies:
            copy.start()
        fast_flows(u, not after, fast, index, splat, total, (1,))
        rim_flows(u, half, rim_a, rim_b, total, near)
        for copy in copies:
            copy.wait()

    by_side(body)


def slow_values(u, after, arrived, height, base, index, splat, total, j, rb):
    sections, _, rows, width = u.shape
    own = pairs_of(after, sections)[j][0]
    value = [total[own, c, rows_of(rb), :] for c in range(2)]
    for p, (section, block, hops) in enumerate(pairs_of(after, sections)):
        if section == own:
            stiff = wide_splat(splat, SLOW + hops - 1, width)
            f = side_flow(u, own, arrived, block, height, base, index, p, stiff, rb)
            value = [value[c] + f[c] for c in range(2)]
    return value


def step_kernel(
    u, total, arrived, half, shift, before, splat, new_u_in, new_w_in, fast_in,
    new_u, new_w, slow, fast, index, rim_a, rim_b,
):
    sections, _, rows, width = u.shape

    def body(after):
        put_index(after, shift, before, index)
        slow_edge = (near_of(after, sections), second_of(after, sections))
        fast_edge = (near_of(not after, sections), second_of(not after, sections))
        for j, s in enumerate(slow_edge):
            moving = wide_splat(splat, MOVING + s, width)
            for rb in range(rows // ROWS):
                at, row = rows_of(rb), rb * ROWS
                value = slow_values(u, after, arrived, rows, 0, index, splat, total, j, rb)
                for c in range(2):
                    v = value[c] * moving
                    moved = u[s, c, at, :] + STEP * v
                    new_w[s, c, at, :] = v
                    new_u[s, c, at, :] = moved
                    for edge, out in ((slow_edge, slow), (fast_edge, fast)):
                        if s in edge:
                            out[pl.ds((2 * edge.index(s) + c) * rows + row, ROWS), :] = moved

    by_side(body)
    last = slice(rows - 1, rows)
    put_rims(
        lambda s, c: new_u[s, c, 0:1, :],
        lambda s, c: new_u[s, c, last, :],
        lambda s: half[s, 1, last, :],
        rim_a,
        rim_b,
        sections,
    )


def last_kernel(
    base, u, total, arrived, index, splat, out_u_in, out_w_in, out_u, out_w, new_u, new_w, sem
):
    sections, _, rows, width = u.shape
    height = arrived.shape[0] // 4
    rbs = height // ROWS
    part = rbs // 2 if rbs % 2 == 0 else rbs

    def body(after):
        copies = []
        for j in range(2):
            own = pairs_of(after, sections)[j][0]
            moving = wide_splat(splat, MOVING + own, width)
            for k in range(rbs):
                rb = base // ROWS + k
                value = slow_values(u, after, arrived, height, base, index, splat, total, j, rb)
                for c in range(2):
                    v = value[c] * moving
                    new_w[j, c, rows_of(k), :] = v
                    new_u[j, c, rows_of(k), :] = u[own, c, rows_of(rb), :] + STEP * v
                if (k + 1) % part == 0:
                    here = pl.ds((k + 1 - part) * ROWS, part * ROWS)
                    there = pl.ds(base + (k + 1 - part) * ROWS, part * ROWS)
                    for source, target in ((new_u, out_u), (new_w, out_w)):
                        copy = pltpu.make_async_copy(
                            source.at[j, :, here], target.at[own, :, there], sem.at[len(copies)]
                        )
                        copy.start()
                        copies.append(copy)
        for copy in copies:
            copy.wait()

    by_side(body)


def call(kernel, outs, ins, alias=None, scratch=(), in_specs=None, out_specs=None, limit=16 << 20, cost=None):
    return pl.pallas_call(
        kernel,
        out_shape=outs,
        in_specs=in_specs or [VMEM] * len(ins),
        out_specs=out_specs or [VMEM] * len(outs),
        input_output_aliases=alias or {},
        scratch_shapes=scratch,
        cost_estimate=cost,
        compiler_params=pltpu.CompilerParams(vmem_limit_bytes=limit),
    )(*ins)


def per_device(u, w, cls, shift, fixed, stiff, cross):
    sections, _, rows, width = u.shape

    def array(*shape, dtype=jnp.float32):
        return jax.ShapeDtypeStruct(shape, dtype)

    full = array(*u.shape)
    two = array(4 * rows, width)
    rim = array(-(-3 * sections // ROWS) * ROWS, width)
    splat = array(MOVING + sections, ROWS, COLS)
    index = array(3, tail_rows(rows), width, dtype=jnp.int32)
    scalars = [
        pltpu.SMEM(shift.shape, jnp.int32),
        pltpu.SemaphoreType.DMA,
        pltpu.VMEM((3 * sections - 3,) + u.shape[1:], jnp.float32),
    ]
    smem = pl.BlockSpec(memory_space=pltpu.SMEM)

    slow, fast = call(lead_kernel, [two, two], [u])
    slow = exchange(slow, "sec", "b")
    fast = exchange(fast, "sec", "a")
    rim_a, rim_b, splat = call(
        prepare_kernel,
        [rim, rim, splat],
        [u, cls, fast, stiff, cross, fixed],
        in_specs=[VMEM] * 2 + [ANY] + [smem] * 3,
    )
    before_fast = exchange(shift, "sec", "a")
    before_slow = exchange(shift, "sec", "b")
    rim_a = exchange(rim_a, "strip", "a")
    rim_b = exchange(rim_b, "strip", "b")
    total, half = call(
        first_inside_kernel, [full, full], [u, cls, shift, splat], scratch=scalars
    )
    total, fast_index, new_u, new_w, fast = call(
        first_rims_kernel,
        [full, index, full, full, two],
        [u, w, total, half, fast, rim_a, rim_b, shift, before_fast, splat],
        {2: 0},
    )
    u, w, slow, fast, index, rim_a, rim_b = call(
        step_kernel,
        [full, full, two, two, index, rim, rim],
        [u, total, slow, half, shift, before_slow, splat, new_u, new_w, fast],
        {7: 0, 8: 1, 9: 3},
    )
    slow = exchange(slow, "sec", "b")
    fast = exchange(fast, "sec", "a")
    rim_a = exchange(rim_a, "strip", "a")
    rim_b = exchange(rim_b, "strip", "b")
    (total,) = call(later_inside_kernel, [full], [u, w, half, shift, splat], scratch=scalars)
    done = max(sections - 2, 1)
    total, out_u, out_w = call(
        later_rims_kernel,
        [full, full, full],
        [u, total, half, fast, rim_a, rim_b, fast_index, splat],
        {1: 0},
        in_specs=[VMEM] * 8,
        scratch=[pltpu.VMEM((done, 2, rows, width), jnp.float32)] * 2
        + [pltpu.SemaphoreType.DMA((2 * done,))],
        out_specs=[VMEM, ANY, ANY],
    )
    return tuple(
        call(
            functools.partial(last_kernel, 0),
            [full, full],
            [u, total, slow, index, splat, out_u, out_w],
            {5: 0, 6: 1},
            scratch=[pltpu.VMEM((2, 2, rows, width), jnp.float32)] * 2
            + [pltpu.SemaphoreType.DMA((8,))],
            in_specs=[VMEM] * 5 + [ANY] * 2,
            out_specs=[ANY] * 2,
        )
    )


def solution(mesh):
    block = P("sec", None, "strip", None)
    return jax.shard_map(
        per_device,
        mesh=mesh,
        in_specs=(block, block, block, block, P("sec"), P(), P()),
        out_specs=(block, block),
        check_vma=False,
    )
```

```python
import functools

import jax
import jax.numpy as jnp
from jax import lax
from jax.experimental import pallas as pl
from jax.experimental.pallas import tpu as pltpu
from jax.sharding import PartitionSpec as P

ROWS = 8
COLS = 128
CLASSES = 8
DAMPING = 0.9
STEP = 0.35

VMEM = pl.BlockSpec(memory_space=pltpu.VMEM)
ANY = pl.BlockSpec(memory_space=pl.ANY)

INSIDE, SLOW, FAST, TABLE, MOVING = 0, 2, 4, 6, 7


def exchange(value, axis, pairing):
    n = lax.axis_size(axis)
    first = 0 if pairing == "a" else 1
    route = []
    for i in range(first, n - 1, 2):
        route += [(i, i + 1), (i + 1, i)]
    return lax.ppermute(value, axis, route)


def slow_after():
    return lax.rem(lax.axis_index("sec"), 2) == 1


def by_side(body):
    after = slow_after()

    @pl.when(after)
    def _():
        body(True)

    @pl.when(jnp.logical_not(after))
    def _():
        body(False)


def near_of(after, sections):
    return sections - 1 if after else 0


def second_of(after, sections):
    return sections - 2 if after else 1


def pairs_of(after, sections):
    near, second = near_of(after, sections), second_of(after, sections)
    return ((near, 0, 1), (second, 0, 2), (near, 1, 2))


def inverse(value):
    guess = pl.reciprocal(value, approx=True)
    return guess * (2.0 - value * guess)


def flow(ex, ey, half):
    gain = half * (3.0 - inverse(1.0 + ex * ex + ey * ey))
    return gain * ex, gain * ey


def cols_of(cb):
    return slice(cb * COLS, (cb + 1) * COLS)


def rows_of(rb):
    start = rb * ROWS
    return pl.ds(start if isinstance(start, int) else pl.multiple_of(start, ROWS), ROWS)


def tail_rows(rows):
    return -(-(rows // ROWS) // ROWS) * ROWS


def per_tile(width, make):
    return jnp.concatenate([make(cb) for cb in range(width // COLS)], axis=1)


def turned(wide, amounts):
    return per_tile(wide.shape[1], lambda cb: pltpu.roll(wide[:, cols_of(cb)], amounts[cb], 1))


def gathered(wide, index):
    def one(cb):
        full = jnp.broadcast_to(index[:, cols_of(cb)], (ROWS, COLS))
        return jnp.take_along_axis(wide[:, cols_of(cb)], full, axis=1, mode="promise_in_bounds")

    return per_tile(wide.shape[1], one)


def spread(blocks, width):
    return per_tile(width, lambda cb: jnp.broadcast_to(blocks[:, cb : cb + 1], (blocks.shape[0], COLS)))


def lanes(rows, width):
    return lax.broadcasted_iota(jnp.int32, (rows, width), 1) & (COLS - 1)


def put_index(after, shift, before, index):
    sections, _, rbs, _ = shift.shape
    width = index.shape[2]
    lane = lanes(rbs, width)
    for j, (own, block, hops) in enumerate(pairs_of(after, sections)):
        if after:
            offset = spread(shift[own, hops - 1], width)
        else:
            offset = -spread(before[sections - 1 - block, hops - 1], width)
        index[j, 0:rbs, :] = (lane + offset) & (COLS - 1)


def put_rims(first_of, last_of, kv_of, rim_a, rim_b, sections):
    odd = lax.rem(lax.axis_index("strip"), 2) == 1

    def put(line, first, last):
        rim_a[line : line + 1, :] = jnp.where(odd, first, last)
        rim_b[line : line + 1, :] = jnp.where(odd, last, first)

    for s in range(sections):
        for c in range(2):
            put(2 * s + c, first_of(s, c), last_of(s, c))
        stiff = kv_of(s)
        put(2 * sections + s, stiff, stiff)


def look_up(table, index):
    def one(cb):
        tile = jnp.broadcast_to(index[:, cols_of(cb)], (ROWS, COLS))
        return jnp.take_along_axis(table, tile, axis=1, mode="promise_in_bounds")[: index.shape[0]]

    return per_tile(index.shape[1], one)


def put_splat(stiff, cross, fixed, splat):
    sections = fixed.shape[0]
    i, n = lax.axis_index("sec"), lax.axis_size("sec")
    odd = slow_after()
    tile = (ROWS, COLS)
    lane = lax.broadcasted_iota(jnp.int32, tile, 1)
    slow_there = jnp.where(odd, i < n - 1, i > 0)
    fast_there = jnp.where(odd, i > 0, i < n - 1)
    for h in range(2):
        k = jnp.full(tile, cross[h] * (0.5 * STEP))
        splat[INSIDE + h] = k
        splat[SLOW + h] = jnp.where(slow_there, k, 0.0)
        splat[FAST + h] = jnp.where(fast_there, k, 0.0)
    table = jnp.zeros(tile, jnp.float32)
    for k in range(CLASSES):
        table = jnp.where(lane == k, stiff[k] * (0.5 * STEP), table)
    splat[TABLE] = table
    for s in range(sections):
        splat[MOVING + s] = jnp.full(tile, jnp.where(fixed[s] == 0, 1.0, 0.0))


def lead_kernel(u, slow, fast):
    sections, _, rows, _ = u.shape

    def body(after):
        for out, side in ((slow, after), (fast, not after)):
            for k, own in enumerate((near_of(side, sections), second_of(side, sections))):
                for c in range(2):
                    out[(2 * k + c) * rows : (2 * k + c + 1) * rows, :] = u[own, c]

    by_side(body)


def prepare_kernel(u, cls, arrived, stiff, cross, fixed, rim_a, rim_b, splat):
    sections, _, rows, _ = u.shape
    last = slice(rows - 1, rows)
    put_splat(stiff, cross, fixed, splat)
    table = splat[TABLE]
    put_rims(
        lambda s, c: u[s, c, 0:1, :],
        lambda s, c: u[s, c, last, :],
        lambda s: look_up(table, cls[s, 1, last, :]),
        rim_a,
        rim_b,
        sections,
    )


def wide_splat(splat, k, width):
    tile = splat[k]
    return per_tile(width, lambda cb: tile)


def chosen(values, index):
    for bit in range(3):
        on = (index & (1 << bit)) != 0
        values = [jnp.where(on, values[k + 1], values[k]) for k in range(0, len(values), 2)]
    return values[0]


def inside(u, w, total, half_across, half_below, shift, splat, scalars, sem, forces):
    sections, _, rows, width = u.shape
    rbs, cbs = rows // ROWS, width // COLS
    load = pltpu.make_async_copy(shift, scalars, sem)
    load.start()
    bottom = lax.broadcasted_iota(jnp.int32, (rows, COLS), 0) == rows - 1

    def below(cb, carry):
        at = pl.ds(pl.multiple_of(cb * COLS, COLS), COLS)
        for s in range(sections):
            x, y = u[s, 0, :, at], u[s, 1, :, at]
            half = jnp.where(bottom, 0.0, half_below(s, at))
            f = flow(pltpu.roll(x, rows - 1, 0) - x, pltpu.roll(y, rows - 1, 0) - y, half)
            new = [f[c] - pltpu.roll(f[c], 1, 0) for c in range(2)]
            if w is not None:
                new = [DAMPING * w[s, c, :, at] + new[c] for c in range(2)]
            for c in range(2):
                total[s, c, :, at] = new[c]
        return carry

    lax.fori_loop(0, cbs, below, 0)
    load.wait()
    last = lax.broadcasted_iota(jnp.int32, (ROWS, width), 1) == width - 1
    pairs = [(s, hops) for hops in (1, 2) for s in range(sections - hops)]

    def over_rows(body):
        lax.fori_loop(0, rbs, lambda rb, carry: body(rb, rows_of(rb)) or carry, 0, unroll=True)

    def put(k, s, at, f):
        for c in range(2):
            total[s, c, at, :] += f[c]
            forces[k, c, at, :] = f[c]

    def across(s, rb, at):
        x, y = u[s, 0, at, :], u[s, 1, at, :]
        half = jnp.where(last, 0.0, half_across(s, at))
        f = flow(pltpu.roll(x, width - 1, 1) - x, pltpu.roll(y, width - 1, 1) - y, half)
        put(len(pairs) + s, s, at, f)

    def across_back(s, rb, at):
        for c in range(2):
            total[s, c, at, :] -= pltpu.roll(forces[len(pairs) + s, c, at, :], 1, 1)

    def between(k, rb, at):
        s, hops = pairs[k]
        there = [(-scalars[s, hops - 1, rb, cb]) & (COLS - 1) for cb in range(cbs)]
        e = [turned(u[s + hops, c, at, :], there) - u[s, c, at, :] for c in range(2)]
        put(k, s, at, flow(e[0], e[1], wide_splat(splat, INSIDE + hops - 1, width)))

    def between_back(k, rb, at):
        s, hops = pairs[k]
        back = [scalars[s, hops - 1, rb, cb] & (COLS - 1) for cb in range(cbs)]
        for c in range(2):
            total[s + hops, c, at, :] -= turned(forces[k, c, at, :], back)

    for body, count in (
        (across, sections),
        (between, len(pairs)),
        (across_back, sections),
        (between_back, len(pairs)),
    ):
        for k in range(count):
            over_rows(functools.partial(body, k))


def first_inside_kernel(u, cls, shift, splat, total, half, scalars, sem, forces):
    table = splat[TABLE]
    values = [jnp.broadcast_to(table[:, k : k + 1], (ROWS, COLS)) for k in range(CLASSES)]
    rows = u.shape[2]

    def half_across(s, at):
        index = cls[s, 0, at, :]
        k = per_tile(index.shape[1], lambda cb: chosen(values, index[:, cols_of(cb)]))
        half[s, 0, at, :] = k
        return k

    def half_below(s, at):
        index = cls[s, 1, :, at]
        k = jnp.concatenate(
            [look_up(table, index[r : r + ROWS]) for r in range(0, rows, ROWS)], axis=0
        )
        half[s, 1, :, at] = k
        return k

    inside(u, None, total, half_across, half_below, shift, splat, scalars, sem, forces)


def later_inside_kernel(u, w, half, shift, splat, total, scalars, sem, forces):
    def half_across(s, at):
        return half[s, 0, at, :]

    def half_below(s, at):
        return half[s, 1, :, at]

    inside(u, w, total, half_across, half_below, shift, splat, scalars, sem, forces)


def side_flow(u, own, arrived, block, height, base, index, j, half, rb):
    at = rows_of(rb)
    number = index[j, rb : rb + 1, :]
    e = [
        gathered(arrived[pl.ds((2 * block + c) * height + rb * ROWS - base, ROWS), :], number)
        - u[own, c, at, :]
        for c in range(2)
    ]
    return flow(e[0], e[1], half)


def rim_flows(u, half, rim_a, rim_b, total, sections):
    rows = u.shape[2]
    strip = lax.axis_index("strip")
    odd = lax.rem(strip, 2) == 1
    has_below = strip < lax.axis_size("strip") - 1

    def below(r):
        return jnp.where(odd, rim_b[r : r + 1, :], rim_a[r : r + 1, :])

    def above(r):
        return jnp.where(odd, rim_a[r : r + 1, :], rim_b[r : r + 1, :])

    count = u.shape[0]
    last, top = slice(rows - 1, rows), slice(0, 1)
    for s in sections:
        stiff = jnp.where(has_below, half[s, 1, last, :], 0.0)
        f = flow(*[below(2 * s + c) - u[s, c, last, :] for c in range(2)], stiff)
        stiff = jnp.where(strip > 0, above(2 * count + s), 0.0)
        g = flow(*[u[s, c, top, :] - above(2 * s + c) for c in range(2)], stiff)
        for c in range(2):
            total[s, c, last, :] += f[c]
            total[s, c, top, :] -= g[c]


def fast_flows(u, after, fast, index, splat, total, which):
    sections, _, rows, width = u.shape
    for j in which:
        own, block, hops = pairs_of(after, sections)[j]
        stiff = wide_splat(splat, FAST + hops - 1, width)
        for rb in range(rows // ROWS):
            f = side_flow(u, own, fast, block, rows, 0, index, j, stiff, rb)
            for c in range(2):
                total[own, c, rows_of(rb), :] += f[c]


def first_rims_kernel(
    u, w, total_in, half, fast, rim_a, rim_b, shift, before, splat, total, index
):
    sections, _, rows, _ = u.shape

    def damp(rb, carry):
        at = rows_of(rb)
        new = [total[s, c, at, :] + DAMPING * w[s, c, at, :] for s in range(sections) for c in range(2)]
        for k, value in enumerate(new):
            total[k // 2, k % 2, at, :] = value
        return carry

    lax.fori_loop(0, rows // ROWS, damp, 0)

    def body(after):
        put_index(not after, shift, before, index)
        fast_flows(u, not after, fast, index, splat, total, range(3))

    by_side(body)
    rim_flows(u, half, rim_a, rim_b, total, range(sections))


def later_rims_kernel(
    u, total_in, half, fast, rim_a, rim_b, index, splat,
    total, out_u, out_w, new_u, new_w, sem,
):
    sections, _, rows, width = u.shape

    def body(after):
        near = (near_of(after, sections), second_of(after, sections))
        done = [s for s in range(sections) if s not in near]
        fast_flows(u, not after, fast, index, splat, total, (0, 2))
        rim_flows(u, half, rim_a, rim_b, total, done)
        copies = []
        for k, s in enumerate(done):
            moving = wide_splat(splat, MOVING + s, width)
            for rb in range(rows // ROWS):
                at = rows_of(rb)
                for c in range(2):
                    v = total[s, c, at, :] * moving
                    new_w[k, c, at, :] = v
                    new_u[k, c, at, :] = u[s, c, at, :] + STEP * v
            copies += [
                pltpu.make_async_copy(new_u.at[k], out_u.at[s], sem.at[2 * k]),
                pltpu.make_async_copy(new_w.at[k], out_w.at[s], sem.at[2 * k + 1]),
            ]
        for copy in copies:
            copy.start()
        fast_flows(u, not after, fast, index, splat, total, (1,))
        rim_flows(u, half, rim_a, rim_b, total, near)
        for copy in copies:
            copy.wait()

    by_side(body)


def slow_values(u, after, arrived, height, base, index, splat, total, j, rb):
    sections, _, rows, width = u.shape
    own = pairs_of(after, sections)[j][0]
    value = [total[own, c, rows_of(rb), :] for c in range(2)]
    for p, (section, block, hops) in enumerate(pairs_of(after, sections)):
        if section == own:
            stiff = wide_splat(splat, SLOW + hops - 1, width)
            f = side_flow(u, own, arrived, block, height, base, index, p, stiff, rb)
            value = [value[c] + f[c] for c in range(2)]
    return value


def step_kernel(
    u, total, arrived, half, shift, before, splat,
    new_u, new_w, slow, fast, index, rim_a, rim_b,
):
    sections, _, rows, width = u.shape

    def body(after):
        put_index(after, shift, before, index)
        slow_edge = (near_of(after, sections), second_of(after, sections))
        fast_edge = (near_of(not after, sections), second_of(not after, sections))
        for s in range(sections):
            moving = wide_splat(splat, MOVING + s, width)
            for rb in range(rows // ROWS):
                at, row = rows_of(rb), rb * ROWS
                if s in slow_edge:
                    value = slow_values(
                        u, after, arrived, rows, 0, index, splat, total, slow_edge.index(s), rb
                    )
                else:
                    value = [total[s, c, at, :] for c in range(2)]
                for c in range(2):
                    v = value[c] * moving
                    moved = u[s, c, at, :] + STEP * v
                    new_w[s, c, at, :] = v
                    new_u[s, c, at, :] = moved
                    for edge, out in ((slow_edge, slow), (fast_edge, fast)):
                        if s in edge:
                            out[pl.ds((2 * edge.index(s) + c) * rows + row, ROWS), :] = moved

    by_side(body)
    last = slice(rows - 1, rows)
    put_rims(
        lambda s, c: new_u[s, c, 0:1, :],
        lambda s, c: new_u[s, c, last, :],
        lambda s: half[s, 1, last, :],
        rim_a,
        rim_b,
        sections,
    )


def last_kernel(
    base, u, total, arrived, index, splat, out_u_in, out_w_in, out_u, out_w, new_u, new_w, sem
):
    sections, _, rows, width = u.shape
    height = arrived.shape[0] // 4
    rbs = height // ROWS
    part = max(rbs // 4, 1) if rbs % max(rbs // 4, 1) == 0 else rbs

    def body(after):
        copies = []
        for j in range(2):
            own = pairs_of(after, sections)[j][0]
            moving = wide_splat(splat, MOVING + own, width)
            for k in range(rbs):
                rb = base // ROWS + k
                value = slow_values(u, after, arrived, height, base, index, splat, total, j, rb)
                for c in range(2):
                    v = value[c] * moving
                    new_w[j, c, rows_of(k), :] = v
                    new_u[j, c, rows_of(k), :] = u[own, c, rows_of(rb), :] + STEP * v
                if (k + 1) % part == 0:
                    here = pl.ds((k + 1 - part) * ROWS, part * ROWS)
                    there = pl.ds(base + (k + 1 - part) * ROWS, part * ROWS)
                    for source, target in ((new_u, out_u), (new_w, out_w)):
                        copy = pltpu.make_async_copy(
                            source.at[j, :, here], target.at[own, :, there], sem.at[len(copies)]
                        )
                        copy.start()
                        copies.append(copy)
        for copy in copies:
            copy.wait()

    by_side(body)


def call(kernel, outs, ins, alias=None, scratch=(), in_specs=None, out_specs=None, limit=16 << 20, cost=None):
    return pl.pallas_call(
        kernel,
        out_shape=outs,
        in_specs=in_specs or [VMEM] * len(ins),
        out_specs=out_specs or [VMEM] * len(outs),
        input_output_aliases=alias or {},
        scratch_shapes=scratch,
        cost_estimate=cost,
        compiler_params=pltpu.CompilerParams(vmem_limit_bytes=limit),
    )(*ins)


def per_device(u, w, cls, shift, fixed, stiff, cross):
    sections, _, rows, width = u.shape

    def array(*shape, dtype=jnp.float32):
        return jax.ShapeDtypeStruct(shape, dtype)

    full = array(*u.shape)
    two = array(4 * rows, width)
    rim = array(-(-3 * sections // ROWS) * ROWS, width)
    splat = array(MOVING + sections, ROWS, COLS)
    index = array(3, tail_rows(rows), width, dtype=jnp.int32)
    scalars = [
        pltpu.SMEM(shift.shape, jnp.int32),
        pltpu.SemaphoreType.DMA,
        pltpu.VMEM((3 * sections - 3,) + u.shape[1:], jnp.float32),
    ]
    smem = pl.BlockSpec(memory_space=pltpu.SMEM)

    slow, fast = call(lead_kernel, [two, two], [u])
    slow = exchange(slow, "sec", "b")
    fast = exchange(fast, "sec", "a")
    rim_a, rim_b, splat = call(
        prepare_kernel,
        [rim, rim, splat],
        [u, cls, fast, stiff, cross, fixed],
        in_specs=[VMEM] * 2 + [ANY] + [smem] * 3,
    )
    before_fast = exchange(shift, "sec", "a")
    before_slow = exchange(shift, "sec", "b")
    rim_a = exchange(rim_a, "strip", "a")
    rim_b = exchange(rim_b, "strip", "b")
    total, half = call(
        first_inside_kernel, [full, full], [u, cls, shift, splat], scratch=scalars
    )
    total, fast_index = call(
        first_rims_kernel,
        [full, index],
        [u, w, total, half, fast, rim_a, rim_b, shift, before_fast, splat],
        {2: 0},
    )
    u, w, slow, fast, index, rim_a, rim_b = call(
        step_kernel,
        [full, full, two, two, index, rim, rim],
        [u, total, slow, half, shift, before_slow, splat],
    )
    slow = exchange(slow, "sec", "b")
    fast = exchange(fast, "sec", "a")
    rim_a = exchange(rim_a, "strip", "a")
    rim_b = exchange(rim_b, "strip", "b")
    (total,) = call(later_inside_kernel, [full], [u, w, half, shift, splat], scratch=scalars)
    done = max(sections - 2, 1)
    total, out_u, out_w = call(
        later_rims_kernel,
        [full, full, full],
        [u, total, half, fast, rim_a, rim_b, fast_index, splat],
        {1: 0},
        in_specs=[VMEM] * 8,
        scratch=[pltpu.VMEM((done, 2, rows, width), jnp.float32)] * 2
        + [pltpu.SemaphoreType.DMA((2 * done,))],
        out_specs=[VMEM, ANY, ANY],
    )
    return tuple(
        call(
            functools.partial(last_kernel, 0),
            [full, full],
            [u, total, slow, index, splat, out_u, out_w],
            {5: 0, 6: 1},
            scratch=[pltpu.VMEM((2, 2, rows, width), jnp.float32)] * 2
            + [pltpu.SemaphoreType.DMA((4 * (rows // ROWS),))],
            in_specs=[VMEM] * 5 + [ANY] * 2,
            out_specs=[ANY] * 2,
        )
    )


def solution(mesh):
    block = P("sec", None, "strip", None)
    return jax.shard_map(
        per_device,
        mesh=mesh,
        in_specs=(block, block, block, block, P("sec"), P(), P()),
        out_specs=(block, block),
        check_vma=False,
    )
```
